32 devices in a mesh: groups: 2 (over x), ctx: 16 (over z, y, core).
Axes of the slice: x: 2, y: 2, z: 4, core: 2. Of those that a mesh axis runs over, the one named last changes fastest.
Arguments:
- query_plain: bfloat16 [4096, 64, 128], P(('groups', 'ctx')), parts along dimension 0, may hold values from -6 to 6
- query_rotary: bfloat16 [4096, 4096], P(('groups', 'ctx')), parts along dimension 0, may hold values from -540 to 540
- key_latent: bfloat16 [4096, 512], P(('groups', 'ctx')), parts along dimension 0, may hold values from -6 to 6
- key_rotary: bfloat16 [4096, 64], P(('groups', 'ctx')), parts along dimension 0, may hold values from -5 to 5
- absorb_weight: bfloat16 [64, 128, 512], P('ctx'), may hold values from -0.5 to 0.5
- value_weight: bfloat16 [64, 512, 128], P('ctx'), may hold values from -0.25 to 0.25
- lengths: int32 [16], P('groups'), parts along dimension 0, may hold values from 1 to 512, 2048 in all
Outputs:
- attended: bfloat16 [4096, 8192], P(('groups', 'ctx')), parts along dimension 0
The draws below stay inside these ranges and needn't reach their ends.
There are 2 independent parts, one for each index of `groups`. The reference program is written for one: setup_inputs(seed, part) draws one part's arguments, and reference() takes and returns one part's arrays. A program takes and returns all parts, laid end to end along the dimension named above; an argument that names none is the same for every part. Nothing has to cross between parts.
Inputs may be any that keep to these rules, and one draw needn't show every extreme that they name: `lengths`: the 8 transcripts lie end to end and fill all 2048 positions; the longest holds exactly 512 tokens.
All inputs are finite; a program needn't handle non-finite values.
Results may differ from the reference program's by a relative error of at most 0.0072.
Values may be sent and summed in bfloat16 or wider, within the bound.
No kernel may reach another device: no remote copies, remote signals or barrier semaphores. Data moves between devices by JAX's collectives and lax.ppermute only.
A program may use at most 128 MiB of HBM per device.

```python
import math
import jax
import jax.numpy as jnp
import numpy as np
from jax import lax

H = 64
DC = 512
DR = 64
DN = 128
DV = 128
DOC_BLOCKS = 4
TOK_DEV = 128
TOKENS = 2048
MOST = 512
DOCS = 8
N_CTX = 16


def rotary_parts(key):
    shared = jnp.clip(jax.random.normal(jax.random.fold_in(key, 11), (TOKENS, DR), jnp.float32), -5.0, 5.0)
    return shared


def draw_key_rotary(key, part):
    shared = rotary_parts(key)
    return shared.astype(jnp.bfloat16)


def draw_query_rotary(key, part):
    key = jax.random.fold_in(key, 5)
    drawn_values = jnp.clip(jax.random.normal(key, (TOKENS, H, DR), jnp.float32), -5.0, 5.0)
    return drawn_values.reshape(TOKENS, H * DR).astype(jnp.bfloat16)


def level_of(rng, extent, cuts, least, largest):
    gain = 1.0
    for axis_at, shards_of in cuts:
        heights = jax.random.uniform(jax.random.fold_in(jax.random.fold_in(rng, 6), axis_at), (shards_of,), jnp.float32, least / len(cuts), largest / len(cuts))
        gain = gain * jnp.repeat(jnp.exp(heights), extent[axis_at] // shards_of).reshape((-1,) + (1,) * (len(extent) - 1 - axis_at))
    return gain


def length_profile(amount, total, bound, lean):
    portions = [(1 << 20) // math.isqrt(standing ** lean) + 1 for standing in range(2, amount + 1)]
    surplus, given = total - bound - (amount - 1), [1] * (amount - 1)
    while surplus > 0:
        movable = [i for i in range(amount - 1) if given[i] < bound]
        whole, budget = sum([portions[i] for i in movable]), surplus
        for i in movable:
            extra = min(bound - given[i], max(1, budget * portions[i] // whole), surplus)
            given[i] = given[i] + extra
            surplus = surplus - extra
    return np.array([bound] + given)


def ragged(stream_key, number_of, total, limit, slope):
    if number_of == 2:
        one = jax.random.randint(stream_key, (), max(1, total - limit), min(limit, total - 1) + 1)
        return jnp.stack([one, total - one])
    tallies = jnp.asarray(length_profile(number_of, total, limit, slope), jnp.int32)
    twos = (number_of - 1) // 2
    giver, sink = tallies[1:1 + 2 * twos:2], tallies[2:2 + 2 * twos:2]
    room = jnp.minimum(giver - 1, limit - sink)
    passed = jax.random.randint(jax.random.fold_in(stream_key, 1), (twos,), 0, 1 << 20) % (room + 1)
    tallies = tallies.at[1:1 + 2 * twos:2].set(giver - passed).at[2:2 + 2 * twos:2].set(sink + passed)
    return tallies[jax.random.permutation(jax.random.fold_in(stream_key, 2), number_of)]


def scatter_about(rng, dims, width, bound, cuts=(), held_as=jnp.bfloat16):
    drawn = width * jax.random.normal(rng, dims, jnp.float32)
    if cuts:
        drawn = drawn * level_of(rng, dims, cuts, -0.22, 0.18)
    return jnp.clip(drawn, -bound, bound).astype(held_as)


def setup_inputs(seed: int = 0, part: int = 0) -> dict:
    seeds = jax.random.split(jax.random.key(seed), 8)
    part_splits = jax.random.split(jax.random.fold_in(seeds[7], part), 8)
    query_plain = scatter_about(part_splits[0], (TOKENS, H, DN), 1.0, 6.0, ((0, 16),))
    query_rotary = draw_query_rotary(jax.random.fold_in(jax.random.fold_in(seeds[7], part), 71), part)
    key_latent = scatter_about(part_splits[2], (TOKENS, DC), 1.0, 6.0, ((0, 16),))
    key_rotary = draw_key_rotary(jax.random.fold_in(jax.random.fold_in(seeds[7], part), 71), part)
    absorb_weight = scatter_about(seeds[4], (H, DN, DC), DN ** -0.5, 0.5, ((0, 16),))
    value_weight = scatter_about(seeds[5], (H, DC, DV), DC ** -0.5, 0.25, ((0, 16),))
    lengths = ragged(part_splits[6], DOCS, TOKENS, MOST, 2).astype(jnp.int32)
    return {"query_plain": query_plain, "query_rotary": query_rotary, "key_latent": key_latent, "key_rotary": key_rotary, "absorb_weight": absorb_weight, "value_weight": value_weight, "lengths": lengths}


def document_numbers(ends_list, positions):
    return lax.optimization_barrier(jnp.sum((positions[:, None] >= ends_list[None, :]).astype(jnp.int32), axis=1))

def reference(query_plain, query_rotary, key_latent, key_rotary, absorb_weight, value_weight, lengths):
    token_count, head_count, plain_width = query_plain.shape
    rotary_width = key_rotary.shape[1]
    factor_scale = 1.0 / math.sqrt(plain_width + rotary_width)
    ends_list = jnp.cumsum(lengths)
    query_latent = jnp.einsum('thn,hnc->thc', query_plain.astype(jnp.float32), absorb_weight.astype(jnp.float32)).astype(jnp.bfloat16)
    query_rot = query_rotary.reshape(token_count, head_count, rotary_width)
    value_float = value_weight.astype(jnp.float32)
    window_rows = (DOC_BLOCKS + 1) * TOK_DEV

    def one_block(block_index):
        first_query = block_index * TOK_DEV
        first_key = jnp.maximum(block_index - DOC_BLOCKS, 0) * TOK_DEV
        latent_rows = lax.dynamic_slice_in_dim(query_latent, first_query, TOK_DEV, 0).astype(jnp.float32)
        rotary_rows = lax.dynamic_slice_in_dim(query_rot, first_query, TOK_DEV, 0).astype(jnp.float32)
        key_values = lax.dynamic_slice_in_dim(key_latent, first_key, window_rows, 0).astype(jnp.float32)
        key_rots = lax.dynamic_slice_in_dim(key_rotary, first_key, window_rows, 0).astype(jnp.float32)
        scores = (jnp.einsum('thc,uc->htu', latent_rows, key_values) + jnp.einsum('thr,ur->htu', rotary_rows, key_rots)) * factor_scale
        query_pos = first_query + jnp.arange(TOK_DEV, dtype=jnp.int32)
        key_pos = first_key + jnp.arange(window_rows, dtype=jnp.int32)
        allowed = document_numbers(ends_list, key_pos)[None, :] == document_numbers(ends_list, query_pos)[:, None]
        allowed = (allowed & (key_pos[None, :] <= query_pos[:, None]))[None]
        masked = jnp.where(allowed, scores, jnp.float32(-1e+30))
        peak = lax.optimization_barrier(jnp.max(masked, axis=-1))
        weights = jnp.where(allowed, jnp.exp(masked - peak[..., None]), jnp.float32(0.0))
        denominator = lax.optimization_barrier(jnp.sum(weights, axis=-1))
        rounded = weights.astype(jnp.bfloat16).astype(jnp.float32)
        mixed = jnp.einsum('htu,uc->htc', rounded, key_values) / denominator[..., None]
        mixed = mixed.astype(jnp.bfloat16).astype(jnp.float32)
        return jnp.einsum('htc,hcv->thv', mixed, value_float).astype(jnp.bfloat16)
    blocks = lax.map(one_block, jnp.arange(N_CTX, dtype=jnp.int32))
    return blocks.reshape(token_count, head_count * value_weight.shape[2])
```

```python
import functools
import math

import jax
import jax.numpy as jnp
import numpy as np
from jax import lax
from jax.experimental import pallas as pl
from jax.experimental.pallas import tpu as pltpu
from jax.sharding import Mesh, PartitionSpec as P

CHIPS_BACK = 2
STEP_HEADS = 4
VMEM = 48 * 1024 * 1024


def dot(a, b):
    return jnp.dot(a, b, preferred_element_type=jnp.float32)


def attend_kernel(
    factor, own_q, far_q, own_r, far_r, absorb, keys_even, keys_odd, latent, bias, mixed
):
    plain = absorb.shape[1]
    pair = 2 * (own_r.shape[1] // STEP_HEADS)
    for head in range(STEP_HEADS):
        at = slice(head * plain, (head + 1) * plain)
        q = jnp.concatenate([own_q[:, at], far_q[:, at]], axis=0)
        at = slice(head // 2 * pair, (head // 2 + 1) * pair)
        r = jnp.concatenate([own_r[:, at], far_r[:, at]], axis=0)
        q_latent = dot(q, absorb[head]).astype(jnp.bfloat16)
        keys = keys_odd if head % 2 else keys_even
        scores = dot(jnp.concatenate([q_latent, r], axis=1), keys[...]) + bias[...]
        peak = jnp.max(scores, axis=-1, keepdims=True)
        weights = jnp.exp2((scores - peak) * factor)
        total = jnp.sum(weights, axis=-1, keepdims=True)
        summed = dot(weights.astype(jnp.bfloat16), latent[...])
        mixed[head] = (summed * (1.0 / total)).astype(jnp.bfloat16)


def value_kernel(core, mixed, value, out):
    width = value.shape[2]
    for head in range(mixed.shape[0]):
        out[:, head * width : (head + 1) * width] = dot(mixed[head], value[head]).astype(
            jnp.bfloat16
        )


def fill_kernel(core, part, whole, out):
    out[...] = part[...]


def attend(own_q, far_q, own_r, far_r, absorb, keys_even, keys_odd, latent, bias, factor):
    rows = own_q.shape[0]
    heads, plain, depth = absorb.shape
    wide, count = keys_even.shape
    q_spec = pl.BlockSpec((rows, STEP_HEADS * plain), lambda i: (0, i))
    r_spec = pl.BlockSpec((rows, own_r.shape[1] // heads * STEP_HEADS), lambda i: (0, i))
    full = lambda a: pl.BlockSpec(a.shape, lambda i: (0, 0))
    flops = 4 * heads * rows * (plain * depth + wide * count + count * depth)
    return pl.pallas_call(
        functools.partial(attend_kernel, factor),
        grid=(heads // STEP_HEADS,),
        in_specs=[
            q_spec,
            q_spec,
            r_spec,
            r_spec,
            pl.BlockSpec((STEP_HEADS, plain, depth), lambda i: (i, 0, 0)),
            full(keys_even),
            full(keys_odd),
            full(latent),
            full(bias),
        ],
        out_specs=pl.BlockSpec((STEP_HEADS, 2 * rows, depth), lambda i: (i, 0, 0)),
        out_shape=jax.ShapeDtypeStruct((heads, 2 * rows, depth), jnp.bfloat16),
        compiler_params=pltpu.CompilerParams(vmem_limit_bytes=VMEM),
        cost_estimate=pl.CostEstimate(
            flops=flops,
            bytes_accessed=4 * heads * rows * depth + 2 * absorb.size,
            transcendentals=2 * heads * rows * count,
        ),
        name="attend",
    )(own_q, far_q, own_r, far_r, absorb, keys_even, keys_odd, latent, bias)


def value_product(core, mixed, value, half, held, columns):
    heads, both, depth = mixed.shape
    width = value.shape[2]
    rows = both // 2
    total = heads if half else 2 * heads
    return pl.pallas_call(
        value_kernel,
        grid_spec=pltpu.PrefetchScalarGridSpec(
            num_scalar_prefetch=1,
            grid=(heads // held,),
            in_specs=[
                pl.BlockSpec((held, rows, depth), lambda i, core: (i, half, 0)),
                pl.BlockSpec((held, depth, width), lambda i, core: (i, 0, 0)),
            ],
            out_specs=pl.BlockSpec((rows, held * width), lambda i, core: (0, columns(i, core))),
        ),
        out_shape=jax.ShapeDtypeStruct((rows, total * width), jnp.bfloat16),
        compiler_params=pltpu.CompilerParams(vmem_limit_bytes=VMEM),
        cost_estimate=pl.CostEstimate(
            flops=2 * heads * rows * depth * width,
            bytes_accessed=2 * heads * (rows * depth + width * depth + rows * width),
            transcendentals=0,
        ),
        name="value",
    )(core, mixed, value)


def fill(core, part, whole, blocks):
    rows, wide = part.shape
    width = wide // blocks
    return pl.pallas_call(
        fill_kernel,
        grid_spec=pltpu.PrefetchScalarGridSpec(
            num_scalar_prefetch=1,
            grid=(blocks,),
            in_specs=[
                pl.BlockSpec((rows, width), lambda i, core: (0, i)),
                pl.BlockSpec(memory_space=pl.ANY),
            ],
            out_specs=pl.BlockSpec((rows, width), lambda i, core: (0, 2 * i + 1 - core[0])),
        ),
        out_shape=jax.ShapeDtypeStruct(whole.shape, whole.dtype),
        input_output_aliases={2: 0},
        compiler_params=pltpu.CompilerParams(vmem_limit_bytes=VMEM),
        name="fill",
    )(core, part, whole)


def of_core(array, chips, core):
    width = array.shape[1] // (2 * chips)
    picks = [
        jnp.concatenate(
            [array[:, (2 * i + c) * width : (2 * i + c + 1) * width] for i in range(chips)], axis=1
        )
        for c in range(2)
    ]
    return jnp.where(core == 0, picks[0], picks[1])


def swap(block):
    return lax.ppermute(block, "core", [(0, 1), (1, 0)])


def on_device(
    query_plain, query_rotary, key_latent, key_rotary, absorb_weight, value_weight, lengths
):
    rows, head_count, plain = query_plain.shape
    rotary = key_rotary.shape[1]
    depth = key_latent.shape[1]
    chips = lax.axis_size("chip")
    chip, core = lax.axis_index("chip"), lax.axis_index("core")
    core_list = core.reshape(1).astype(jnp.int32)

    absorb = lax.all_gather(absorb_weight, "chip", axis=0, tiled=True)
    value = lax.all_gather(value_weight, "chip", axis=0, tiled=True)

    flat = query_plain.reshape(rows, head_count * plain)
    own_q, far_q = of_core(flat, chips, core), swap(of_core(flat, chips, 1 - core))
    own_r, far_r = of_core(query_rotary, chips, core), swap(of_core(query_rotary, chips, 1 - core))

    joined = jnp.concatenate([key_latent, key_rotary], axis=1)
    reach = [joined]
    for back in range(1, CHIPS_BACK + 1):
        route = [(i - back, i) for i in range(back, chips)]
        reach.insert(0, lax.ppermute(joined, "chip", route))
    mine = jnp.stack(reach)
    other = swap(mine)
    keys = jnp.where(core == 0, jnp.stack([mine, other], 1), jnp.stack([other, mine], 1))
    keys = keys.reshape(-1, depth + rotary)
    latent = keys[:, :depth]
    turned = keys.T
    blank = jnp.zeros((rotary, keys.shape[0]), jnp.bfloat16)
    keys_even = jnp.concatenate([turned, blank], axis=0)
    keys_odd = jnp.concatenate([turned[:depth], blank, turned[depth:]], axis=0)

    ends = jnp.cumsum(lengths)
    span = jnp.arange(rows, dtype=jnp.int32)
    place = jnp.concatenate([(2 * chip + core) * rows + span, (2 * chip + 1 - core) * rows + span])
    begin = jnp.max(jnp.where(ends[None, :] <= place[:, None], ends[None, :], 0), axis=1)
    key_place = (chip - CHIPS_BACK) * 2 * rows + jnp.arange(keys.shape[0], dtype=jnp.int32)
    allowed = (key_place[None, :] >= begin[:, None]) & (key_place[None, :] <= place[:, None])
    bias = jnp.where(allowed, jnp.float32(0.0), jnp.float32(-1e30))

    factor = math.log2(math.e) / math.sqrt(plain + rotary)
    mixed = attend(
        own_q, far_q, own_r, far_r, absorb, keys_even, keys_odd, latent, bias, factor
    )

    held = head_count // (2 * chips)
    far = swap(value_product(core_list, mixed, value, 1, held, lambda i, c: i))
    mine = value_product(core_list, mixed, value, 0, held, lambda i, c: 2 * i + c[0])
    return fill(core_list, far, mine, chips)


def solution(mesh):
    groups, ctx = mesh.shape["groups"], mesh.shape["ctx"]
    by_core = Mesh(
        np.asarray(mesh.devices).reshape(groups, ctx // 2, 2), ("groups", "chip", "core")
    )
    tokens = ("groups", "chip", "core")
    return jax.shard_map(
        on_device,
        mesh=by_core,
        in_specs=(
            P(tokens, None, None),
            P(tokens, None),
            P(tokens, None),
            P(tokens, None),
            P(("chip", "core"), None, None),
            P(("chip", "core"), None, None),
            P("groups"),
        ),
        out_specs=P(tokens, None),
        check_vma=False,
    )
```

```python
import functools
import math

import jax
import jax.numpy as jnp
import numpy as np
from jax import lax
from jax.experimental import pallas as pl
from jax.experimental.pallas import tpu as pltpu
from jax.sharding import Mesh, PartitionSpec as P

QUAD = 4
STEP_HEADS = 4
VMEM = 48 * 1024 * 1024


def dot(a, b):
    return jnp.dot(a, b, preferred_element_type=jnp.float32)


def call(kernel, **kw):
    return pl.pallas_call(
        kernel, compiler_params=pltpu.CompilerParams(vmem_limit_bytes=VMEM), **kw
    )


def pack_kernel(place, *refs):
    plain, rotary, packs = refs[:QUAD], refs[QUAD : 2 * QUAD], refs[2 * QUAD :]
    for k in range(QUAD):
        wide = plain[k].shape[1]
        packs[k][:, :wide] = plain[k][...]
        packs[k][:, wide:] = rotary[k][...]


def pack(place, plain, rotary, pairs):
    rows = plain.shape[0]
    wide, thin = plain.shape[1] // (QUAD * pairs), rotary.shape[1] // (QUAD * pairs)
    if thin % 128 or wide != STEP_HEADS * 128:
        return pack_by_slices(place, plain, rotary, pairs)
    spec = lambda width, k: pl.BlockSpec(
        (rows, width), lambda i, place: (0, QUAD * i + (place[0] ^ k))
    )
    return call(
        pack_kernel,
        grid_spec=pltpu.PrefetchScalarGridSpec(
            num_scalar_prefetch=1,
            grid=(pairs,),
            in_specs=[spec(wide, k) for k in range(QUAD)] + [spec(thin, k) for k in range(QUAD)],
            out_specs=[pl.BlockSpec((rows, wide + thin), lambda i, place: (0, i))] * QUAD,
        ),
        out_shape=[jax.ShapeDtypeStruct((rows, pairs * (wide + thin)), plain.dtype)] * QUAD,
        name="pack",
    )(place, *([plain] * QUAD), *([rotary] * QUAD))


def pack_by_slices(place, plain, rotary, pairs):
    def sets(array):
        width = array.shape[1] // (QUAD * pairs)
        pick = lambda s: [
            array[:, (QUAD * i + s) * width : (QUAD * i + s + 1) * width] for i in range(pairs)
        ]
        whole = jnp.stack([jnp.concatenate(pick(s), axis=1) for s in range(QUAD)])
        steps = whole.shape[2] // (STEP_HEADS * (array.shape[1] // heads))
        return whole.reshape(QUAD, array.shape[0], steps, -1)

    heads = plain.shape[1] // 128
    both = jnp.concatenate([sets(plain), sets(rotary)], axis=3)
    both = both.reshape(QUAD, plain.shape[0], -1)
    return [lax.dynamic_index_in_dim(both, place[0] ^ k, 0, False) for k in range(QUAD)]


def attend_kernel(factor, plain, rotary, place, *refs):
    packs, (absorb, keys, latent, bias, mixed) = refs[:QUAD], refs[QUAD:]
    rows = packs[0].shape[0]
    count = bias.shape[1]
    side = place[0] // 2
    lane = lax.broadcasted_iota(jnp.int32, (2 * rows, 2 * rotary), 1)
    for half in range(2):
        near, far = packs[2 * half], packs[2 * half + 1]
        first = pl.multiple_of((side ^ half) * 2 * rows, 2 * rows)
        window = pl.ds(first, count)
        mask = bias[half * 2 * rows : (half + 1) * 2 * rows, :]
        for head in range(0, STEP_HEADS, 2):
            left = []
            for h in (head, head + 1):
                at = slice(h * plain, (h + 1) * plain)
                q = jnp.concatenate([near[:, at], far[:, at]], axis=0)
                q = dot(q, absorb[h]).astype(jnp.bfloat16)
                start = STEP_HEADS * plain + head * rotary
                at = slice(start, start + 2 * rotary)
                r = jnp.concatenate([near[:, at], far[:, at]], axis=0)
                mine = (lane < rotary) if h == head else (lane >= rotary)
                left.append(jnp.concatenate([q, jnp.where(mine, r, jnp.zeros_like(r))], axis=1))
            scores = dot(jnp.concatenate(left, axis=0), keys[:, window])
            scores = scores + jnp.concatenate([mask, mask], axis=0)
            peak = jnp.max(scores, axis=-1, keepdims=True)
            weights = jnp.exp2((scores - peak) * factor)
            total = jnp.sum(weights, axis=-1, keepdims=True)
            summed = dot(weights.astype(jnp.bfloat16), latent[window, :])
            summed = (summed * (1.0 / total)).astype(jnp.bfloat16)
            for h in range(2):
                mixed[head + h, half * 2 * rows : (half + 1) * 2 * rows, :] = summed[
                    h * 2 * rows : (h + 1) * 2 * rows
                ]


def attend(place, packs, absorb, keys, latent, bias, rotary):
    rows = packs[0].shape[0]
    heads, plain, depth = absorb.shape
    count = bias.shape[1]
    full = lambda a: pl.BlockSpec(a.shape, lambda i, place: (0, 0))
    factor = math.log2(math.e) / math.sqrt(plain + rotary)
    width = STEP_HEADS * (plain + rotary)
    return call(
        functools.partial(attend_kernel, factor, plain, rotary),
        grid_spec=pltpu.PrefetchScalarGridSpec(
            num_scalar_prefetch=1,
            grid=(heads // STEP_HEADS,),
            in_specs=[pl.BlockSpec((rows, width), lambda i, place: (0, i))] * QUAD
            + [
                pl.BlockSpec((STEP_HEADS, plain, depth), lambda i, place: (i, 0, 0)),
                full(keys),
                full(latent),
                full(bias),
            ],
            out_specs=pl.BlockSpec((STEP_HEADS, QUAD * rows, depth), lambda i, place: (i, 0, 0)),
        ),
        out_shape=jax.ShapeDtypeStruct((heads, QUAD * rows, depth), jnp.bfloat16),
        cost_estimate=pl.CostEstimate(
            flops=2 * heads * QUAD * rows * (plain * depth + (2 * depth + 2 * rotary) * count),
            bytes_accessed=2 * heads * depth * (QUAD * rows + plain),
            transcendentals=heads * QUAD * rows * count,
        ),
        name="attend",
    )(place, *packs, absorb, keys, latent, bias)


def value_kernel(mixed, value, one, two):
    rows, width = one.shape[0], value.shape[2]
    for head in range(mixed.shape[0]):
        out = dot(mixed[head], value[head]).astype(jnp.bfloat16)
        one[:, head * width : (head + 1) * width] = out[:rows]
        two[:, head * width : (head + 1) * width] = out[rows:]


def value_product(mixed, value, half):
    heads, rows, depth = mixed.shape
    rows, width = rows // QUAD, value.shape[2]
    out = pl.BlockSpec((rows, STEP_HEADS * width), lambda i: (0, i))
    return call(
        value_kernel,
        grid=(heads // STEP_HEADS,),
        in_specs=[
            pl.BlockSpec((STEP_HEADS, 2 * rows, depth), lambda i: (i, half, 0)),
            pl.BlockSpec((STEP_HEADS, depth, width), lambda i: (i, 0, 0)),
        ],
        out_specs=[out] * 2,
        out_shape=[jax.ShapeDtypeStruct((rows, heads * width), jnp.bfloat16)] * 2,
        cost_estimate=pl.CostEstimate(
            flops=4 * heads * rows * depth * width,
            bytes_accessed=2 * heads * (2 * rows * depth + width * depth + 2 * rows * width),
            transcendentals=0,
        ),
        name="value",
    )(mixed, value)


def join_kernel(place, *refs):
    parts, out = refs[:QUAD], refs[QUAD]
    width = parts[0].shape[1]
    for k in range(QUAD):
        first = pl.multiple_of((place[0] ^ k) * width, width)
        out[:, pl.ds(first, width)] = parts[k][...]


def join(place, parts, pairs):
    rows, wide = parts[0].shape
    width = wide // pairs
    return call(
        join_kernel,
        grid_spec=pltpu.PrefetchScalarGridSpec(
            num_scalar_prefetch=1,
            grid=(pairs,),
            in_specs=[pl.BlockSpec((rows, width), lambda i, place: (0, i))] * QUAD,
            out_specs=pl.BlockSpec((rows, QUAD * width), lambda i, place: (0, i)),
        ),
        out_shape=jax.ShapeDtypeStruct((rows, QUAD * wide), jnp.bfloat16),
        name="join",
    )(place, *parts)


def swap(block, k):
    return lax.ppermute(block, ("side", "core"), [(i, i ^ k) for i in range(QUAD)])


def gather(weight):
    held, groups = weight.shape[0], lax.axis_size("groups")
    if held % groups:
        return lax.all_gather(weight, "pair", axis=0, tiled=True)
    held //= groups
    part = lax.dynamic_slice_in_dim(weight, lax.axis_index("groups") * held, held, 0)
    return lax.all_gather(part, ("pair", "groups"), axis=0, tiled=True)


def on_device(
    query_plain, query_rotary, key_latent, key_rotary, absorb_weight, value_weight, lengths
):
    rows, head_count, plain = query_plain.shape
    rotary = key_rotary.shape[1]
    depth = key_latent.shape[1]
    pairs = lax.axis_size("pair")
    pair, side, core = (lax.axis_index(name) for name in ("pair", "side", "core"))
    here = 2 * side + core
    place = here.reshape(1).astype(jnp.int32)

    absorb = gather(absorb_weight)
    value = gather(value_weight)

    joined = jnp.concatenate([key_latent, key_rotary], axis=1)
    before = lax.ppermute(joined, "pair", [(i - 1, i) for i in range(1, pairs)])

    flat = query_plain.reshape(rows, head_count * plain)
    packs = list(pack(place, flat, query_rotary, pairs))
    packs = packs[:1] + [swap(packs[k], k) for k in range(1, QUAD)]

    mine = jnp.stack([before, joined])
    other = swap(mine, 2)
    mine = jnp.where(side == 0, jnp.stack([mine, other], 1), jnp.stack([other, mine], 1))
    other = swap(mine, 1)
    keys = jnp.where(core == 0, jnp.stack([mine, other], 2), jnp.stack([other, mine], 2))
    keys = keys.reshape(-1, depth + rotary)
    latent = keys[:, :depth]
    turned = keys.T
    turned = jnp.concatenate([turned, turned[depth:]], axis=0)

    ends = jnp.cumsum(lengths)
    span = jnp.arange(rows, dtype=jnp.int32)
    place_of = jnp.concatenate([(QUAD * pair + (here ^ k)) * rows + span for k in range(QUAD)])
    begin = jnp.max(jnp.where(ends[None, :] <= place_of[:, None], ends[None, :], 0), axis=1)
    count = (QUAD + 2) * rows
    first = (QUAD * (pair - 1) + 2 * jnp.stack([side, 1 - side])) * rows
    key_place = first[:, None] + jnp.arange(count, dtype=jnp.int32)[None, :]
    key_place = jnp.repeat(key_place, 2 * rows, axis=0)
    allowed = (key_place >= begin[:, None]) & (key_place <= place_of[:, None])
    bias = jnp.where(allowed, jnp.float32(0.0), jnp.float32(-1e30))

    mixed = attend(place, packs, absorb, turned, latent, bias, rotary)

    far = list(value_product(mixed, value, 1))
    far = [swap(far[k - 2], k) for k in (2, 3)]
    mine, near = value_product(mixed, value, 0)
    return join(place, [mine, swap(near, 1)] + far, pairs)


def solution(mesh):
    groups, ctx = mesh.shape["groups"], mesh.shape["ctx"]
    names = ("groups", "pair", "side", "core")
    fine = Mesh(np.asarray(mesh.devices).reshape(groups, ctx // QUAD, 2, 2), names)
    return jax.shard_map(
        on_device,
        mesh=fine,
        in_specs=(
            P(names, None, None),
            P(names, None),
            P(names, None),
            P(names, None),
            P(names[1:], None, None),
            P(names[1:], None, None),
            P("groups"),
        ),
        out_specs=P(names, None),
        check_vma=False,
    )
```

```python
import functools
import math

import jax
import jax.numpy as jnp
import numpy as np
from jax import lax
from jax.experimental import pallas as pl
from jax.experimental.pallas import tpu as pltpu
from jax.sharding import Mesh, PartitionSpec as P

QUAD = 4
UNIT = 2
STEP_HEADS = 4
VMEM = 48 * 1024 * 1024


def dot(a, b):
    return jnp.dot(a, b, preferred_element_type=jnp.float32)


def call(kernel, **kw):
    return pl.pallas_call(
        kernel, compiler_params=pltpu.CompilerParams(vmem_limit_bytes=VMEM), **kw
    )


def pack_kernel(groups, place, plain, rotary, *refs):
    packs, flat = refs[:-1], refs[-1]
    for head in range(plain.shape[1]):
        flat[:, head * 128 : (head + 1) * 128] = plain[:, head, :]
    wide, thin = UNIT * 128, rotary.shape[1] // (QUAD * groups)
    for c in range(groups):
        for k in range(QUAD):
            at = (place[0] ^ k) * groups + lax.rem(place[2] + c, groups)
            out = packs[c * QUAD + k]
            out[:, :wide] = flat[:, pl.ds(pl.multiple_of(at * wide, wide), wide)]
            out[:, wide:] = rotary[:, pl.ds(pl.multiple_of(at * thin, thin), thin)]


def pack(place, plain, rotary, pairs, groups):
    rows, heads, _ = plain.shape
    held = heads // pairs
    thin = rotary.shape[1] // pairs
    width = held * 128 // (QUAD * groups) + thin // (QUAD * groups)
    count = QUAD * groups
    packs = call(
        functools.partial(pack_kernel, groups),
        grid_spec=pltpu.PrefetchScalarGridSpec(
            num_scalar_prefetch=1,
            grid=(pairs,),
            in_specs=[
                pl.BlockSpec((rows, held, 128), lambda i, place: (0, i, 0)),
                pl.BlockSpec((rows, thin), lambda i, place: (0, i)),
            ],
            out_specs=[pl.BlockSpec((rows, width), lambda i, place: (0, place[1] ^ i))] * count,
            scratch_shapes=[pltpu.VMEM((rows, held * 128), plain.dtype)],
        ),
        out_shape=[jax.ShapeDtypeStruct((rows, pairs * width), plain.dtype)] * count,
        name="pack",
    )(place, plain, rotary)
    return [list(packs[c * QUAD : (c + 1) * QUAD]) for c in range(groups)]


def pack_by_slices(place, plain, rotary, pairs):
    def sets(array):
        width = array.shape[1] // (QUAD * pairs)
        pick = lambda s: [
            array[:, (QUAD * i + s) * width : (QUAD * i + s + 1) * width] for i in range(pairs)
        ]
        whole = jnp.stack([jnp.concatenate(pick(s), axis=1) for s in range(QUAD)])
        steps = whole.shape[2] // (UNIT * (array.shape[1] // heads))
        return whole.reshape(QUAD, array.shape[0], steps, -1)

    heads = plain.shape[1] // 128
    both = jnp.concatenate([sets(plain), sets(rotary)], axis=3)
    both = both.reshape(QUAD, plain.shape[0], -1)
    return [lax.dynamic_index_in_dim(both, place[0] ^ k, 0, False) for k in range(QUAD)]


def attend_kernel(factor, plain, rotary, place, *refs):
    packs, (absorb, keys, latent, bias, mixed) = refs[:QUAD], refs[QUAD:]
    rows = packs[0].shape[0]
    count = bias.shape[1]
    side = place[0] // 2
    lane = lax.broadcasted_iota(jnp.int32, (2 * rows, 2 * rotary), 1)
    for half in range(2):
        near, far = packs[2 * half], packs[2 * half + 1]
        first = pl.multiple_of((side ^ half) * 2 * rows, 2 * rows)
        window = pl.ds(first, count)
        mask = bias[half * 2 * rows : (half + 1) * 2 * rows, :]
        for head in range(0, STEP_HEADS, 2):
            left = []
            for h in (head, head + 1):
                base = h // UNIT * UNIT * (plain + rotary)
                at = slice(base + h % UNIT * plain, base + (h % UNIT + 1) * plain)
                q = jnp.concatenate([near[:, at], far[:, at]], axis=0)
                q = dot(q, absorb[h]).astype(jnp.bfloat16)
                start = base + UNIT * plain + h % UNIT // 2 * 2 * rotary
                at = slice(start, start + 2 * rotary)
                r = jnp.concatenate([near[:, at], far[:, at]], axis=0)
                mine = (lane < rotary) if h == head else (lane >= rotary)
                left.append(jnp.concatenate([q, jnp.where(mine, r, jnp.zeros_like(r))], axis=1))
            scores = dot(jnp.concatenate(left, axis=0), keys[:, window])
            scores = scores + jnp.concatenate([mask, mask], axis=0)
            peak = jnp.max(scores, axis=-1, keepdims=True)
            weights = jnp.exp2((scores - peak) * factor)
            total = jnp.sum(weights, axis=-1, keepdims=True)
            summed = dot(weights.astype(jnp.bfloat16), latent[window, :])
            summed = (summed * (1.0 / total)).astype(jnp.bfloat16)
            for h in range(2):
                mixed[head + h, half * 2 * rows : (half + 1) * 2 * rows, :] = summed[
                    h * 2 * rows : (h + 1) * 2 * rows
                ]


def attend(place, packs, absorb, keys, latent, bias, rotary):
    rows = packs[0].shape[0]
    heads, plain, depth = absorb.shape
    count = bias.shape[1]
    full = lambda a: pl.BlockSpec(a.shape, lambda i, place: (0, 0))
    factor = math.log2(math.e) / math.sqrt(plain + rotary)
    width = STEP_HEADS * (plain + rotary)
    return call(
        functools.partial(attend_kernel, factor, plain, rotary),
        grid_spec=pltpu.PrefetchScalarGridSpec(
            num_scalar_prefetch=1,
            grid=(heads // STEP_HEADS,),
            in_specs=[pl.BlockSpec((rows, width), lambda i, place: (0, i))] * QUAD
            + [
                pl.BlockSpec((STEP_HEADS, plain, depth), lambda i, place: (i, 0, 0)),
                full(keys),
                full(latent),
                full(bias),
            ],
            out_specs=pl.BlockSpec((STEP_HEADS, QUAD * rows, depth), lambda i, place: (i, 0, 0)),
        ),
        out_shape=jax.ShapeDtypeStruct((heads, QUAD * rows, depth), jnp.bfloat16),
        cost_estimate=pl.CostEstimate(
            flops=2 * heads * QUAD * rows * (plain * depth + (2 * depth + 2 * rotary) * count),
            bytes_accessed=2 * heads * depth * (QUAD * rows + plain),
            transcendentals=heads * QUAD * rows * count,
        ),
        name="attend",
    )(place, *packs, absorb, keys, latent, bias)


def value_kernel(mixed, value, one, two):
    rows, width = one.shape[0], value.shape[2]
    for head in range(mixed.shape[0]):
        out = dot(mixed[head], value[head]).astype(jnp.bfloat16)
        one[:, head * width : (head + 1) * width] = out[:rows]
        two[:, head * width : (head + 1) * width] = out[rows:]


def value_product(mixed, value, half):
    heads, rows, depth = mixed.shape
    rows, width = rows // QUAD, value.shape[2]
    out = pl.BlockSpec((rows, STEP_HEADS * width), lambda i: (0, i))
    return call(
        value_kernel,
        grid=(heads // STEP_HEADS,),
        in_specs=[
            pl.BlockSpec((STEP_HEADS, 2 * rows, depth), lambda i: (i, half, 0)),
            pl.BlockSpec((STEP_HEADS, depth, width), lambda i: (i, 0, 0)),
        ],
        out_specs=[out] * 2,
        out_shape=[jax.ShapeDtypeStruct((rows, heads * width), jnp.bfloat16)] * 2,
        cost_estimate=pl.CostEstimate(
            flops=4 * heads * rows * depth * width,
            bytes_accessed=2 * heads * (2 * rows * depth + width * depth + 2 * rows * width),
            transcendentals=0,
        ),
        name="value",
    )(mixed, value)


def join_kernel(chunks, place, *refs):
    parts, out = refs[:-1], refs[-1]
    width = parts[0].shape[1]
    for c in range(chunks):
        for k in range(QUAD):
            at = (place[0] ^ k) * chunks + lax.rem(place[2] + c, chunks)
            out[:, pl.ds(pl.multiple_of(at * width, width), width)] = parts[c * QUAD + k][...]


def join(place, parts, pairs, shifted):
    chunks = len(parts)
    rows, wide = parts[0][0].shape
    width = wide // pairs
    if shifted:
        spec = pl.BlockSpec((rows, width), lambda i, place: (0, place[1] ^ i))
    else:
        spec = pl.BlockSpec((rows, width), lambda i, place: (0, i))
    return call(
        functools.partial(join_kernel, chunks),
        grid_spec=pltpu.PrefetchScalarGridSpec(
            num_scalar_prefetch=1,
            grid=(pairs,),
            in_specs=[spec] * (chunks * QUAD),
            out_specs=pl.BlockSpec((rows, chunks * QUAD * width), lambda i, place: (0, i)),
        ),
        out_shape=jax.ShapeDtypeStruct((rows, chunks * QUAD * wide), jnp.bfloat16),
        name="join",
    )(place, *[part for chunk in parts for part in chunk])


def swap(block, k):
    return lax.ppermute(block, ("side", "core"), [(i, i ^ k) for i in range(QUAD)])


def after(later, *earlier):
    return lax.optimization_barrier((later, earlier))[0]


def across(part, distance):
    pairs = lax.axis_size("pair")
    return lax.ppermute(part, "pair", [(i, i ^ distance) for i in range(pairs)])


def from_group(part, c):
    groups = lax.axis_size("groups")
    return lax.ppermute(part, "groups", [((i + c) % groups, i) for i in range(groups)])


def key_window(joined, before, other, side, core):
    mine = jnp.stack([before, joined])
    other = jnp.stack(jnp.split(other, 2, axis=1))
    mine = jnp.where(side == 0, jnp.stack([mine, other], 1), jnp.stack([other, mine], 1))
    other = swap(mine, 1)
    keys = jnp.where(core == 0, jnp.stack([mine, other], 2), jnp.stack([other, mine], 2))
    return keys.reshape(-1, joined.shape[1])


def allowed_bias(lengths, pair, side, here, rows):
    ends = jnp.cumsum(lengths)
    span = jnp.arange(rows, dtype=jnp.int32)
    place_of = jnp.concatenate([(QUAD * pair + (here ^ k)) * rows + span for k in range(QUAD)])
    begin = jnp.max(jnp.where(ends[None, :] <= place_of[:, None], ends[None, :], 0), axis=1)
    count = (QUAD + 2) * rows
    first = (QUAD * (pair - 1) + 2 * jnp.stack([side, 1 - side])) * rows
    key_place = first[:, None] + jnp.arange(count, dtype=jnp.int32)[None, :]
    key_place = jnp.repeat(key_place, 2 * rows, axis=0)
    allowed = (key_place >= begin[:, None]) & (key_place <= place_of[:, None])
    return jnp.where(allowed, jnp.float32(0.0), jnp.float32(-1e30))


def on_device(
    query_plain, query_rotary, key_latent, key_rotary, absorb_weight, value_weight, lengths
):
    rows, head_count, plain = query_plain.shape
    rotary = key_rotary.shape[1]
    depth = key_latent.shape[1]
    held = absorb_weight.shape[0]
    pairs, groups = lax.axis_size("pair"), lax.axis_size("groups")
    names = ("groups", "pair", "side", "core")
    group, pair, side, core = (lax.axis_index(name) for name in names)
    here = 2 * side + core
    place = jnp.stack([here, pair, group]).astype(jnp.int32)
    by_group = held == groups * UNIT and plain == 128 and UNIT * rotary == 128
    by_group = by_group and pairs & (pairs - 1) == 0

    joined = jnp.concatenate([key_latent, key_rotary], axis=1)
    before = lax.ppermute(joined, "pair", [(i - 1, i) for i in range(1, pairs)])

    def own(weight, c):
        return lax.dynamic_slice_in_dim(weight, (group + c) % groups * UNIT, UNIT, 0)

    def near_quad(weight):
        part = own(weight, 0)
        return jnp.concatenate([part, across(part, 1)])

    def far_quads(weight):
        distance = 2
        while distance < pairs:
            weight = jnp.concatenate([weight, across(weight, distance)])
            distance *= 2
        return weight

    if by_group:
        absorb = near_quad(absorb_weight)
        value = near_quad(value_weight)
        packs = pack(place, query_plain, query_rotary, pairs, groups)
        before, absorb, value, packs = lax.optimization_barrier((before, absorb, value, packs))
        absorb = far_quads(absorb)
        value = far_quads(after(value, absorb))
    else:
        absorb = lax.all_gather(absorb_weight, "pair", axis=0, tiled=True)
        value = lax.all_gather(value_weight, "pair", axis=0, tiled=True)
        flat = query_plain.reshape(rows, head_count * plain)
        packs = [pack_by_slices(place, flat, query_rotary, pairs)]
    chunks = len(packs)

    def queries(packs_of):
        return [packs_of[0]] + [swap(packs_of[k], k) for k in range(1, QUAD)]

    wide = packs[0][2].shape[1]
    first = list(packs[0])
    first[2] = jnp.concatenate([first[2], before, joined], axis=1)
    first = queries(first)
    first[2], other = first[2][:, :wide], first[2][:, wide:]
    keys = key_window(joined, before, other, side, core)
    latent = keys[:, :depth]
    turned = keys.T
    turned = jnp.concatenate([turned, turned[depth:]], axis=0)
    bias = allowed_bias(lengths, pair, side, here, rows)

    arrived, sent, parts = first, (), []
    for c in range(chunks):
        coming = queries(after(packs[c + 1], *arrived)) if c + 1 < chunks else None
        absorb_c, value_c = absorb, value
        if c:
            absorb_c = jnp.concatenate([own(absorb_weight, c), from_group(absorb[UNIT:], c)])
            value_c = jnp.concatenate([own(value_weight, c), from_group(value[UNIT:], c)])
        mixed = attend(place, after(arrived, *sent), absorb_c, turned, latent, bias, rotary)
        if c == 0:
            value_c = value = after(value, mixed)
        sent = list(value_product(mixed, value_c, 1))
        sent = list(value_product(mixed, value_c, 0)) + sent
        parts.append([sent[0]] + [swap(sent[k], k) for k in range(1, QUAD)])
        arrived = coming
    return join(place, parts, pairs, by_group)


def solution(mesh):
    groups, ctx = mesh.shape["groups"], mesh.shape["ctx"]
    names = ("groups", "pair", "side", "core")
    fine = Mesh(np.asarray(mesh.devices).reshape(groups, ctx // QUAD, 2, 2), names)
    return jax.shard_map(
        on_device,
        mesh=fine,
        in_specs=(
            P(names, None, None),
            P(names, None),
            P(names, None),
            P(names, None),
            P(names[1:], None, None),
            P(names[1:], None, None),
            P("groups"),
        ),
        out_specs=P(names, None),
        check_vma=False,
    )
```

```python
import functools
import math

import jax
import jax.numpy as jnp
import numpy as np
from jax import lax
from jax.experimental import pallas as pl
from jax.experimental.pallas import tpu as pltpu
from jax.sharding import Mesh, PartitionSpec as P

QUAD = 4
UNIT = 2
STEP_HEADS = 4
STRIP = 32
VMEM = 32 * 1024 * 1024


def dot(a, b):
    return jnp.dot(a, b, preferred_element_type=jnp.float32)


def call(kernel, **kw):
    return pl.pallas_call(
        kernel, compiler_params=pltpu.CompilerParams(vmem_limit_bytes=VMEM), **kw
    )


def pack_kernel(groups, place, plain, rotary, *refs):
    both, (single, flat) = refs[:-2], refs[-2:]
    rows, heads, width = plain.shape
    single[...] = plain[...].astype(jnp.float32).reshape(rows * heads, width)
    for head in range(heads):
        part = single[pl.ds(head, rows, stride=heads), :]
        flat[:, head * width : (head + 1) * width] = part.astype(flat.dtype)
    wide, thin = UNIT * width, rotary.shape[1] // (QUAD * groups)
    for c in range(groups):
        for k in range(QUAD):
            at = (place[0] ^ k) * groups + lax.rem(place[2] + c, groups)
            out = both[k].at[c] if k < 2 else both[2 + c * 2 + k - 2]
            out[:, :wide] = flat[:, pl.ds(pl.multiple_of(at * wide, wide), wide)]
            out[:, wide:] = rotary[:, pl.ds(pl.multiple_of(at * thin, thin), thin)]


def pack(place, plain, rotary, pairs, groups):
    rows, heads, wide = plain.shape
    held = heads // pairs
    thin = rotary.shape[1] // pairs
    width = (held * wide + thin) // (QUAD * groups)
    every = pl.BlockSpec((groups, rows, width), lambda i, place: (0, 0, place[1] ^ i))
    one = pl.BlockSpec((rows, width), lambda i, place: (0, place[1] ^ i))
    packs = call(
        functools.partial(pack_kernel, groups),
        grid_spec=pltpu.PrefetchScalarGridSpec(
            num_scalar_prefetch=1,
            grid=(pairs,),
            in_specs=[
                pl.BlockSpec((rows, held, wide), lambda i, place: (0, i, 0)),
                pl.BlockSpec((rows, thin), lambda i, place: (0, i)),
            ],
            out_specs=[every] * 2 + [one] * (2 * groups),
            scratch_shapes=[
                pltpu.VMEM((rows * held, wide), jnp.float32),
                pltpu.VMEM((rows, held * wide), plain.dtype),
            ],
        ),
        out_shape=[jax.ShapeDtypeStruct((groups, rows, pairs * width), plain.dtype)] * 2
        + [jax.ShapeDtypeStruct((rows, pairs * width), plain.dtype)] * (2 * groups),
        name="pack",
    )(place, plain, rotary)
    return packs[:2], [list(packs[2 + 2 * c : 4 + 2 * c]) for c in range(groups)]


def pack_by_slices(place, plain, rotary, pairs):
    def sets(array):
        width = array.shape[1] // (QUAD * pairs)
        pick = lambda s: [
            array[:, (QUAD * i + s) * width : (QUAD * i + s + 1) * width] for i in range(pairs)
        ]
        whole = jnp.stack([jnp.concatenate(pick(s), axis=1) for s in range(QUAD)])
        steps = whole.shape[2] // (UNIT * (array.shape[1] // heads))
        return whole.reshape(QUAD, array.shape[0], steps, -1)

    heads = plain.shape[1] // 128
    both = jnp.concatenate([sets(plain), sets(rotary)], axis=3)
    both = both.reshape(QUAD, plain.shape[0], -1)
    packs = [lax.dynamic_index_in_dim(both, place[0] ^ k, 0, False) for k in range(QUAD)]
    return [pack[None] for pack in packs[:2]], [packs[2:]]


def keys_kernel(place, near, far, begin, end, latent, turned, bias):
    rows, depth = near.shape[1], latent.shape[1]
    side, core = place[0] // 2, place[0] % 2
    for c, blocks in enumerate((near, far)):
        for k in range(2):
            for quad in range(2):
                first = (quad * 2 + (side ^ k)) * 2 * rows + c * rows
                at = pl.ds(pl.multiple_of(first, rows), rows)
                block = blocks[k * 2 + quad]
                latent[at, :] = block[:, :depth]
                rotary = block[:, depth:]
                turned[:depth, at] = block[:, :depth].T
                turned[depth:, at] = jnp.concatenate([rotary, rotary], axis=1).T
    count = bias.shape[1]
    spot = lax.broadcasted_iota(jnp.int32, (2 * rows, count), 1) ^ (core * rows)
    for half in range(2):
        at = slice(half * 2 * rows, (half + 1) * 2 * rows)
        spots = spot + (QUAD * (place[1] - 1) + 2 * (side ^ half)) * rows
        allowed = (spots >= begin[at, :]) & (spots <= end[at, :])
        bias[at, :] = jnp.where(allowed, jnp.float32(0.0), jnp.float32(-1e30))


def prepare_keys(place, near, far, begin, end, depth):
    rows, wide = near.shape[1:]
    whole = pl.BlockSpec(memory_space=pltpu.VMEM)
    return call(
        keys_kernel,
        in_specs=[pl.BlockSpec(memory_space=pltpu.SMEM)] + [whole] * 4,
        out_specs=[whole] * 3,
        out_shape=[
            jax.ShapeDtypeStruct((2 * QUAD * rows, depth), near.dtype),
            jax.ShapeDtypeStruct((2 * wide - depth, 2 * QUAD * rows), near.dtype),
            jax.ShapeDtypeStruct((QUAD * rows, (QUAD + 2) * rows), jnp.float32),
        ],
        name="keys",
    )(place, near, far, begin, end)


def attend_kernel(factor, plain, rotary, place, *refs):
    packs, (absorb, keys, latent, bias, mixed, scores, weights) = refs[:QUAD], refs[QUAD:]
    rows = packs[0].shape[0]
    both, count = 2 * rows, bias.shape[1]
    side = place[0] // 2
    lane = lax.broadcasted_iota(jnp.int32, (both, 2 * rotary), 1)
    units = [(half, head) for half in range(2) for head in range(0, STEP_HEADS, 2)]

    def window(half):
        return pl.ds(pl.multiple_of((side ^ half) * both, both), count)

    def score(u):
        half, head = units[u]
        near, far = packs[2 * half], packs[2 * half + 1]
        base = head // UNIT * UNIT * (plain + rotary)
        for h in range(2):
            at = slice(base + (head % UNIT + h) * plain, base + (head % UNIT + h + 1) * plain)
            q = jnp.concatenate([near[:, at], far[:, at]], axis=0)
            q = dot(q, absorb[head + h]).astype(jnp.bfloat16)
            start = base + UNIT * plain + head % UNIT * rotary
            at = slice(start, start + 2 * rotary)
            r = jnp.concatenate([near[:, at], far[:, at]], axis=0)
            mine = (lane < rotary) if h == 0 else (lane >= rotary)
            left = jnp.concatenate([q, jnp.where(mine, r, jnp.zeros_like(r))], axis=1)
            scores[u % 2, h * both : (h + 1) * both, :] = dot(left, keys[:, window(half)])

    def weigh(u):
        half = units[u][0]
        scale = []
        for first in range(0, 2 * both, STRIP):
            at = slice(first, first + STRIP)
            start = half * both + first % both
            s = scores[u % 2, at, :] + bias[start : start + STRIP, :]
            w = jnp.exp2((s - jnp.max(s, axis=-1, keepdims=True)) * factor)
            scale.append(1.0 / jnp.sum(w, axis=-1, keepdims=True))
            weights[u % 2, at, :] = w.astype(jnp.bfloat16)
        return jnp.concatenate(scale, axis=0)

    score(0)
    for u, (half, head) in enumerate(units):
        if u + 1 < len(units):
            score(u + 1)
        scale = weigh(u)
        for h in range(2):
            at = slice(h * both, (h + 1) * both)
            summed = dot(weights[u % 2, at, :], latent[window(half), :])
            mixed[head + h, half * both : (half + 1) * both, :] = (summed * scale[at]).astype(
                jnp.bfloat16
            )


def attend(place, near, far, chunk, absorb, keys, latent, bias, rotary):
    rows = far[0].shape[0]
    heads, plain, depth = absorb.shape
    count = bias.shape[1]
    whole = pl.BlockSpec(memory_space=pltpu.VMEM)
    factor = math.log2(math.e) / math.sqrt(plain + rotary)
    width = STEP_HEADS * (plain + rotary)
    return call(
        functools.partial(attend_kernel, factor, plain, rotary),
        grid_spec=pltpu.PrefetchScalarGridSpec(
            num_scalar_prefetch=1,
            grid=(heads // STEP_HEADS,),
            in_specs=[pl.BlockSpec((None, rows, width), lambda i, place: (chunk, 0, i))] * 2
            + [pl.BlockSpec((rows, width), lambda i, place: (0, i))] * 2
            + [pl.BlockSpec((STEP_HEADS, plain, depth), lambda i, place: (i, 0, 0))]
            + [whole] * 3,
            out_specs=pl.BlockSpec((STEP_HEADS, QUAD * rows, depth), lambda i, place: (i, 0, 0)),
            scratch_shapes=[
                pltpu.VMEM((2, QUAD * rows, count), jnp.float32),
                pltpu.VMEM((2, QUAD * rows, count), jnp.bfloat16),
            ],
        ),
        out_shape=jax.ShapeDtypeStruct((heads, QUAD * rows, depth), jnp.bfloat16),
        cost_estimate=pl.CostEstimate(
            flops=2 * heads * QUAD * rows * (plain * depth + (2 * depth + 2 * rotary) * count),
            bytes_accessed=2 * heads * depth * (QUAD * rows + plain),
            transcendentals=heads * QUAD * rows * count,
        ),
        name="attend",
    )(place, *near, *far, absorb, keys, latent, bias)


def value_kernel(mixed, value, one, two):
    rows, width = one.shape[0], value.shape[2]
    for head in range(mixed.shape[0]):
        out = dot(mixed[head], value[head]).astype(jnp.bfloat16)
        one[:, head * width : (head + 1) * width] = out[:rows]
        two[:, head * width : (head + 1) * width] = out[rows:]


def value_product(mixed, value, half):
    heads, rows, depth = mixed.shape
    rows, width = rows // QUAD, value.shape[2]
    out = pl.BlockSpec((rows, STEP_HEADS * width), lambda i: (0, i))
    return call(
        value_kernel,
        grid=(heads // STEP_HEADS,),
        in_specs=[
            pl.BlockSpec((STEP_HEADS, 2 * rows, depth), lambda i: (i, half, 0)),
            pl.BlockSpec((STEP_HEADS, depth, width), lambda i: (i, 0, 0)),
        ],
        out_specs=[out] * 2,
        out_shape=[jax.ShapeDtypeStruct((rows, heads * width), jnp.bfloat16)] * 2,
        cost_estimate=pl.CostEstimate(
            flops=4 * heads * rows * depth * width,
            bytes_accessed=2 * heads * (2 * rows * depth + width * depth + 2 * rows * width),
            transcendentals=0,
        ),
        name="value",
    )(mixed, value)


def join_kernel(chunks, place, *refs):
    parts, out = refs[:-1], refs[-1]
    width = parts[0].shape[1]
    for c in range(chunks):
        for k in range(QUAD):
            at = (place[0] ^ k) * chunks + lax.rem(place[2] + c, chunks)
            out[:, pl.ds(pl.multiple_of(at * width, width), width)] = parts[c * QUAD + k][...]


def join(place, parts, pairs, shifted):
    chunks = len(parts)
    rows, wide = parts[0][0].shape
    width = wide // pairs
    if shifted:
        spec = pl.BlockSpec((rows, width), lambda i, place: (0, place[1] ^ i))
    else:
        spec = pl.BlockSpec((rows, width), lambda i, place: (0, i))
    return call(
        functools.partial(join_kernel, chunks),
        grid_spec=pltpu.PrefetchScalarGridSpec(
            num_scalar_prefetch=1,
            grid=(pairs,),
            in_specs=[spec] * (chunks * QUAD),
            out_specs=pl.BlockSpec((rows, chunks * QUAD * width), lambda i, place: (0, i)),
        ),
        out_shape=jax.ShapeDtypeStruct((rows, chunks * QUAD * wide), jnp.bfloat16),
        name="join",
    )(place, *[part for chunk in parts for part in chunk])


def swap(block, k):
    return lax.ppermute(block, ("side", "core"), [(i, i ^ k) for i in range(QUAD)])


def after(later, *earlier):
    return lax.optimization_barrier((later, earlier))[0]


def across(part, distance):
    pairs = lax.axis_size("pair")
    return lax.ppermute(part, "pair", [(i, i ^ distance) for i in range(pairs)])


def from_group(part, c):
    groups = lax.axis_size("groups")
    return lax.ppermute(part, "groups", [((i + c) % groups, i) for i in range(groups)])


def query_bounds(lengths, pair, here, rows):
    ends = jnp.cumsum(lengths)
    span = jnp.arange(rows, dtype=jnp.int32)
    place_of = jnp.concatenate([(QUAD * pair + (here ^ k)) * rows + span for k in range(QUAD)])
    begin = jnp.max(jnp.where(ends[None, :] <= place_of[:, None], ends[None, :], 0), axis=1)
    return begin[:, None], place_of[:, None]


def on_device(
    query_plain, query_rotary, key_latent, key_rotary, absorb_weight, value_weight, lengths
):
    rows, head_count, plain = query_plain.shape
    rotary = key_rotary.shape[1]
    depth = key_latent.shape[1]
    held = absorb_weight.shape[0]
    pairs, groups = lax.axis_size("pair"), lax.axis_size("groups")
    names = ("groups", "pair", "side", "core")
    group, pair, side, core = (lax.axis_index(name) for name in names)
    here = 2 * side + core
    place = jnp.stack([here, pair, group]).astype(jnp.int32)
    by_group = held == groups * UNIT and plain == 128 and UNIT * rotary == 128
    by_group = by_group and pairs & (pairs - 1) == 0

    def own(weight, c):
        return lax.dynamic_slice_in_dim(weight, (group + c) % groups * UNIT, UNIT, 0)

    def near_quad(weight):
        part = own(weight, 0)
        return jnp.concatenate([part, across(part, 1)])

    def far_quads(weight):
        distance = 2
        while distance < pairs:
            weight = jnp.concatenate([weight, across(weight, distance)])
            distance *= 2
        return weight

    joined = jnp.concatenate([key_latent, key_rotary], axis=1)
    before = lax.ppermute(joined, "pair", [(i - 1, i) for i in range(1, pairs)])
    if by_group:
        absorb = near_quad(after(absorb_weight, joined))
        near, far = pack(place, query_plain, query_rotary, pairs, groups)
        value = near_quad(after(value_weight, absorb))
        absorb = far_quads(absorb)
        value = far_quads(after(value, absorb))
    else:
        absorb = lax.all_gather(absorb_weight, "pair", axis=0, tiled=True)
        value = lax.all_gather(value_weight, "pair", axis=0, tiled=True)
        flat = query_plain.reshape(rows, head_count * plain)
        near, far = pack_by_slices(place, flat, query_rotary, pairs)
    chunks = len(far)

    keys = jnp.stack([before, joined])
    keys = jnp.concatenate([keys, swap(keys, 2)])
    near = [near[0], swap(near[1], 1)]
    coming = [swap(far[0][k - 2], k) for k in (2, 3)]
    begin, end = query_bounds(lengths, pair, here, rows)
    latent, turned, bias = prepare_keys(place, keys, swap(keys, 1), begin, end, depth)

    sent, parts = (), []
    for c in range(chunks):
        arrived = coming
        if c + 1 < chunks:
            following = after(far[c + 1], *arrived)
            coming = [swap(following[k - 2], k) for k in (2, 3)]
        absorb_c, value_c = absorb, value
        if c:
            absorb_c = jnp.concatenate([own(absorb_weight, c), from_group(absorb[UNIT:], c)])
            value_c = jnp.concatenate([own(value_weight, c), from_group(value[UNIT:], c)])
        arrived = after(arrived, *sent)
        mixed = attend(place, near, arrived, c, absorb_c, turned, latent, bias, rotary)
        if c == 0:
            value_c = value = after(value, mixed)
        sent = list(value_product(mixed, value_c, 1))
        sent = list(value_product(mixed, value_c, 0)) + sent
        parts.append([sent[0]] + [swap(sent[k], k) for k in range(1, QUAD)])
    return join(place, parts, pairs, by_group)


def solution(mesh):
    groups, ctx = mesh.shape["groups"], mesh.shape["ctx"]
    names = ("groups", "pair", "side", "core")
    fine = Mesh(np.asarray(mesh.devices).reshape(groups, ctx // QUAD, 2, 2), names)
    return jax.shard_map(
        on_device,
        mesh=fine,
        in_specs=(
            P(names, None, None),
            P(names, None),
            P(names, None),
            P(names, None),
            P(names[1:], None, None),
            P(names[1:], None, None),
            P("groups"),
        ),
        out_specs=P(names, None),
        check_vma=False,
    )
```

```python
import functools
import math

import jax
import jax.numpy as jnp
import numpy as np
from jax import lax
from jax.experimental import pallas as pl
from jax.experimental.pallas import tpu as pltpu
from jax.sharding import Mesh, PartitionSpec as P

QUAD = 4
UNIT = 2
STEP_HEADS = 4
STRIP = 32


def dot(a, b):
    return jnp.dot(a, b, preferred_element_type=jnp.float32)


def call(kernel, mib=16, **kw):
    return pl.pallas_call(
        kernel, compiler_params=pltpu.CompilerParams(vmem_limit_bytes=mib * 2**20), **kw
    )


def take_heads(pieces, held):
    where = []
    for piece in pieces:
        where += [(piece, h) for h in range(piece.shape[0])]
    for first in range(0, len(where), STEP_HEADS):

        @pl.when(pl.program_id(0) == first // STEP_HEADS)
        def _():
            for h in range(STEP_HEADS):
                piece, at = where[first + h]
                held[h] = piece[at]


def order_of(quad, here, pairs):
    distance = quad ^ here
    order = jnp.where(distance == 1, pairs - 1, distance - 1)
    return jnp.where(distance == 0, 0, order)


def pack_kernel(groups, place, plain, rotary, *refs):
    both, (single, flat) = refs[:-2], refs[-2:]
    rows, heads, width = plain.shape
    single[...] = plain[...].astype(jnp.float32).reshape(rows * heads, width)
    for head in range(heads):
        part = single[pl.ds(head, rows, stride=heads), :]
        flat[:, head * width : (head + 1) * width] = part.astype(flat.dtype)
    wide, thin = UNIT * width, rotary.shape[1] // (QUAD * groups)
    for c in range(groups):
        for k in range(QUAD):
            at = (place[0] ^ k) * groups + lax.rem(place[2] + c, groups)
            out = both[k].at[c] if k < 2 else both[2 + c * 2 + k - 2]
            out[:, :wide] = flat[:, pl.ds(pl.multiple_of(at * wide, wide), wide)]
            out[:, wide:] = rotary[:, pl.ds(pl.multiple_of(at * thin, thin), thin)]


def pack(place, plain, rotary, pairs, groups):
    rows, heads, wide = plain.shape
    held = heads // pairs
    thin = rotary.shape[1] // pairs
    width = (held * wide + thin) // (QUAD * groups)
    at = lambda i, place: order_of(i, place[1], pairs)
    every = pl.BlockSpec((groups, rows, width), lambda i, place: (0, 0, at(i, place)))
    one = pl.BlockSpec((rows, width), lambda i, place: (0, at(i, place)))
    packs = call(
        functools.partial(pack_kernel, groups),
        grid_spec=pltpu.PrefetchScalarGridSpec(
            num_scalar_prefetch=1,
            grid=(pairs,),
            in_specs=[
                pl.BlockSpec((rows, held, wide), lambda i, place: (0, i, 0)),
                pl.BlockSpec((rows, thin), lambda i, place: (0, i)),
            ],
            out_specs=[every] * 2 + [one] * (2 * groups),
            scratch_shapes=[
                pltpu.VMEM((rows * held, wide), jnp.float32),
                pltpu.VMEM((rows, held * wide), plain.dtype),
            ],
        ),
        out_shape=[jax.ShapeDtypeStruct((groups, rows, pairs * width), plain.dtype)] * 2
        + [jax.ShapeDtypeStruct((rows, pairs * width), plain.dtype)] * (2 * groups),
        name="pack",
    )(place, plain, rotary)
    return packs[:2], [list(packs[2 + 2 * c : 4 + 2 * c]) for c in range(groups)]


def pack_by_slices(place, plain, rotary, pairs):
    def sets(array):
        width = array.shape[1] // (QUAD * pairs)
        pick = lambda s: [
            array[:, (QUAD * i + s) * width : (QUAD * i + s + 1) * width] for i in range(pairs)
        ]
        whole = jnp.stack([jnp.concatenate(pick(s), axis=1) for s in range(QUAD)])
        steps = whole.shape[2] // (UNIT * (array.shape[1] // heads))
        return whole.reshape(QUAD, array.shape[0], steps, -1)

    heads = plain.shape[1] // 128
    both = jnp.concatenate([sets(plain), sets(rotary)], axis=3)
    both = both.reshape(QUAD, plain.shape[0], -1)
    packs = [lax.dynamic_index_in_dim(both, place[0] ^ k, 0, False) for k in range(QUAD)]
    return [pack[None] for pack in packs[:2]], [packs[2:]]


def keys_kernel(place, near, far, begin, end, latent, turned, bias):
    rows, depth = near.shape[1], latent.shape[1]
    side, core = place[0] // 2, place[0] % 2
    for c, blocks in enumerate((near, far)):
        for k in range(2):
            for quad in range(2):
                first = (quad * 2 + (side ^ k)) * 2 * rows + c * rows
                at = pl.ds(pl.multiple_of(first, rows), rows)
                block = blocks[k * 2 + quad]
                latent[at, :] = block[:, :depth]
                rotary = block[:, depth:]
                turned[:depth, at] = block[:, :depth].T
                turned[depth:, at] = jnp.concatenate([rotary, rotary], axis=1).T
    count = bias.shape[1]
    spot = lax.broadcasted_iota(jnp.int32, (2 * rows, count), 1) ^ (core * rows)
    for half in range(2):
        at = slice(half * 2 * rows, (half + 1) * 2 * rows)
        spots = spot + (QUAD * (place[1] - 1) + 2 * (side ^ half)) * rows
        allowed = (spots >= begin[at, :]) & (spots <= end[at, :])
        bias[at, :] = jnp.where(allowed, jnp.float32(0.0), jnp.float32(-1e30))


def prepare_keys(place, near, far, begin, end, depth):
    rows, wide = near.shape[1:]
    whole = pl.BlockSpec(memory_space=pltpu.VMEM)
    return call(
        keys_kernel,
        in_specs=[pl.BlockSpec(memory_space=pltpu.SMEM)] + [whole] * 4,
        out_specs=[whole] * 3,
        out_shape=[
            jax.ShapeDtypeStruct((2 * QUAD * rows, depth), near.dtype),
            jax.ShapeDtypeStruct((2 * wide - depth, 2 * QUAD * rows), near.dtype),
            jax.ShapeDtypeStruct((QUAD * rows, (QUAD + 2) * rows), jnp.float32),
        ],
        name="keys",
    )(place, near, far, begin, end)


def attend_kernel(factor, plain, rotary, place, *refs):
    packs, pieces = refs[:QUAD], refs[QUAD:-7]
    keys, latent, bias, mixed, absorb, scores, weights = refs[-7:]
    take_heads(pieces, absorb)
    rows = packs[0].shape[0]
    both, count = 2 * rows, bias.shape[1]
    side = place[0] // 2
    lane = lax.broadcasted_iota(jnp.int32, (both, 2 * rotary), 1)
    units = [(half, head) for half in range(2) for head in range(0, STEP_HEADS, 2)]

    def window(half):
        return pl.ds(pl.multiple_of((side ^ half) * both, both), count)

    def score(u):
        half, head = units[u]
        near, far = packs[2 * half], packs[2 * half + 1]
        base = head // UNIT * UNIT * (plain + rotary)
        for h in range(2):
            at = slice(base + (head % UNIT + h) * plain, base + (head % UNIT + h + 1) * plain)
            q = jnp.concatenate([near[:, at], far[:, at]], axis=0)
            q = dot(q, absorb[head + h]).astype(jnp.bfloat16)
            start = base + UNIT * plain + head % UNIT * rotary
            at = slice(start, start + 2 * rotary)
            r = jnp.concatenate([near[:, at], far[:, at]], axis=0)
            mine = (lane < rotary) if h == 0 else (lane >= rotary)
            left = jnp.concatenate([q, jnp.where(mine, r, jnp.zeros_like(r))], axis=1)
            scores[u % 2, h * both : (h + 1) * both, :] = dot(left, keys[:, window(half)])

    def weigh(u):
        half = units[u][0]
        scale = []
        for first in range(0, 2 * both, STRIP):
            at = slice(first, first + STRIP)
            start = half * both + first % both
            s = scores[u % 2, at, :] + bias[start : start + STRIP, :]
            w = jnp.exp2((s - jnp.max(s, axis=-1, keepdims=True)) * factor)
            scale.append(1.0 / jnp.sum(w, axis=-1, keepdims=True))
            weights[u % 2, at, :] = w.astype(jnp.bfloat16)
        return jnp.concatenate(scale, axis=0)

    score(0)
    for u, (half, head) in enumerate(units):
        if u + 1 < len(units):
            score(u + 1)
        scale = weigh(u)
        for h in range(2):
            at = slice(h * both, (h + 1) * both)
            summed = dot(weights[u % 2, at, :], latent[window(half), :])
            mixed[head + h, half * both : (half + 1) * both, :] = (summed * scale[at]).astype(
                jnp.bfloat16
            )


def attend(place, near, far, chunk, absorb, keys, latent, bias, rotary):
    rows = far[0].shape[0]
    heads = sum(piece.shape[0] for piece in absorb)
    plain, depth = absorb[0].shape[1:]
    count = bias.shape[1]
    whole = pl.BlockSpec(memory_space=pltpu.VMEM)
    factor = math.log2(math.e) / math.sqrt(plain + rotary)
    width = STEP_HEADS * (plain + rotary)
    return call(
        functools.partial(attend_kernel, factor, plain, rotary),
        grid_spec=pltpu.PrefetchScalarGridSpec(
            num_scalar_prefetch=1,
            grid=(heads // STEP_HEADS,),
            in_specs=[pl.BlockSpec((None, rows, width), lambda i, place: (chunk, 0, i))] * 2
            + [pl.BlockSpec((rows, width), lambda i, place: (0, i))] * 2
            + [whole] * (len(absorb) + 3),
            out_specs=pl.BlockSpec((STEP_HEADS, QUAD * rows, depth), lambda i, place: (i, 0, 0)),
            scratch_shapes=[
                pltpu.VMEM((STEP_HEADS, plain, depth), jnp.bfloat16),
                pltpu.VMEM((2, QUAD * rows, count), jnp.float32),
                pltpu.VMEM((2, QUAD * rows, count), jnp.bfloat16),
            ],
        ),
        out_shape=jax.ShapeDtypeStruct((heads, QUAD * rows, depth), jnp.bfloat16),
        cost_estimate=pl.CostEstimate(
            flops=2 * heads * QUAD * rows * (plain * depth + (2 * depth + 2 * rotary) * count),
            bytes_accessed=2 * heads * depth * (QUAD * rows + plain),
            transcendentals=heads * QUAD * rows * count,
        ),
        name="attend",
        mib=24,
    )(place, *near, *far, *absorb, keys, latent, bias)


def value_kernel(mixed, *refs):
    pieces, (one, two, value) = refs[:-3], refs[-3:]
    take_heads(pieces, value)
    rows, width = one.shape[0], value.shape[2]
    for head in range(STEP_HEADS):
        out = dot(mixed[head], value[head]).astype(jnp.bfloat16)
        one[:, head * width : (head + 1) * width] = out[:rows]
        two[:, head * width : (head + 1) * width] = out[rows:]


def value_product(mixed, value, half):
    heads, rows, depth = mixed.shape
    rows, width = rows // QUAD, value[0].shape[2]
    out = pl.BlockSpec((rows, STEP_HEADS * width), lambda i: (0, i))
    return call(
        value_kernel,
        grid=(heads // STEP_HEADS,),
        in_specs=[pl.BlockSpec((STEP_HEADS, 2 * rows, depth), lambda i: (i, half, 0))]
        + [pl.BlockSpec(memory_space=pltpu.VMEM)] * len(value),
        out_specs=[out] * 2,
        out_shape=[jax.ShapeDtypeStruct((rows, heads * width), jnp.bfloat16)] * 2,
        scratch_shapes=[pltpu.VMEM((STEP_HEADS, depth, width), jnp.bfloat16)],
        cost_estimate=pl.CostEstimate(
            flops=4 * heads * rows * depth * width,
            bytes_accessed=2 * heads * (2 * rows * depth + width * depth + 2 * rows * width),
            transcendentals=0,
        ),
        name="value",
    )(mixed, *value)


def join_kernel(chunks, shifted, place, *refs):
    parts, out = refs[:-1], refs[-1]
    width = out.shape[1] // (chunks * QUAD)
    block = pl.program_id(0)
    if shifted:
        block = order_of(block, place[1], pl.num_programs(0))
    source = pl.ds(pl.multiple_of(block * width, width), width)
    for c in range(chunks):
        for k in range(QUAD):
            at = (place[0] ^ k) * chunks + lax.rem(place[2] + c, chunks)
            out[:, pl.ds(pl.multiple_of(at * width, width), width)] = parts[c * QUAD + k][:, source]


def join(place, parts, pairs, shifted):
    chunks = len(parts)
    rows, wide = parts[0][0].shape
    return call(
        functools.partial(join_kernel, chunks, shifted),
        grid_spec=pltpu.PrefetchScalarGridSpec(
            num_scalar_prefetch=1,
            grid=(pairs,),
            in_specs=[pl.BlockSpec(memory_space=pltpu.VMEM)] * (chunks * QUAD),
            out_specs=pl.BlockSpec(
                (rows, chunks * QUAD * wide // pairs), lambda i, place: (0, i)
            ),
        ),
        out_shape=jax.ShapeDtypeStruct((rows, chunks * QUAD * wide), jnp.bfloat16),
        name="join",
    )(place, *[part for chunk in parts for part in chunk])


def swap(block, k):
    return lax.ppermute(block, ("side", "core"), [(i, i ^ k) for i in range(QUAD)])


def after(later, *earlier):
    return lax.optimization_barrier((later, earlier))[0]


def across(part, distance):
    pairs = lax.axis_size("pair")
    return lax.ppermute(part, "pair", [(i, i ^ distance) for i in range(pairs)])


def from_group(part, c):
    groups = lax.axis_size("groups")
    return lax.ppermute(part, "groups", [((i + c) % groups, i) for i in range(groups)])


def query_bounds(lengths, pair, here, rows):
    ends = jnp.cumsum(lengths)
    span = jnp.arange(rows, dtype=jnp.int32)
    place_of = jnp.concatenate([(QUAD * pair + (here ^ k)) * rows + span for k in range(QUAD)])
    begin = jnp.max(jnp.where(ends[None, :] <= place_of[:, None], ends[None, :], 0), axis=1)
    return begin[:, None], place_of[:, None]


def on_device(
    query_plain, query_rotary, key_latent, key_rotary, absorb_weight, value_weight, lengths
):
    rows, head_count, plain = query_plain.shape
    rotary = key_rotary.shape[1]
    depth = key_latent.shape[1]
    held = absorb_weight.shape[0]
    pairs, groups = lax.axis_size("pair"), lax.axis_size("groups")
    names = ("groups", "pair", "side", "core")
    group, pair, side, core = (lax.axis_index(name) for name in names)
    here = 2 * side + core
    place = jnp.stack([here, pair, group]).astype(jnp.int32)
    by_group = held == groups * UNIT and plain == 128 and UNIT * rotary == 128
    by_group = by_group and pairs & (pairs - 1) == 0

    def own(weight, c):
        return lax.dynamic_slice_in_dim(weight, (group + c) % groups * UNIT, UNIT, 0)

    def far_quads(near):
        known, far, distance = near, [], 2
        while distance < pairs:
            far.append(across(known, distance))
            known = jnp.concatenate([known, far[-1]])
            distance *= 2
        return far

    joined = jnp.concatenate([key_latent, key_rotary], axis=1)
    if by_group:
        absorb = [own(absorb_weight, 0)]
        absorb += [across(absorb[0], distance) for distance in (*range(2, pairs), 1)]
        joined = after(joined, absorb[0])
    before = lax.ppermute(joined, "pair", [(i - 1, i) for i in range(1, pairs)])
    keys = jnp.stack([before, joined])
    if by_group:
        near, far = pack(place, after(query_plain, keys), query_rotary, pairs, groups)
    else:
        absorb = [lax.all_gather(absorb_weight, "pair", axis=0, tiled=True)]
        value = [lax.all_gather(value_weight, "pair", axis=0, tiled=True)]
        flat = query_plain.reshape(rows, head_count * plain)
        near, far = pack_by_slices(place, flat, query_rotary, pairs)
    chunks = len(far)

    keys = jnp.concatenate([keys, swap(keys, 2)])
    if by_group:
        value = [own(after(value_weight, keys), 0)]
        value.append(across(value[0], 1))
        value[1:1] = far_quads(after(jnp.concatenate(value), *absorb))
    near = [near[0], swap(near[1], 1)]
    coming = [swap(far[0][k - 2], k) for k in (2, 3)]
    begin, end = query_bounds(lengths, pair, here, rows)
    latent, turned, bias = prepare_keys(place, keys, swap(keys, 1), begin, end, depth)

    sent, parts = (), []
    for c in range(chunks):
        arrived = coming
        if c + 1 < chunks:
            following = after(far[c + 1], *arrived)
            coming = [swap(following[k - 2], k) for k in (2, 3)]
        absorb_c, value_c = absorb, value
        if c:
            absorb_c = [own(absorb_weight, c), from_group(jnp.concatenate(absorb[1:]), c)]
            value_c = [own(value_weight, c), from_group(jnp.concatenate(value[1:]), c)]
        arrived = after(arrived, *sent)
        mixed = attend(place, near, arrived, c, absorb_c, turned, latent, bias, rotary)
        if c == 0:
            value_c = value = after(value, mixed)
        sent = list(value_product(mixed, value_c, 1))
        sent = list(value_product(mixed, value_c, 0)) + sent
        parts.append([sent[0]] + [swap(sent[k], k) for k in range(1, QUAD)])
    return join(place, parts, pairs, by_group)


def solution(mesh):
    groups, ctx = mesh.shape["groups"], mesh.shape["ctx"]
    names = ("groups", "pair", "side", "core")
    fine = Mesh(np.asarray(mesh.devices).reshape(groups, ctx // QUAD, 2, 2), names)
    return jax.shard_map(
        on_device,
        mesh=fine,
        in_specs=(
            P(names, None, None),
            P(names, None),
            P(names, None),
            P(names, None),
            P(names[1:], None, None),
            P(names[1:], None, None),
            P("groups"),
        ),
        out_specs=P(names, None),
        check_vma=False,
    )
```

```python
import functools
import math

import jax
import jax.numpy as jnp
import numpy as np
from jax import lax
from jax.experimental import pallas as pl
from jax.experimental.pallas import tpu as pltpu
from jax.sharding import Mesh, PartitionSpec as P

QUAD = 4
JOIN_ORDER = (0, 2, 3, 1)
UNIT = 2
STEP_HEADS = 4
STRIP = 32


def dot(a, b):
    return jnp.dot(a, b, preferred_element_type=jnp.float32)


def call(kernel, mib=16, **kw):
    return pl.pallas_call(
        kernel,
        compiler_params=pltpu.CompilerParams(vmem_limit_bytes=mib * 2**20),
        cost_estimate=pl.CostEstimate(flops=0, bytes_accessed=0, transcendentals=0),
        **kw,
    )


def take_heads(pieces, held):
    where = []
    for piece in pieces:
        where += [(piece, h) for h in range(piece.shape[0])]
    for first in range(0, len(where), STEP_HEADS):

        @pl.when(pl.program_id(0) == first // STEP_HEADS)
        def _():
            for h in range(STEP_HEADS):
                piece, at = where[first + h]
                held[h] = piece[at, piece.shape[1] - held.shape[1] :, :]


def order_of(quad, here, pairs):
    distance = quad ^ here
    order = jnp.where(distance == 1, pairs - 1, distance - 1)
    return jnp.where(distance == 0, 0, order)


def pack_kernel(groups, place, plain, rotary, *refs):
    both, (single, flat) = refs[:-2], refs[-2:]
    rows, heads, width = plain.shape
    single[...] = plain[...].astype(jnp.float32).reshape(rows * heads, width)
    for head in range(heads):
        part = single[pl.ds(head, rows, stride=heads), :]
        flat[:, head * width : (head + 1) * width] = part.astype(flat.dtype)
    wide, thin = UNIT * width, rotary.shape[1] // (QUAD * groups)
    for c in range(groups):
        for k in range(QUAD):
            at = (place[0] ^ k) * groups + lax.rem(place[2] + c, groups)
            out = both[k].at[c] if k < 2 else both[2 + c * 2 + k - 2]
            out[:, :wide] = flat[:, pl.ds(pl.multiple_of(at * wide, wide), wide)]
            out[:, wide:] = rotary[:, pl.ds(pl.multiple_of(at * thin, thin), thin)]


def pack(place, plain, rotary, pairs, groups):
    rows, heads, wide = plain.shape
    held = heads // pairs
    thin = rotary.shape[1] // pairs
    width = (held * wide + thin) // (QUAD * groups)
    at = lambda i, place: order_of(i, place[1], pairs)
    every = pl.BlockSpec((groups, rows, width), lambda i, place: (0, 0, at(i, place)))
    one = pl.BlockSpec((rows, width), lambda i, place: (0, at(i, place)))
    packs = call(
        functools.partial(pack_kernel, groups),
        grid_spec=pltpu.PrefetchScalarGridSpec(
            num_scalar_prefetch=1,
            grid=(pairs,),
            in_specs=[
                pl.BlockSpec((rows, held, wide), lambda i, place: (0, i, 0)),
                pl.BlockSpec((rows, thin), lambda i, place: (0, i)),
            ],
            out_specs=[every] * 2 + [one] * (2 * groups),
            scratch_shapes=[
                pltpu.VMEM((rows * held, wide), jnp.float32),
                pltpu.VMEM((rows, held * wide), plain.dtype),
            ],
        ),
        out_shape=[jax.ShapeDtypeStruct((groups, rows, pairs * width), plain.dtype)] * 2
        + [jax.ShapeDtypeStruct((rows, pairs * width), plain.dtype)] * (2 * groups),
        name="pack",
    )(place, plain, rotary)
    return packs[:2], [list(packs[2 + 2 * c : 4 + 2 * c]) for c in range(groups)]


def pack_by_slices(place, plain, rotary, pairs):
    def sets(array):
        width = array.shape[1] // (QUAD * pairs)
        pick = lambda s: [
            array[:, (QUAD * i + s) * width : (QUAD * i + s + 1) * width] for i in range(pairs)
        ]
        whole = jnp.stack([jnp.concatenate(pick(s), axis=1) for s in range(QUAD)])
        steps = whole.shape[2] // (UNIT * (array.shape[1] // heads))
        return whole.reshape(QUAD, array.shape[0], steps, -1)

    heads = plain.shape[1] // 128
    both = jnp.concatenate([sets(plain), sets(rotary)], axis=3)
    both = both.reshape(QUAD, plain.shape[0], -1)
    packs = [lax.dynamic_index_in_dim(both, place[0] ^ k, 0, False) for k in range(QUAD)]
    return [pack[None] for pack in packs[:2]], [packs[2:]]


def start_kernel(groups, place, *refs):
    absorb, value, latent, rotary = refs[:groups], refs[groups : 2 * groups], *refs[2 * groups :][:2]
    outs = refs[2 * groups + 2 :]
    stacked, plain, pair, joined = outs[:groups], outs[groups : 2 * groups], *outs[2 * groups :]
    depth, width = value[0].shape[1:]
    for c in range(groups):
        for first in range(0, depth, width):
            stacked[c][:, first : first + width, :] = absorb[c][:, :, first : first + width]
        plain[c][...] = value[c][...]
    pair[:, :depth, :] = stacked[0][...]
    pair[:, depth:, :] = value[0][...]
    joined[:, :depth] = latent[...]
    joined[:, depth:] = jnp.concatenate([rotary[...]] * 2, axis=0).T


def start(place, absorb, value, latent, rotary, groups):
    held = absorb.shape[0] // groups
    spec = lambda a: [
        pl.BlockSpec(
            (held, *a.shape[1:]),
            functools.partial(lambda c, i, place: (lax.rem(place[2] + c, groups), 0, 0), c),
        )
        for c in range(groups)
    ]
    whole = lambda shape: pl.BlockSpec(shape, lambda i, place: (0,) * len(shape))
    part = (held, *value.shape[1:])
    pair = (held, 2 * value.shape[1], value.shape[2])
    joined = (latent.shape[0], latent.shape[1] + 2 * rotary.shape[1])
    shapes = [part] * (2 * groups) + [pair, joined]
    outs = call(
        functools.partial(start_kernel, groups),
        grid_spec=pltpu.PrefetchScalarGridSpec(
            num_scalar_prefetch=1,
            grid=(1,),
            in_specs=spec(absorb)
            + spec(value)
            + [whole(latent.shape), whole(rotary.shape[::-1])],
            out_specs=[whole(shape) for shape in shapes],
        ),
        out_shape=[jax.ShapeDtypeStruct(shape, latent.dtype) for shape in shapes],
        name="start",
    )(place, *([absorb] * groups), *([value] * groups), latent, rotary.T)
    return outs[:groups], outs[groups : 2 * groups], outs[-2], outs[-1]


def keys_kernel(place, near, far, begin, end, latent, turned, bias):
    rows, depth = near.shape[1], latent.shape[1]
    side, core = place[0] // 2, place[0] % 2
    for c, blocks in enumerate((near, far)):
        for k in range(2):
            for quad in range(2):
                first = (quad * 2 + (side ^ k)) * 2 * rows + c * rows
                at = pl.ds(pl.multiple_of(first, rows), rows)
                block = blocks[k * 2 + quad]
                latent[at, :] = block[:, :depth]
                turned[:depth, at] = block[:, :depth].T
                turned[depth:, at] = block[:, depth:].T
    count = bias.shape[1]
    spot = lax.broadcasted_iota(jnp.int32, (2 * rows, count), 1) ^ (core * rows)
    for half in range(2):
        at = slice(half * 2 * rows, (half + 1) * 2 * rows)
        spots = spot + (QUAD * (place[1] - 1) + 2 * (side ^ half)) * rows
        allowed = (spots >= begin[at, :]) & (spots <= end[at, :])
        bias[at, :] = jnp.where(allowed, jnp.float32(0.0), jnp.float32(-1e30))


def prepare_keys(place, near, far, begin, end, depth):
    rows, wide = near.shape[1:]
    whole = pl.BlockSpec(memory_space=pltpu.VMEM)
    return call(
        keys_kernel,
        in_specs=[pl.BlockSpec(memory_space=pltpu.SMEM)] + [whole] * 4,
        out_specs=[whole] * 3,
        out_shape=[
            jax.ShapeDtypeStruct((2 * QUAD * rows, depth), near.dtype),
            jax.ShapeDtypeStruct((wide, 2 * QUAD * rows), near.dtype),
            jax.ShapeDtypeStruct((QUAD * rows, (QUAD + 2) * rows), jnp.float32),
        ],
        name="keys",
    )(place, near, far, begin, end)


def attend_kernel(factor, half, chunk, rotary, place, *refs):
    sources, pieces = refs[:2], refs[2:-10]
    keys, latent, bias, mixed, near, far, absorb, scores, weights, sems = refs[-10:]
    rows, (heads, plain, depth), count = near.shape[0], absorb.shape, bias.shape[1]
    both = 2 * rows

    copies = [
        pltpu.make_async_copy(source if chunk is None else source.at[chunk], held, sems.at[n])
        for n, (source, held) in enumerate(zip(sources, (near, far)))
    ]
    ready, first = [], 0
    for piece in pieces:
        held = absorb.at[pl.ds(first, piece.shape[0])]
        width = depth if piece.shape[1] == plain else piece.shape[2]
        for at in range(0, depth, width):
            source = piece if width == depth else piece.at[:, pl.ds(at // width * plain, plain)]
            target = held if width == depth else held.at[:, :, pl.ds(at, width)]
            copies.append(pltpu.make_async_copy(source, target, sems.at[len(copies)]))
            ready.append((first, copies[-1]))
        first += piece.shape[0]
    for copy in copies:
        copy.start()
    copies[0].wait()
    copies[1].wait()

    window = pl.ds(pl.multiple_of((place[0] // 2 ^ half) * both, both), count)
    lane = lax.broadcasted_iota(jnp.int32, (both, 2 * rotary), 1)

    def score(u):
        for at_head, copy in ready:
            if at_head == 2 * u:
                copy.wait()
        base = 2 * u // UNIT * UNIT * (plain + rotary)
        for h in range(2):
            at = slice(base + h * plain, base + (h + 1) * plain)
            q = jnp.concatenate([near[:, at], far[:, at]], axis=0)
            q = dot(q, absorb[2 * u + h]).astype(jnp.bfloat16)
            at = slice(base + UNIT * plain, base + UNIT * plain + 2 * rotary)
            r = jnp.concatenate([near[:, at], far[:, at]], axis=0)
            mine = (lane < rotary) if h == 0 else (lane >= rotary)
            left = jnp.concatenate([q, jnp.where(mine, r, jnp.zeros_like(r))], axis=1)
            scores[u % 2, h * both : (h + 1) * both, :] = dot(left, keys[:, window])

    def weigh(u):
        scale = []
        for first in range(0, 2 * both, STRIP):
            at = slice(first, first + STRIP)
            start = half * both + first % both
            s = scores[u % 2, at, :] + bias[start : start + STRIP, :]
            w = jnp.exp2((s - jnp.max(s, axis=-1, keepdims=True)) * factor)
            scale.append(1.0 / jnp.sum(w, axis=-1, keepdims=True))
            weights[u % 2, at, :] = w.astype(jnp.bfloat16)
        return jnp.concatenate(scale, axis=0)

    score(0)
    for u in range(heads // 2):
        if u + 1 < heads // 2:
            score(u + 1)
        scale = weigh(u)
        for h in range(2):
            at = slice(h * both, (h + 1) * both)
            summed = dot(weights[u % 2, at, :], latent[window, :])
            mixed[2 * u + h] = (summed * scale[at]).astype(jnp.bfloat16)


def attend(place, sources, half, chunk, absorb, keys, latent, bias, rotary):
    rows, wide = sources[0].shape[-2:]
    heads = sum(piece.shape[0] for piece in absorb)
    depth, plain = latent.shape[1], wide // heads - rotary
    count = bias.shape[1]
    whole, far = pl.BlockSpec(memory_space=pltpu.VMEM), pl.BlockSpec(memory_space=pltpu.HBM)
    factor = math.log2(math.e) / math.sqrt(plain + rotary)
    return call(
        functools.partial(attend_kernel, factor, half, chunk, rotary),
        in_specs=[pl.BlockSpec(memory_space=pltpu.SMEM)]
        + [far] * (2 + len(absorb))
        + [whole] * 3,
        out_specs=whole,
        out_shape=jax.ShapeDtypeStruct((heads, 2 * rows, depth), jnp.bfloat16),
        scratch_shapes=[
            pltpu.VMEM((rows, wide), jnp.bfloat16),
            pltpu.VMEM((rows, wide), jnp.bfloat16),
            pltpu.VMEM((heads, plain, depth), jnp.bfloat16),
            pltpu.VMEM((2, QUAD * rows, count), jnp.float32),
            pltpu.VMEM((2, QUAD * rows, count), jnp.bfloat16),
            pltpu.SemaphoreType.DMA((2 + len(absorb) * depth // 128,)),
        ],
        name="attend",
        mib=20,
    )(place, *sources, *absorb, keys, latent, bias)


def value_kernel(mixed, *refs):
    pieces, (one, two, value) = refs[:-3], refs[-3:]
    take_heads(pieces, value)
    rows, width = one.shape[0], value.shape[2]
    for head in range(STEP_HEADS):
        out = dot(mixed[head], value[head]).astype(jnp.bfloat16)
        one[:, head * width : (head + 1) * width] = out[:rows]
        two[:, head * width : (head + 1) * width] = out[rows:]


def value_product(mixed, value):
    heads, rows, depth = mixed.shape
    rows, width = rows // 2, value[0].shape[2]
    out = pl.BlockSpec((rows, STEP_HEADS * width), lambda i: (0, i))
    return call(
        value_kernel,
        grid=(heads // STEP_HEADS,),
        in_specs=[pl.BlockSpec((STEP_HEADS, 2 * rows, depth), lambda i: (i, 0, 0))]
        + [pl.BlockSpec(memory_space=pltpu.VMEM)] * len(value),
        out_specs=[out] * 2,
        out_shape=[jax.ShapeDtypeStruct((rows, heads * width), jnp.bfloat16)] * 2,
        scratch_shapes=[pltpu.VMEM((STEP_HEADS, depth, width), jnp.bfloat16)],
        name="value",
    )(mixed, *value)


def join_kernel(chunks, shifted, place, *refs):
    parts, out = refs[:-1], refs[-1]
    width = out.shape[1] // (chunks * QUAD)
    block = pl.program_id(0)
    if shifted:
        block = order_of(block, place[1], pl.num_programs(0))
    source = pl.ds(pl.multiple_of(block * width, width), width)
    for c in range(chunks):
        for n, k in enumerate(JOIN_ORDER):
            at = (place[0] ^ k) * chunks + lax.rem(place[2] + c, chunks)
            out[:, pl.ds(pl.multiple_of(at * width, width), width)] = parts[c * QUAD + n][:, source]


def join(place, parts, pairs, shifted):
    chunks = len(parts)
    rows, wide = parts[0][0].shape
    return call(
        functools.partial(join_kernel, chunks, shifted),
        grid_spec=pltpu.PrefetchScalarGridSpec(
            num_scalar_prefetch=1,
            grid=(pairs,),
            in_specs=[pl.BlockSpec(memory_space=pltpu.VMEM)] * (chunks * QUAD),
            out_specs=pl.BlockSpec(
                (rows, chunks * QUAD * wide // pairs), lambda i, place: (0, i)
            ),
        ),
        out_shape=jax.ShapeDtypeStruct((rows, chunks * QUAD * wide), jnp.bfloat16),
        name="join",
    )(place, *[chunk[k] for chunk in parts for k in JOIN_ORDER])


def swap(block, k):
    return lax.ppermute(block, ("side", "core"), [(i, i ^ k) for i in range(QUAD)])


def after(later, *earlier):
    return lax.optimization_barrier((later, earlier))[0]


def across(part, distance):
    pairs = lax.axis_size("pair")
    return lax.ppermute(part, "pair", [(i, i ^ distance) for i in range(pairs)])


def from_group(part, c):
    groups = lax.axis_size("groups")
    return lax.ppermute(part, "groups", [((i + c) % groups, i) for i in range(groups)])


def query_bounds(lengths, pair, here, rows):
    ends = jnp.cumsum(lengths)
    span = jnp.arange(rows, dtype=jnp.int32)
    place_of = jnp.concatenate([(QUAD * pair + (here ^ k)) * rows + span for k in range(QUAD)])
    begin = jnp.max(jnp.where(ends[None, :] <= place_of[:, None], ends[None, :], 0), axis=1)
    return begin[:, None], place_of[:, None]


def on_device(
    query_plain, query_rotary, key_latent, key_rotary, absorb_weight, value_weight, lengths
):
    rows, head_count, plain = query_plain.shape
    rotary = key_rotary.shape[1]
    depth = key_latent.shape[1]
    held = absorb_weight.shape[0]
    pairs, groups = lax.axis_size("pair"), lax.axis_size("groups")
    names = ("groups", "pair", "side", "core")
    group, pair, side, core = (lax.axis_index(name) for name in names)
    here = 2 * side + core
    place = jnp.stack([here, pair, group]).astype(jnp.int32)
    by_group = held == groups * UNIT and plain == 128 and UNIT * rotary == 128
    by_group = by_group and pairs & (pairs - 1) == 0

    def far_quads(near):
        known, far, distance = near, [], 2
        while distance < pairs:
            far.append(across(known, distance))
            known = jnp.concatenate([known, far[-1]])
            distance *= 2
        return far

    if by_group:
        mine, mine_value, pair_out, joined = start(
            place, absorb_weight, value_weight, key_latent, key_rotary, groups
        )
        near_pair = across(pair_out, 1)
        absorb = [mine[0]] + [across(mine[0], d) for d in range(2, pairs)] + [near_pair]
    else:
        joined = jnp.concatenate([key_latent, key_rotary, key_rotary], axis=1)
    before = lax.ppermute(joined, "pair", [(i - 1, i) for i in range(1, pairs)])
    keys = jnp.stack([before, joined])
    if by_group:
        near, far = pack(place, after(query_plain, keys), query_rotary, pairs, groups)
    else:
        absorb = [lax.all_gather(absorb_weight, "pair", axis=0, tiled=True)]
        value = [lax.all_gather(value_weight, "pair", axis=0, tiled=True)]
        flat = query_plain.reshape(rows, head_count * plain)
        near, far = pack_by_slices(place, flat, query_rotary, pairs)
    chunks = len(far)

    keys = jnp.concatenate([keys, swap(keys, 2)])
    if by_group:
        both = jnp.concatenate([mine_value[0], near_pair[:, depth:]])
        value = [mine_value[0], *far_quads(after(both, *absorb)), near_pair]
    near = [near[0], swap(near[1], 1)]
    coming = [swap(far[0][k - 2], k) for k in (2, 3)]
    begin, end = query_bounds(lengths, pair, here, rows)
    prepared = prepare_keys(place, keys, swap(keys, 1), begin, end, depth)

    def one_half(half, c, sources, absorb_c):
        chunk = None if half else c
        latent, turned, bias = prepared
        return attend(place, sources, half, chunk, absorb_c, turned, latent, bias, rotary)

    parts = []
    for c in range(chunks):
        last = c + 1 == chunks
        arrived = coming
        if not last:
            following = after(far[c + 1], *arrived)
            coming = [swap(following[k - 2], k) for k in (2, 3)]
        if c == 0:
            absorb_c, value_c = absorb, value
        else:
            crossed = from_group(near_pair, c)
            absorb_c = [mine[c], from_group(jnp.concatenate(absorb[1:-1]), c), crossed]
            value_c = [mine_value[c]] + [from_group(piece, c) for piece in value[1:-1]] + [crossed]
        out = [None] * 2
        for half in (1, 0) if last else (0, 1):
            mixed = one_half(half, c, (near, arrived)[half], absorb_c)
            if c == 0:
                value[1:-1] = value_c[1:-1] = after(value_c[1:-1], mixed)
            out[half] = value_product(mixed, value_c)
            near = after(near, *out[half])
        back = swap(out[0][1], 1)
        coming = after(coming, back, *out[1])
        parts.append([out[0][0], back] + [swap(out[1][k - 2], k) for k in (2, 3)])
    return join(place, parts, pairs, by_group)


def solution(mesh):
    groups, ctx = mesh.shape["groups"], mesh.shape["ctx"]
    names = ("groups", "pair", "side", "core")
    fine = Mesh(np.asarray(mesh.devices).reshape(groups, ctx // QUAD, 2, 2), names)
    return jax.shard_map(
        on_device,
        mesh=fine,
        in_specs=(
            P(names, None, None),
            P(names, None),
            P(names, None),
            P(names, None),
            P(names[1:], None, None),
            P(names[1:], None, None),
            P("groups"),
        ),
        out_specs=P(names, None),
        check_vma=False,
    )
```

```python
import functools
import math

import jax
import jax.numpy as jnp
import numpy as np
from jax import lax
from jax.experimental import pallas as pl
from jax.experimental.pallas import tpu as pltpu
from jax.sharding import Mesh, PartitionSpec as P

QUAD = 4
JOIN_ORDER = (0, 2, 3, 1)
UNIT = 2
STEP_HEADS = 4
STRIP = 32


def dot(a, b):
    return jnp.dot(a, b, preferred_element_type=jnp.float32)


def call(kernel, mib=16, moved=0, **kw):
    return pl.pallas_call(
        kernel,
        compiler_params=pltpu.CompilerParams(vmem_limit_bytes=mib * 2**20),
        cost_estimate=pl.CostEstimate(flops=0, bytes_accessed=moved, transcendentals=0),
        **kw,
    )


HBM, IN_VMEM = pl.BlockSpec(memory_space=pltpu.HBM), pl.BlockSpec(memory_space=pltpu.VMEM)
ANY, SMEM = pl.BlockSpec(memory_space=pl.ANY), pl.BlockSpec(memory_space=pltpu.SMEM)


def take_heads(pieces, held):
    where = []
    for piece in pieces:
        where += [(piece, h) for h in range(piece.shape[0])]
    for first in range(0, len(where), STEP_HEADS):

        @pl.when(pl.program_id(0) == first // STEP_HEADS)
        def _():
            for h in range(STEP_HEADS):
                piece, at = where[first + h]
                held[h] = piece[at, piece.shape[1] - held.shape[1] :, :]


def order_of(quad, here, pairs):
    distance = quad ^ here
    order = jnp.where(distance == 1, pairs - 1, distance - 1)
    return jnp.where(distance == 0, 0, order)


def prepare_kernel(groups, pairs, place, *refs):
    plain, rotary, absorb, value = refs[:4]
    packs, refs = refs[4 : 6 + 2 * groups], refs[6 + 2 * groups :]
    stacked, values, pair = refs[:groups], refs[groups : 2 * groups], refs[2 * groups]
    refs = refs[2 * groups + 1 :]
    plain_in, rotary_in, absorb_in, value_in, single, flat, sems = refs
    rows, heads, width = plain_in.shape
    depth = value_in.shape[2]
    held, carried = heads // pairs, absorb_in.shape[1]
    copies = []

    def fetch(source, target):
        copies.append(pltpu.make_async_copy(source, target, sems.at[len(copies)]))
        copies[-1].start()

    for c in range(groups):
        at = pl.ds(lax.rem(place[2] + c, groups) * carried, carried)
        fetch(absorb.at[at], absorb_in.at[c])
        fetch(value.at[at], value_in.at[c])
    for i in range(pairs):
        at = pl.ds(i * held, held)
        fetch(plain.at[:, at], plain_in.at[:, at])
    fetch(rotary, rotary_in)

    for c in range(groups):
        copies[2 * c].wait()
        copies[2 * c + 1].wait()
        for first in range(0, depth, width):
            stacked[c][:, first : first + width, :] = absorb_in[c, :, :, first : first + width]
        values[c][...] = value_in[c]
    pair[:, :depth, :] = stacked[0][...]
    pair[:, depth:, :] = value_in[0]

    wide, thin = UNIT * width, rotary_in.shape[1] // (pairs * QUAD * groups)
    copies[-1].wait()
    for i in range(pairs):
        copies[2 * groups + i].wait()
        part = plain_in[:, i * held : (i + 1) * held, :]
        single[...] = part.astype(jnp.float32).reshape(rows * held, width)
        for head in range(held):
            part = single[pl.ds(head, rows, stride=held), :]
            flat[:, head * width : (head + 1) * width] = part.astype(flat.dtype)
        first = pl.multiple_of(order_of(i, place[1], pairs) * (wide + thin), wide + thin)
        for c in range(groups):
            for k in range(QUAD):
                at = (place[0] ^ k) * groups + lax.rem(place[2] + c, groups)
                out = packs[k].at[c] if k < 2 else packs[2 + c * 2 + k - 2]
                part = flat[:, pl.ds(pl.multiple_of(at * wide, wide), wide)]
                out[:, pl.ds(first, wide)] = part
                at = at * thin + i * thin * QUAD * groups
                part = rotary_in[:, pl.ds(pl.multiple_of(at, thin), thin)]
                out[:, pl.ds(pl.multiple_of(first + wide, thin), thin)] = part


def prepare(place, plain, rotary, absorb, value, pairs, groups):
    rows, heads, wide = plain.shape
    width = (heads * wide + rotary.shape[1]) // (QUAD * groups)
    held = absorb.shape[0] // groups
    part, dtype = (held, *value.shape[1:]), plain.dtype
    shapes = [(groups, rows, width)] * 2 + [(rows, width)] * (2 * groups)
    shapes += [part] * (2 * groups) + [(held, 2 * part[1], part[2])]
    outs = call(
        functools.partial(prepare_kernel, groups, pairs),
        in_specs=[SMEM] + [HBM] * 4,
        out_specs=[IN_VMEM] * len(shapes),
        out_shape=[jax.ShapeDtypeStruct(shape, dtype) for shape in shapes],
        scratch_shapes=[
            pltpu.VMEM(plain.shape, dtype),
            pltpu.VMEM(rotary.shape, dtype),
            pltpu.VMEM((groups, held, *absorb.shape[1:]), dtype),
            pltpu.VMEM((groups, held, *value.shape[1:]), dtype),
            pltpu.VMEM((rows * heads // pairs, wide), jnp.float32),
            pltpu.VMEM((rows, heads // pairs * wide), dtype),
            pltpu.SemaphoreType.DMA((2 * groups + pairs + 1,)),
        ],
        moved=12 * 2**20,
        name="prepare",
    )(place, plain, rotary, absorb, value)
    far = outs[2 : 2 + 2 * groups]
    weights = outs[2 + 2 * groups :]
    return (
        outs[:2],
        [list(far[2 * c : 2 * c + 2]) for c in range(groups)],
        weights[:groups],
        weights[groups : 2 * groups],
        weights[-1],
    )


def pack_by_slices(place, plain, rotary, pairs):
    def sets(array):
        width = array.shape[1] // (QUAD * pairs)
        pick = lambda s: [
            array[:, (QUAD * i + s) * width : (QUAD * i + s + 1) * width] for i in range(pairs)
        ]
        whole = jnp.stack([jnp.concatenate(pick(s), axis=1) for s in range(QUAD)])
        steps = whole.shape[2] // (UNIT * (array.shape[1] // heads))
        return whole.reshape(QUAD, array.shape[0], steps, -1)

    heads = plain.shape[1] // 128
    both = jnp.concatenate([sets(plain), sets(rotary)], axis=3)
    both = both.reshape(QUAD, plain.shape[0], -1)
    packs = [lax.dynamic_index_in_dim(both, place[0] ^ k, 0, False) for k in range(QUAD)]
    return [pack[None] for pack in packs[:2]], [packs[2:]]


def joined_kernel(latent, rotary, joined, rotary_in, sems):
    depth = latent.shape[1]
    copies = [
        pltpu.make_async_copy(rotary, rotary_in, sems.at[0]),
        pltpu.make_async_copy(latent, joined.at[:, pl.ds(0, depth)], sems.at[1]),
    ]
    for copy in copies:
        copy.start()
    copies[0].wait()
    joined[:, depth:] = jnp.concatenate([rotary_in[...]] * 2, axis=0).T
    copies[1].wait()


def join_keys(latent, rotary):
    shape = (latent.shape[0], latent.shape[1] + 2 * rotary.shape[1])
    return call(
        joined_kernel,
        in_specs=[HBM, HBM],
        out_specs=IN_VMEM,
        out_shape=jax.ShapeDtypeStruct(shape, latent.dtype),
        scratch_shapes=[
            pltpu.VMEM(rotary.shape[::-1], rotary.dtype),
            pltpu.SemaphoreType.DMA((2,)),
        ],
        name="joined",
    )(latent, rotary.T)


def keys_kernel(place, lengths, near, far, latent, turned, bias):
    rows, depth, wide = near.shape[0], latent.shape[1], turned.shape[0]
    side, core = place[0] // 2, place[0] % 2
    for c, blocks in enumerate((near, far)):
        for k in range(2):
            for quad in range(2):
                first = (quad * 2 + (side ^ k)) * 2 * rows + c * rows
                at = pl.ds(pl.multiple_of(first, rows), rows)
                block = blocks[:, (k * 2 + quad) * wide : (k * 2 + quad + 1) * wide]
                latent[at, :] = block[:, :depth]
                turned[:depth, at] = block[:, :depth].T
                turned[depth:, at] = block[:, depth:].T
    count = bias.shape[1]
    spot = lax.broadcasted_iota(jnp.int32, (rows, count), 1) ^ (core * rows)
    row = lax.broadcasted_iota(jnp.int32, (rows, 1), 0)
    for k in range(QUAD):
        spots = spot + (QUAD * (place[1] - 1) + 2 * (side ^ (k // 2))) * rows
        mine = row + (QUAD * place[1] + (place[0] ^ k)) * rows
        begin, end = jnp.zeros_like(mine), 0
        for n in range(lengths.shape[0]):
            end = end + lengths[n]
            begin = jnp.where(mine >= end, end, begin)
        allowed = (spots >= begin) & (spots <= mine)
        bias[k * rows : (k + 1) * rows, :] = jnp.where(allowed, 0.0, -1e30).astype(jnp.float32)


def prepare_keys(place, lengths, near, far, depth):
    rows, wide = near.shape[0], near.shape[1] // QUAD
    return call(
        keys_kernel,
        in_specs=[SMEM] * 2 + [IN_VMEM] * 2,
        out_specs=[IN_VMEM] * 3,
        out_shape=[
            jax.ShapeDtypeStruct((2 * QUAD * rows, depth), near.dtype),
            jax.ShapeDtypeStruct((wide, 2 * QUAD * rows), near.dtype),
            jax.ShapeDtypeStruct((QUAD * rows, (QUAD + 2) * rows), jnp.float32),
        ],
        name="keys",
    )(place, lengths, near, far)


def attend_kernel(factor, halves, chunk, rotary, place, *refs):
    sources, pieces = refs[: 2 * len(halves)], refs[2 * len(halves) : -9]
    keys, latent, bias, mixed, packs, absorb, scores, weights, sems = refs[-9:]
    rows, (heads, plain, depth), count = packs.shape[1], absorb.shape, bias.shape[1]
    both = 2 * rows

    def fetch(source, target):
        copies.append(pltpu.make_async_copy(source, target, sems.at[len(copies)]))
        copies[-1].start()
        return copies[-1]

    copies, ready, first = [], {}, 0
    for n, source in enumerate(sources):
        source = source.at[chunk] if len(source.shape) == 3 else source
        copy = fetch(source.at[:, pl.ds(0, packs.shape[2])], packs.at[n])
        ready.setdefault((n // 2, 0), []).append(copy)
    for piece in pieces:
        held = absorb.at[pl.ds(first, piece.shape[0])]
        width = depth if piece.shape[1] == plain else piece.shape[2]
        for at in range(0, depth, width):
            source = piece if width == depth else piece.at[:, pl.ds(at // width * plain, plain)]
            target = held if width == depth else held.at[:, :, pl.ds(at, width)]
            ready.setdefault((0, first), []).append(fetch(source, target))
        first += piece.shape[0]

    lane = lax.broadcasted_iota(jnp.int32, (both, 2 * rotary), 1)
    units = [(n, head) for head in range(0, heads, 2) for n in range(len(halves))]

    def window(n):
        return pl.ds(pl.multiple_of((place[0] // 2 ^ halves[n]) * both, both), count)

    def score(u):
        n, head = units[u]
        for copy in ready.get((n, head), []):
            copy.wait()
        near, far = packs.at[2 * n], packs.at[2 * n + 1]
        base = head // UNIT * UNIT * (plain + rotary)
        for h in range(2):
            at = slice(base + h * plain, base + (h + 1) * plain)
            q = jnp.concatenate([near[:, at], far[:, at]], axis=0)
            q = dot(q, absorb[head + h]).astype(jnp.bfloat16)
            at = slice(base + UNIT * plain, base + UNIT * plain + 2 * rotary)
            r = jnp.concatenate([near[:, at], far[:, at]], axis=0)
            mine = (lane < rotary) if h == 0 else (lane >= rotary)
            left = jnp.concatenate([q, jnp.where(mine, r, jnp.zeros_like(r))], axis=1)
            scores[u % 2, h * both : (h + 1) * both, :] = dot(left, keys[:, window(n)])

    def weigh(u):
        scale = []
        for first in range(0, 2 * both, STRIP):
            at = slice(first, first + STRIP)
            start = halves[units[u][0]] * both + first % both
            s = scores[u % 2, at, :] + bias[start : start + STRIP, :]
            w = jnp.exp2((s - jnp.max(s, axis=-1, keepdims=True)) * factor)
            scale.append(1.0 / jnp.sum(w, axis=-1, keepdims=True))
            weights[u % 2, at, :] = w.astype(jnp.bfloat16)
        return jnp.concatenate(scale, axis=0)

    score(0)
    for u, (n, head) in enumerate(units):
        if u + 1 < len(units):
            score(u + 1)
        scale = weigh(u)
        for h in range(2):
            at = slice(h * both, (h + 1) * both)
            summed = dot(weights[u % 2, at, :], latent[window(n), :])
            mixed[head + h, n * both : (n + 1) * both, :] = (summed * scale[at]).astype(jnp.bfloat16)


def attend(place, sources, halves, chunk, absorb, keys, latent, bias, rotary, width):
    rows = sources[0].shape[-2]
    heads = sum(piece.shape[0] for piece in absorb)
    depth, plain = latent.shape[1], width // heads - rotary
    count = bias.shape[1]
    factor = math.log2(math.e) / math.sqrt(plain + rotary)
    return call(
        functools.partial(attend_kernel, factor, halves, chunk, rotary),
        in_specs=[SMEM] + [ANY] * (len(sources) + len(absorb)) + [IN_VMEM] * 3,
        out_specs=IN_VMEM,
        out_shape=jax.ShapeDtypeStruct((heads, 2 * len(halves) * rows, depth), jnp.bfloat16),
        scratch_shapes=[
            pltpu.VMEM((len(sources), rows, width), jnp.bfloat16),
            pltpu.VMEM((heads, plain, depth), jnp.bfloat16),
            pltpu.VMEM((2, QUAD * rows, count), jnp.float32),
            pltpu.VMEM((2, QUAD * rows, count), jnp.bfloat16),
            pltpu.SemaphoreType.DMA((len(sources) + len(absorb) * depth // 128,)),
        ],
        name="attend",
        mib=24,
    )(place, *sources, *absorb, keys, latent, bias)


def value_kernel(mixed, *refs):
    pieces, (one, two, value) = refs[:-3], refs[-3:]
    take_heads(pieces, value)
    rows, width = one.shape[0], value.shape[2]
    for head in range(STEP_HEADS):
        out = dot(mixed[head], value[head]).astype(jnp.bfloat16)
        one[:, head * width : (head + 1) * width] = out[:rows]
        two[:, head * width : (head + 1) * width] = out[rows:]


def value_product(mixed, value, half, rows):
    heads, _, depth = mixed.shape
    width = value[0].shape[2]
    out = pl.BlockSpec((rows, STEP_HEADS * width), lambda i: (0, i))
    return call(
        value_kernel,
        grid=(heads // STEP_HEADS,),
        in_specs=[pl.BlockSpec((STEP_HEADS, 2 * rows, depth), lambda i: (i, half, 0))]
        + [IN_VMEM] * len(value),
        out_specs=[out] * 2,
        out_shape=[jax.ShapeDtypeStruct((rows, heads * width), jnp.bfloat16)] * 2,
        scratch_shapes=[pltpu.VMEM((STEP_HEADS, depth, width), jnp.bfloat16)],
        name="value",
    )(mixed, *value)


def join_kernel(chunks, shifted, place, *refs):
    parts, out = refs[:-1], refs[-1]
    width = out.shape[1] // (chunks * QUAD)
    block = pl.program_id(0)
    if shifted:
        block = order_of(block, place[1], pl.num_programs(0))
    source = pl.ds(pl.multiple_of(block * width, width), width)
    for c in range(chunks):
        for n, k in enumerate(JOIN_ORDER):
            at = (place[0] ^ k) * chunks + lax.rem(place[2] + c, chunks)
            out[:, pl.ds(pl.multiple_of(at * width, width), width)] = parts[c * QUAD + n][:, source]


def join(place, parts, pairs, shifted):
    chunks = len(parts)
    rows, wide = parts[0][0].shape
    return call(
        functools.partial(join_kernel, chunks, shifted),
        grid_spec=pltpu.PrefetchScalarGridSpec(
            num_scalar_prefetch=1,
            grid=(pairs,),
            in_specs=[pl.BlockSpec(memory_space=pltpu.VMEM)] * (chunks * QUAD),
            out_specs=pl.BlockSpec(
                (rows, chunks * QUAD * wide // pairs), lambda i, place: (0, i)
            ),
        ),
        out_shape=jax.ShapeDtypeStruct((rows, chunks * QUAD * wide), jnp.bfloat16),
        name="join",
    )(place, *[chunk[k] for chunk in parts for k in JOIN_ORDER])


def swap(block, k):
    return lax.ppermute(block, ("side", "core"), [(i, i ^ k) for i in range(QUAD)])


def after(later, *earlier):
    return lax.optimization_barrier((later, earlier))[0]


def across(part, distance):
    pairs = lax.axis_size("pair")
    return lax.ppermute(part, "pair", [(i, i ^ distance) for i in range(pairs)])


def from_group(part, c):
    groups = lax.axis_size("groups")
    return lax.ppermute(part, "groups", [((i + c) % groups, i) for i in range(groups)])


def on_device(
    query_plain, query_rotary, key_latent, key_rotary, absorb_weight, value_weight, lengths
):
    rows, head_count, plain = query_plain.shape
    rotary = key_rotary.shape[1]
    depth = key_latent.shape[1]
    held = absorb_weight.shape[0]
    pairs, groups = lax.axis_size("pair"), lax.axis_size("groups")
    names = ("groups", "pair", "side", "core")
    group, pair, side, core = (lax.axis_index(name) for name in names)
    here = 2 * side + core
    place = jnp.stack([here, pair, group]).astype(jnp.int32)
    by_group = held == groups * UNIT and plain == 128 and UNIT * rotary == 128
    by_group = by_group and pairs & (pairs - 1) == 0

    def far_quads(near):
        known, far, distance = near, [], 2
        while distance < pairs:
            far.append(across(known, distance))
            known = jnp.concatenate([known, far[-1]])
            distance *= 2
        return far

    if by_group:
        joined = join_keys(key_latent, key_rotary)
    else:
        joined = jnp.concatenate([key_latent, key_rotary, key_rotary], axis=1)
    before = lax.ppermute(joined, "pair", [(i - 1, i) for i in range(1, pairs)])
    if by_group:
        near, far, mine, mine_value, pair_out = prepare(
            place, query_plain, query_rotary, absorb_weight, value_weight, pairs, groups
        )
        near_pair = across(pair_out, 1)
        absorb = [mine[0]] + [across(mine[0], d) for d in range(2, pairs)] + [near_pair]
        both = jnp.concatenate([mine_value[0], near_pair[:, depth:]])
        value = [mine_value[0], *far_quads(after(both, *absorb)), near_pair]
    else:
        absorb = [lax.all_gather(absorb_weight, "pair", axis=0, tiled=True)]
        value = [lax.all_gather(value_weight, "pair", axis=0, tiled=True)]
        flat = query_plain.reshape(rows, head_count * plain)
        near, far = pack_by_slices(place, flat, query_rotary, pairs)
    chunks, width = len(far), far[0][0].shape[1]

    keys = jnp.concatenate([before, joined], axis=1)
    coming = [swap(jnp.concatenate([far[0][0], keys], axis=1), 2), swap(far[0][1], 3)]
    near = [near[0], swap(after(near[1], coming[0]), 1)]
    keys = jnp.concatenate([keys, coming[0][:, width:]], axis=1)
    latent, turned, bias = prepare_keys(place, lengths, keys, swap(keys, 1), depth)

    def work(halves, c, sources, absorb_c):
        return attend(
            place, sources, halves, c, absorb_c, turned, latent, bias, rotary, width
        )

    parts = []
    for c in range(chunks):
        arrived = coming
        if c + 1 < chunks:
            following = after(far[c + 1], *arrived)
            coming = [swap(following[k - 2], k) for k in (2, 3)]
        if c == 0:
            absorb_c, value_c = absorb, value
        else:
            crossed = from_group(near_pair, c)
            absorb_c = [mine[c], from_group(jnp.concatenate(absorb[1:-1]), c), crossed]
            value_c = [mine_value[c]] + [from_group(piece, c) for piece in value[1:-1]] + [crossed]
        out = [None] * 2
        if c + 1 < chunks:
            mixed = work((0, 1), c, [*near, *arrived], absorb_c)
            value[1:-1] = value_c[1:-1] = after(value_c[1:-1], mixed)
            mixed = after(mixed, *coming)
            for half in (1, 0):
                out[half] = value_product(mixed, value_c, half, rows)
        else:
            for half in (1, 0):
                mixed = work((half,), c, (near, arrived)[half], absorb_c)
                out[half] = value_product(mixed, value_c, 0, rows)
                near = after(near, *out[half])
        back = swap(out[0][1], 1)
        coming = after(coming, back, *out[1])
        parts.append([out[0][0], back] + [swap(out[1][k - 2], k) for k in (2, 3)])
    return join(place, parts, pairs, by_group)


def solution(mesh):
    groups, ctx = mesh.shape["groups"], mesh.shape["ctx"]
    names = ("groups", "pair", "side", "core")
    fine = Mesh(np.asarray(mesh.devices).reshape(groups, ctx // QUAD, 2, 2), names)
    return jax.shard_map(
        on_device,
        mesh=fine,
        in_specs=(
            P(names, None, None),
            P(names, None),
            P(names, None),
            P(names, None),
            P(names[1:], None, None),
            P(names[1:], None, None),
            P("groups"),
        ),
        out_specs=P(names, None),
        check_vma=False,
    )
```

```python
import functools
import math

import jax
import jax.numpy as jnp
import numpy as np
from jax import lax
from jax.experimental import pallas as pl
from jax.experimental.pallas import tpu as pltpu
from jax.sharding import Mesh, PartitionSpec as P

QUAD = 4
JOIN_ORDER = (0, 2, 3, 1)
UNIT = 2
STEP_HEADS = 4
STRIP = 32


def dot(a, b):
    return jnp.dot(a, b, preferred_element_type=jnp.float32)


def call(kernel, mib=16, moved=0, **kw):
    return pl.pallas_call(
        kernel,
        compiler_params=pltpu.CompilerParams(vmem_limit_bytes=mib * 2**20),
        cost_estimate=pl.CostEstimate(flops=0, bytes_accessed=moved, transcendentals=0),
        **kw,
    )


HBM, IN_VMEM = pl.BlockSpec(memory_space=pltpu.HBM), pl.BlockSpec(memory_space=pltpu.VMEM)
ANY, SMEM = pl.BlockSpec(memory_space=pl.ANY), pl.BlockSpec(memory_space=pltpu.SMEM)


def take_heads(pieces, held):
    where = []
    for piece in pieces:
        where += [(piece, h) for h in range(piece.shape[0])]
    for first in range(0, len(where), STEP_HEADS):

        @pl.when(pl.program_id(0) == first // STEP_HEADS)
        def _():
            for h in range(STEP_HEADS):
                piece, at = where[first + h]
                held[h] = piece[at, piece.shape[1] - held.shape[1] :, :]


def order_of(quad, here, pairs):
    distance = quad ^ here
    order = jnp.where(distance == 1, pairs - 1, distance - 1)
    return jnp.where(distance == 0, 0, order)


def prepare_kernel(groups, pairs, place, *refs):
    plain, rotary, absorb, value = refs[:4]
    packs, refs = refs[4 : 6 + 2 * groups], refs[6 + 2 * groups :]
    stacked, values, pair = refs[:groups], refs[groups : 2 * groups], refs[2 * groups]
    refs = refs[2 * groups + 1 :]
    plain_in, rotary_in, absorb_in, value_in, single, flat, sems = refs
    rows, heads, width = plain_in.shape
    depth = value_in.shape[2]
    held, carried = heads // pairs, absorb_in.shape[1]
    copies = []

    def fetch(source, target):
        copies.append(pltpu.make_async_copy(source, target, sems.at[len(copies)]))
        copies[-1].start()

    for c in range(groups):
        at = pl.ds(lax.rem(place[2] + c, groups) * carried, carried)
        fetch(absorb.at[at], absorb_in.at[c])
        fetch(value.at[at], value_in.at[c])
    for i in range(pairs):
        at = pl.ds(i * held, held)
        fetch(plain.at[:, at], plain_in.at[:, at])
    fetch(rotary, rotary_in)

    for c in range(groups):
        copies[2 * c].wait()
        copies[2 * c + 1].wait()
        for first in range(0, depth, width):
            stacked[c][:, first : first + width, :] = absorb_in[c, :, :, first : first + width]
        values[c][...] = value_in[c]
    pair[:, :depth, :] = stacked[0][...]
    pair[:, depth:, :] = value_in[0]

    wide, thin = UNIT * width, rotary_in.shape[1] // (pairs * QUAD * groups)
    copies[-1].wait()
    for i in range(pairs):
        copies[2 * groups + i].wait()
        part = plain_in[:, i * held : (i + 1) * held, :]
        single[...] = part.astype(jnp.float32).reshape(rows * held, width)
        for head in range(held):
            part = single[pl.ds(head, rows, stride=held), :]
            flat[:, head * width : (head + 1) * width] = part.astype(flat.dtype)
        first = pl.multiple_of(order_of(i, place[1], pairs) * (wide + thin), wide + thin)
        for c in range(groups):
            for k in range(QUAD):
                at = (place[0] ^ k) * groups + lax.rem(place[2] + c, groups)
                out = packs[k].at[c] if k < 2 else packs[2 + c * 2 + k - 2]
                part = flat[:, pl.ds(pl.multiple_of(at * wide, wide), wide)]
                out[:, pl.ds(first, wide)] = part
                at = at * thin + i * thin * QUAD * groups
                part = rotary_in[:, pl.ds(pl.multiple_of(at, thin), thin)]
                out[:, pl.ds(pl.multiple_of(first + wide, thin), thin)] = part


def prepare(place, plain, rotary, absorb, value, pairs, groups):
    rows, heads, wide = plain.shape
    width = (heads * wide + rotary.shape[1]) // (QUAD * groups)
    held = absorb.shape[0] // groups
    part, dtype = (held, *value.shape[1:]), plain.dtype
    shapes = [(groups, rows, width)] * 2 + [(rows, width)] * (2 * groups)
    shapes += [part] * (2 * groups) + [(held, 2 * part[1], part[2])]
    outs = call(
        functools.partial(prepare_kernel, groups, pairs),
        in_specs=[SMEM] + [HBM] * 4,
        out_specs=[IN_VMEM] * len(shapes),
        out_shape=[jax.ShapeDtypeStruct(shape, dtype) for shape in shapes],
        scratch_shapes=[
            pltpu.VMEM(plain.shape, dtype),
            pltpu.VMEM(rotary.shape, dtype),
            pltpu.VMEM((groups, held, *absorb.shape[1:]), dtype),
            pltpu.VMEM((groups, held, *value.shape[1:]), dtype),
            pltpu.VMEM((rows * heads // pairs, wide), jnp.float32),
            pltpu.VMEM((rows, heads // pairs * wide), dtype),
            pltpu.SemaphoreType.DMA((2 * groups + pairs + 1,)),
        ],
        moved=12 * 2**20,
        name="prepare",
    )(place, plain, rotary, absorb, value)
    far = outs[2 : 2 + 2 * groups]
    weights = outs[2 + 2 * groups :]
    return (
        outs[:2],
        [list(far[2 * c : 2 * c + 2]) for c in range(groups)],
        weights[:groups],
        weights[groups : 2 * groups],
        weights[-1],
    )


def pack_by_slices(place, plain, rotary, pairs):
    def sets(array):
        width = array.shape[1] // (QUAD * pairs)
        pick = lambda s: [
            array[:, (QUAD * i + s) * width : (QUAD * i + s + 1) * width] for i in range(pairs)
        ]
        whole = jnp.stack([jnp.concatenate(pick(s), axis=1) for s in range(QUAD)])
        steps = whole.shape[2] // (UNIT * (array.shape[1] // heads))
        return whole.reshape(QUAD, array.shape[0], steps, -1)

    heads = plain.shape[1] // 128
    both = jnp.concatenate([sets(plain), sets(rotary)], axis=3)
    both = both.reshape(QUAD, plain.shape[0], -1)
    packs = [lax.dynamic_index_in_dim(both, place[0] ^ k, 0, False) for k in range(QUAD)]
    return [pack[None] for pack in packs[:2]], [packs[2:]]


def joined_kernel(latent, rotary, joined, rotary_in, sems):
    depth = latent.shape[1]
    copies = [
        pltpu.make_async_copy(rotary, rotary_in, sems.at[0]),
        pltpu.make_async_copy(latent, joined.at[:, pl.ds(0, depth)], sems.at[1]),
    ]
    for copy in copies:
        copy.start()
    copies[0].wait()
    joined[:, depth:] = jnp.concatenate([rotary_in[...]] * 2, axis=0).T
    copies[1].wait()


def join_keys(latent, rotary):
    shape = (latent.shape[0], latent.shape[1] + 2 * rotary.shape[1])
    return call(
        joined_kernel,
        in_specs=[HBM, HBM],
        out_specs=IN_VMEM,
        out_shape=jax.ShapeDtypeStruct(shape, latent.dtype),
        scratch_shapes=[
            pltpu.VMEM(rotary.shape[::-1], rotary.dtype),
            pltpu.SemaphoreType.DMA((2,)),
        ],
        name="joined",
    )(latent, rotary.T)


def keys_kernel(place, lengths, near, far, latent, turned, bias):
    rows, depth, wide = near.shape[0], latent.shape[1], turned.shape[0]
    side, core = place[0] // 2, place[0] % 2
    for c, blocks in enumerate((near, far)):
        for k in range(2):
            for quad in range(2):
                first = (quad * 2 + (side ^ k)) * 2 * rows + c * rows
                at = pl.ds(pl.multiple_of(first, rows), rows)
                block = blocks[:, (k * 2 + quad) * wide : (k * 2 + quad + 1) * wide]
                latent[at, :] = block[:, :depth]
                turned[:depth, at] = block[:, :depth].T
                turned[depth:, at] = block[:, depth:].T
    count = bias.shape[1]
    spot = lax.broadcasted_iota(jnp.int32, (rows, count), 1) ^ (core * rows)
    row = lax.broadcasted_iota(jnp.int32, (rows, 1), 0)
    for k in range(QUAD):
        spots = spot + (QUAD * (place[1] - 1) + 2 * (side ^ (k // 2))) * rows
        mine = row + (QUAD * place[1] + (place[0] ^ k)) * rows
        begin, end = jnp.zeros_like(mine), 0
        for n in range(lengths.shape[0]):
            end = end + lengths[n]
            begin = jnp.where(mine >= end, end, begin)
        allowed = (spots >= begin) & (spots <= mine)
        bias[k * rows : (k + 1) * rows, :] = jnp.where(allowed, 0.0, -1e30).astype(jnp.float32)


def prepare_keys(place, lengths, near, far, depth):
    rows, wide = near.shape[0], near.shape[1] // QUAD
    return call(
        keys_kernel,
        in_specs=[SMEM] * 2 + [IN_VMEM] * 2,
        out_specs=[IN_VMEM] * 3,
        out_shape=[
            jax.ShapeDtypeStruct((2 * QUAD * rows, depth), near.dtype),
            jax.ShapeDtypeStruct((wide, 2 * QUAD * rows), near.dtype),
            jax.ShapeDtypeStruct((QUAD * rows, (QUAD + 2) * rows), jnp.float32),
        ],
        name="keys",
    )(place, lengths, near, far)


def attend_kernel(factor, halves, chunk, rotary, place, *refs):
    sources, pieces = refs[: 2 * len(halves)], refs[2 * len(halves) : -10]
    keys, latent, bias, mixed, packs, absorb, left, scores, weights, sems = refs[-10:]
    rows, (heads, plain, depth), count = packs.shape[1], absorb.shape, bias.shape[1]
    both = 2 * rows

    def fetch(source, target):
        copies.append(pltpu.make_async_copy(source, target, sems.at[len(copies)]))
        copies[-1].start()
        return copies[-1]

    copies, ready, first = [], {}, 0
    for n, source in enumerate(sources):
        source = source.at[chunk] if len(source.shape) == 3 else source
        copy = fetch(source.at[:, pl.ds(0, packs.shape[2])], packs.at[n])
        ready.setdefault((n // 2, 0), []).append(copy)
    for piece in pieces:
        held = absorb.at[pl.ds(first, piece.shape[0])]
        width = depth if piece.shape[1] == plain else piece.shape[2]
        for at in range(0, depth, width):
            source = piece if width == depth else piece.at[:, pl.ds(at // width * plain, plain)]
            target = held if width == depth else held.at[:, :, pl.ds(at, width)]
            ready.setdefault((0, first), []).append(fetch(source, target))
        first += piece.shape[0]

    lane = lax.broadcasted_iota(jnp.int32, (both, 2 * rotary), 1)
    units = [(n, head) for head in range(0, heads, 2) for n in range(len(halves))]

    def window(n):
        return pl.ds(pl.multiple_of((place[0] // 2 ^ halves[n]) * both, both), count)

    def score(u):
        n, head = units[u]
        for copy in ready.get((n, head), []):
            copy.wait()
        near, far = packs.at[2 * n], packs.at[2 * n + 1]
        base = head // UNIT * UNIT * (plain + rotary)
        for h in range(2):
            at = slice(base + h * plain, base + (h + 1) * plain)
            q = jnp.concatenate([near[:, at], far[:, at]], axis=0)
            q = dot(q, absorb[head + h]).astype(jnp.bfloat16)
            at = slice(base + UNIT * plain, base + UNIT * plain + 2 * rotary)
            r = jnp.concatenate([near[:, at], far[:, at]], axis=0)
            mine = (lane < rotary) if h == 0 else (lane >= rotary)
            rows_of = slice(h * both, (h + 1) * both)
            left[u % 2, rows_of, :depth] = q
            left[u % 2, rows_of, depth:] = jnp.where(mine, r, jnp.zeros_like(r))
        scores[u % 2] = dot(left[u % 2], keys[:, window(n)])

    def weigh(u):
        scale = []
        for first in range(0, 2 * both, STRIP):
            at = slice(first, first + STRIP)
            start = halves[units[u][0]] * both + first % both
            s = scores[u % 2, at, :] + bias[start : start + STRIP, :]
            w = jnp.exp2((s - jnp.max(s, axis=-1, keepdims=True)) * factor)
            scale.append(1.0 / jnp.sum(w, axis=-1, keepdims=True))
            weights[u % 2, at, :] = w.astype(jnp.bfloat16)
        return jnp.concatenate(scale, axis=0)

    score(0)
    for u, (n, head) in enumerate(units):
        if u + 1 < len(units):
            score(u + 1)
        scale = weigh(u)
        summed = (dot(weights[u % 2], latent[window(n), :]) * scale).astype(jnp.bfloat16)
        for h in range(2):
            mixed[head + h, n * both : (n + 1) * both, :] = summed[h * both : (h + 1) * both]


def attend(place, sources, halves, chunk, absorb, keys, latent, bias, rotary, width):
    rows = sources[0].shape[-2]
    heads = sum(piece.shape[0] for piece in absorb)
    depth, plain = latent.shape[1], width // heads - rotary
    count = bias.shape[1]
    factor = math.log2(math.e) / math.sqrt(plain + rotary)
    return call(
        functools.partial(attend_kernel, factor, halves, chunk, rotary),
        in_specs=[SMEM] + [ANY] * (len(sources) + len(absorb)) + [IN_VMEM] * 3,
        out_specs=IN_VMEM,
        out_shape=jax.ShapeDtypeStruct((heads, 2 * len(halves) * rows, depth), jnp.bfloat16),
        scratch_shapes=[
            pltpu.VMEM((len(sources), rows, width), jnp.bfloat16),
            pltpu.VMEM((heads, plain, depth), jnp.bfloat16),
            pltpu.VMEM((2, QUAD * rows, keys.shape[0]), jnp.bfloat16),
            pltpu.VMEM((2, QUAD * rows, count), jnp.float32),
            pltpu.VMEM((2, QUAD * rows, count), jnp.bfloat16),
            pltpu.SemaphoreType.DMA((len(sources) + len(absorb) * depth // 128,)),
        ],
        name="attend",
        mib=24,
    )(place, *sources, *absorb, keys, latent, bias)


def value_kernel(mixed, *refs):
    pieces, (one, two, value) = refs[:-3], refs[-3:]
    take_heads(pieces, value)
    rows, width = one.shape[0], value.shape[2]
    for head in range(STEP_HEADS):
        out = dot(mixed[head], value[head]).astype(jnp.bfloat16)
        one[:, head * width : (head + 1) * width] = out[:rows]
        two[:, head * width : (head + 1) * width] = out[rows:]


def value_product(mixed, value, half, rows):
    heads, _, depth = mixed.shape
    width = value[0].shape[2]
    out = pl.BlockSpec((rows, STEP_HEADS * width), lambda i: (0, i))
    return call(
        value_kernel,
        grid=(heads // STEP_HEADS,),
        in_specs=[pl.BlockSpec((STEP_HEADS, 2 * rows, depth), lambda i: (i, half, 0))]
        + [IN_VMEM] * len(value),
        out_specs=[out] * 2,
        out_shape=[jax.ShapeDtypeStruct((rows, heads * width), jnp.bfloat16)] * 2,
        scratch_shapes=[pltpu.VMEM((STEP_HEADS, depth, width), jnp.bfloat16)],
        name="value",
    )(mixed, *value)


def join_kernel(chunks, shifted, place, *refs):
    parts, out = refs[:-1], refs[-1]
    width = out.shape[1] // (chunks * QUAD)
    block = pl.program_id(0)
    if shifted:
        block = order_of(block, place[1], pl.num_programs(0))
    source = pl.ds(pl.multiple_of(block * width, width), width)
    for c in range(chunks):
        for n, k in enumerate(JOIN_ORDER):
            at = (place[0] ^ k) * chunks + lax.rem(place[2] + c, chunks)
            out[:, pl.ds(pl.multiple_of(at * width, width), width)] = parts[c * QUAD + n][:, source]


def join(place, parts, pairs, shifted):
    chunks = len(parts)
    rows, wide = parts[0][0].shape
    return call(
        functools.partial(join_kernel, chunks, shifted),
        grid_spec=pltpu.PrefetchScalarGridSpec(
            num_scalar_prefetch=1,
            grid=(pairs,),
            in_specs=[pl.BlockSpec(memory_space=pltpu.VMEM)] * (chunks * QUAD),
            out_specs=pl.BlockSpec(
                (rows, chunks * QUAD * wide // pairs), lambda i, place: (0, i)
            ),
        ),
        out_shape=jax.ShapeDtypeStruct((rows, chunks * QUAD * wide), jnp.bfloat16),
        name="join",
    )(place, *[chunk[k] for chunk in parts for k in JOIN_ORDER])


def swap(block, k):
    return lax.ppermute(block, ("side", "core"), [(i, i ^ k) for i in range(QUAD)])


def after(later, *earlier):
    return lax.optimization_barrier((later, earlier))[0]


def across(part, distance):
    pairs = lax.axis_size("pair")
    return lax.ppermute(part, "pair", [(i, i ^ distance) for i in range(pairs)])


def from_group(part, c):
    groups = lax.axis_size("groups")
    return lax.ppermute(part, "groups", [((i + c) % groups, i) for i in range(groups)])


def on_device(
    query_plain, query_rotary, key_latent, key_rotary, absorb_weight, value_weight, lengths
):
    rows, head_count, plain = query_plain.shape
    rotary = key_rotary.shape[1]
    depth = key_latent.shape[1]
    held = absorb_weight.shape[0]
    pairs, groups = lax.axis_size("pair"), lax.axis_size("groups")
    names = ("groups", "pair", "side", "core")
    group, pair, side, core = (lax.axis_index(name) for name in names)
    here = 2 * side + core
    place = jnp.stack([here, pair, group]).astype(jnp.int32)
    by_group = held == groups * UNIT and plain == 128 and UNIT * rotary == 128
    by_group = by_group and pairs & (pairs - 1) == 0

    def far_quads(near):
        known, far, distance = near, [], 2
        while distance < pairs:
            far.append(across(known, distance))
            known = jnp.concatenate([known, far[-1]])
            distance *= 2
        return far

    if by_group:
        joined = join_keys(key_latent, key_rotary)
    else:
        joined = jnp.concatenate([key_latent, key_rotary, key_rotary], axis=1)
    before = lax.ppermute(joined, "pair", [(i - 1, i) for i in range(1, pairs)])
    if by_group:
        near, far, mine, mine_value, pair_out = prepare(
            place, query_plain, query_rotary, absorb_weight, value_weight, pairs, groups
        )
        near_pair = across(pair_out, 1)
        absorb = [mine[0]] + [across(mine[0], d) for d in range(2, pairs)] + [near_pair]
        both = jnp.concatenate([mine_value[0], near_pair[:, depth:]])
    else:
        absorb = [lax.all_gather(absorb_weight, "pair", axis=0, tiled=True)]
        value = [lax.all_gather(value_weight, "pair", axis=0, tiled=True)]
        flat = query_plain.reshape(rows, head_count * plain)
        near, far = pack_by_slices(place, flat, query_rotary, pairs)
    chunks, width = len(far), far[0][0].shape[1]

    keys = jnp.concatenate([before, joined], axis=1)
    coming = [swap(jnp.concatenate([far[0][0], keys], axis=1), 2), swap(far[0][1], 3)]
    near = [near[0], swap(near[1], 1)]
    keys = jnp.concatenate([after(keys, near[1]), coming[0][:, width:]], axis=1)
    latent, turned, bias = prepare_keys(place, lengths, keys, swap(keys, 1), depth)
    if by_group:
        crossed = [None] + [from_group(near_pair, c) for c in range(1, groups)]
        value = far_quads(after(both, *absorb))
        value = [mine_value[0], *value, near_pair]

    def work(halves, c, sources, absorb_c):
        return attend(
            place, sources, halves, c, absorb_c, turned, latent, bias, rotary, width
        )

    parts = []
    for c in range(chunks):
        arrived = coming
        if c + 1 < chunks:
            following = after(far[c + 1], *arrived)
            coming = [swap(following[k - 2], k) for k in (2, 3)]
        if c == 0:
            absorb_c, value_c = absorb, value
        else:
            absorb_c = [mine[c], from_group(after(jnp.concatenate(absorb[1:-1]), crossed[c]), c), crossed[c]]
            value_c = [mine_value[c]] + [from_group(piece, c) for piece in value[1:-1]]
            value_c.append(crossed[c])
        out = [None] * 2
        if c + 1 < chunks:
            mixed = work((0, 1), c, [*near, *arrived], absorb_c)
            value[1:-1] = value_c[1:-1] = after(value_c[1:-1], mixed)
            mixed = after(mixed, *coming)
            for half in (1, 0):
                out[half] = value_product(mixed, value_c, half, rows)
        else:
            for half in (1, 0):
                mixed = work((half,), c, (near, arrived)[half], absorb_c)
                out[half] = value_product(mixed, value_c, 0, rows)
                near = after(near, *out[half])
        back = swap(out[0][1], 1)
        coming = after(coming, back, *out[1])
        parts.append([out[0][0], back] + [swap(out[1][k - 2], k) for k in (2, 3)])
    return join(place, parts, pairs, by_group)


def solution(mesh):
    groups, ctx = mesh.shape["groups"], mesh.shape["ctx"]
    names = ("groups", "pair", "side", "core")
    fine = Mesh(np.asarray(mesh.devices).reshape(groups, ctx // QUAD, 2, 2), names)
    return jax.shard_map(
        on_device,
        mesh=fine,
        in_specs=(
            P(names, None, None),
            P(names, None),
            P(names, None),
            P(names, None),
            P(names[1:], None, None),
            P(names[1:], None, None),
            P("groups"),
        ),
        out_specs=P(names, None),
        check_vma=False,
    )
```

```python
import functools
import math

import jax
import jax.numpy as jnp
import numpy as np
from jax import lax
from jax.experimental import pallas as pl
from jax.experimental.pallas import tpu as pltpu
from jax.sharding import Mesh, PartitionSpec as P

QUAD = 4
JOIN_ORDER = (0, 2, 3, 1)
UNIT = 2
STEP_HEADS = 4
BLOCK = 256
STRIP = 32


def dot(a, b):
    return jnp.dot(a, b, preferred_element_type=jnp.float32)


def call(kernel, mib=16, moved=0, **kw):
    return pl.pallas_call(
        kernel,
        compiler_params=pltpu.CompilerParams(vmem_limit_bytes=mib * 2**20),
        cost_estimate=pl.CostEstimate(flops=0, bytes_accessed=moved, transcendentals=0),
        **kw,
    )


HBM, IN_VMEM = pl.BlockSpec(memory_space=pltpu.HBM), pl.BlockSpec(memory_space=pltpu.VMEM)
ANY, SMEM = pl.BlockSpec(memory_space=pl.ANY), pl.BlockSpec(memory_space=pltpu.SMEM)


def take_heads(pieces, held):
    where = []
    for piece in pieces:
        where += [(piece, h) for h in range(piece.shape[0])]
    for first in range(0, len(where), STEP_HEADS):

        @pl.when(pl.program_id(0) == first // STEP_HEADS)
        def _():
            for h in range(STEP_HEADS):
                piece, at = where[first + h]
                held[h] = piece[at, piece.shape[1] - held.shape[1] :, :]


def order_of(quad, here, pairs):
    distance = quad ^ here
    order = jnp.where(distance == 1, pairs - 1, distance - 1)
    return jnp.where(distance == 0, 0, order)


def prepare_kernel(groups, pairs, place, *refs):
    plain, rotary, absorb, value = refs[:4]
    packs, refs = refs[4 : 6 + 2 * groups], refs[6 + 2 * groups :]
    stacked, values, pair = refs[:groups], refs[groups : 2 * groups], refs[2 * groups]
    refs = refs[2 * groups + 1 :]
    plain_in, rotary_in, absorb_in, value_in, single, flat, sems = refs
    rows, heads, width = plain_in.shape
    depth = value_in.shape[2]
    held, carried = heads // pairs, absorb_in.shape[1]
    copies = []

    def fetch(source, target):
        copies.append(pltpu.make_async_copy(source, target, sems.at[len(copies)]))
        copies[-1].start()

    for c in range(groups):
        at = pl.ds(lax.rem(place[2] + c, groups) * carried, carried)
        fetch(absorb.at[at], absorb_in.at[c])
        fetch(value.at[at], value_in.at[c])
    for i in range(pairs):
        at = pl.ds(i * held, held)
        fetch(plain.at[:, at], plain_in.at[:, at])
    fetch(rotary, rotary_in)

    for c in range(groups):
        copies[2 * c].wait()
        copies[2 * c + 1].wait()
        for first in range(0, depth, width):
            stacked[c][:, first : first + width, :] = absorb_in[c, :, :, first : first + width]
        values[c][...] = value_in[c]
    pair[:, :depth, :] = stacked[0][...]
    pair[:, depth:, :] = value_in[0]

    wide, thin = UNIT * width, rotary_in.shape[1] // (pairs * QUAD * groups)
    copies[-1].wait()
    for i in range(pairs):
        copies[2 * groups + i].wait()
        part = plain_in[:, i * held : (i + 1) * held, :]
        single[...] = part.astype(jnp.float32).reshape(rows * held, width)
        for head in range(held):
            part = single[pl.ds(head, rows, stride=held), :]
            flat[:, head * width : (head + 1) * width] = part.astype(flat.dtype)
        first = pl.multiple_of(order_of(i, place[1], pairs) * (wide + thin), wide + thin)
        for c in range(groups):
            for k in range(QUAD):
                at = (place[0] ^ k) * groups + lax.rem(place[2] + c, groups)
                out = packs[k].at[c] if k < 2 else packs[2 + c * 2 + k - 2]
                part = flat[:, pl.ds(pl.multiple_of(at * wide, wide), wide)]
                out[:, pl.ds(first, wide)] = part
                at = at * thin + i * thin * QUAD * groups
                part = rotary_in[:, pl.ds(pl.multiple_of(at, thin), thin)]
                out[:, pl.ds(pl.multiple_of(first + wide, thin), thin)] = part


def prepare(place, plain, rotary, absorb, value, pairs, groups):
    rows, heads, wide = plain.shape
    width = (heads * wide + rotary.shape[1]) // (QUAD * groups)
    held = absorb.shape[0] // groups
    part, dtype = (held, *value.shape[1:]), plain.dtype
    shapes = [(groups, rows, width)] * 2 + [(rows, width)] * (2 * groups)
    shapes += [part] * (2 * groups) + [(held, 2 * part[1], part[2])]
    outs = call(
        functools.partial(prepare_kernel, groups, pairs),
        in_specs=[SMEM] + [HBM] * 4,
        out_specs=[IN_VMEM] * len(shapes),
        out_shape=[jax.ShapeDtypeStruct(shape, dtype) for shape in shapes],
        scratch_shapes=[
            pltpu.VMEM(plain.shape, dtype),
            pltpu.VMEM(rotary.shape, dtype),
            pltpu.VMEM((groups, held, *absorb.shape[1:]), dtype),
            pltpu.VMEM((groups, held, *value.shape[1:]), dtype),
            pltpu.VMEM((rows * heads // pairs, wide), jnp.float32),
            pltpu.VMEM((rows, heads // pairs * wide), dtype),
            pltpu.SemaphoreType.DMA((2 * groups + pairs + 1,)),
        ],
        moved=12 * 2**20,
        name="prepare",
    )(place, plain, rotary, absorb, value)
    far = outs[2 : 2 + 2 * groups]
    weights = outs[2 + 2 * groups :]
    return (
        outs[:2],
        [list(far[2 * c : 2 * c + 2]) for c in range(groups)],
        weights[:groups],
        weights[groups : 2 * groups],
        weights[-1],
    )


def pack_by_slices(place, plain, rotary, pairs):
    def sets(array):
        width = array.shape[1] // (QUAD * pairs)
        pick = lambda s: [
            array[:, (QUAD * i + s) * width : (QUAD * i + s + 1) * width] for i in range(pairs)
        ]
        whole = jnp.stack([jnp.concatenate(pick(s), axis=1) for s in range(QUAD)])
        steps = whole.shape[2] // (UNIT * (array.shape[1] // heads))
        return whole.reshape(QUAD, array.shape[0], steps, -1)

    heads = plain.shape[1] // 128
    both = jnp.concatenate([sets(plain), sets(rotary)], axis=3)
    both = both.reshape(QUAD, plain.shape[0], -1)
    packs = [lax.dynamic_index_in_dim(both, place[0] ^ k, 0, False) for k in range(QUAD)]
    return [pack[None] for pack in packs[:2]], [packs[2:]]


def joined_kernel(latent, rotary, joined, rotary_in, sems):
    depth = latent.shape[1]
    copies = [
        pltpu.make_async_copy(rotary, rotary_in, sems.at[0]),
        pltpu.make_async_copy(latent, joined.at[:, pl.ds(0, depth)], sems.at[1]),
    ]
    for copy in copies:
        copy.start()
    copies[0].wait()
    joined[:, depth:] = jnp.concatenate([rotary_in[...]] * 2, axis=0).T
    copies[1].wait()


def join_keys(latent, rotary):
    shape = (latent.shape[0], latent.shape[1] + 2 * rotary.shape[1])
    return call(
        joined_kernel,
        in_specs=[HBM, HBM],
        out_specs=IN_VMEM,
        out_shape=jax.ShapeDtypeStruct(shape, latent.dtype),
        scratch_shapes=[
            pltpu.VMEM(rotary.shape[::-1], rotary.dtype),
            pltpu.SemaphoreType.DMA((2,)),
        ],
        name="joined",
    )(latent, rotary.T)


def keys_kernel(place, lengths, near, far, latent, turned, bias):
    rows, depth, wide = near.shape[0], latent.shape[1], turned.shape[0]
    side, core = place[0] // 2, place[0] % 2
    for c, blocks in enumerate((near, far)):
        for k in range(2):
            for quad in range(2):
                first = (quad * 2 + (side ^ k)) * 2 * rows + c * rows
                at = pl.ds(pl.multiple_of(first, rows), rows)
                block = blocks[:, (k * 2 + quad) * wide : (k * 2 + quad + 1) * wide]
                latent[at, :] = block[:, :depth]
                turned[:depth, at] = block[:, :depth].T
                turned[depth:, at] = block[:, depth:].T
    count = bias.shape[1]
    spot = lax.broadcasted_iota(jnp.int32, (rows, count), 1) ^ (core * rows)
    row = lax.broadcasted_iota(jnp.int32, (rows, 1), 0)
    for k in range(QUAD):
        spots = spot + (QUAD * (place[1] - 1) + 2 * (side ^ (k // 2))) * rows
        mine = row + (QUAD * place[1] + (place[0] ^ k)) * rows
        begin, end = jnp.zeros_like(mine), 0
        for n in range(lengths.shape[0]):
            end = end + lengths[n]
            begin = jnp.where(mine >= end, end, begin)
        allowed = (spots >= begin) & (spots <= mine)
        bias[k * rows : (k + 1) * rows, :] = jnp.where(allowed, 0.0, -1e30).astype(jnp.float32)


def prepare_keys(place, lengths, near, far, depth):
    rows, wide = near.shape[0], near.shape[1] // QUAD
    return call(
        keys_kernel,
        in_specs=[SMEM] * 2 + [IN_VMEM] * 2,
        out_specs=[IN_VMEM] * 3,
        out_shape=[
            jax.ShapeDtypeStruct((2 * QUAD * rows, depth), near.dtype),
            jax.ShapeDtypeStruct((wide, 2 * QUAD * rows), near.dtype),
            jax.ShapeDtypeStruct((QUAD * rows, (QUAD + 2) * rows), jnp.float32),
        ],
        name="keys",
    )(place, lengths, near, far)


def attend_kernel(factor, halves, chunk, rotary, place, *refs):
    sources, pieces = refs[: 2 * len(halves)], refs[2 * len(halves) : -11]
    keys, latent, bias, mixed, packs, absorb, left, scores, weights, scale, sems = refs[-11:]
    rows, (heads, plain, depth), count = packs.shape[1], absorb.shape, bias.shape[1]
    both = 2 * rows

    def fetch(source, target):
        copies.append(pltpu.make_async_copy(source, target, sems.at[len(copies)]))
        copies[-1].start()
        return copies[-1]

    copies, ready, first = [], {}, 0
    for n, source in enumerate(sources):
        source = source.at[chunk] if len(source.shape) == 3 else source
        copy = fetch(source.at[:, pl.ds(0, packs.shape[2])], packs.at[n])
        ready.setdefault((n // 2, 0), []).append(copy)
    for piece in pieces:
        held = absorb.at[pl.ds(first, piece.shape[0])]
        width = depth if piece.shape[1] == plain else piece.shape[2]
        for at in range(0, depth, width):
            source = piece if width == depth else piece.at[:, pl.ds(at // width * plain, plain)]
            target = held if width == depth else held.at[:, :, pl.ds(at, width)]
            ready.setdefault((0, first), []).append(fetch(source, target))
        first += piece.shape[0]

    lane = lax.broadcasted_iota(jnp.int32, (both, 2 * rotary), 1)
    units = [(n, head) for head in range(0, heads, 2) for n in range(len(halves))]

    def window_of(n):
        return (place[0] // 2 ^ halves[n]) * both

    def project(u):
        n, head = units[u]
        for copy in ready.get((n, head), []):
            copy.wait()
        near, far = packs.at[2 * n], packs.at[2 * n + 1]
        base = head // UNIT * UNIT * (plain + rotary)
        for h in range(2):
            at = slice(base + h * plain, base + (h + 1) * plain)
            q = jnp.concatenate([near[:, at], far[:, at]], axis=0)
            q = dot(q, absorb[head + h]).astype(jnp.bfloat16)
            at = slice(base + UNIT * plain, base + UNIT * plain + 2 * rotary)
            r = jnp.concatenate([near[:, at], far[:, at]], axis=0)
            mine = (lane < rotary) if h == 0 else (lane >= rotary)
            rows_of = slice(h * both, (h + 1) * both)
            left[u % 2, rows_of, :depth] = q
            left[u % 2, rows_of, depth:] = jnp.where(mine, r, jnp.zeros_like(r))

    def score(u, first):
        at = pl.ds(pl.multiple_of(window_of(units[u][0]) + first, BLOCK), BLOCK)
        scores[u % 2, :, first : first + BLOCK] = dot(left[u % 2], keys[:, at])

    def weigh(u, first):
        at = slice(first, first + STRIP)
        start = halves[units[u][0]] * both + first % both
        s = scores[u % 2, at, :] + bias[start : start + STRIP, :]
        w = jnp.exp2((s - jnp.max(s, axis=-1, keepdims=True)) * factor)
        scale[u % 2, at, :] = 1.0 / jnp.sum(w, axis=-1, keepdims=True)
        weights[u % 2, at, :] = w.astype(jnp.bfloat16)

    def mix(u, first):
        n, head = units[u]
        at = pl.ds(pl.multiple_of(window_of(n), BLOCK), count)
        summed = dot(weights[u % 2], latent[at, first : first + BLOCK])
        summed = (summed * scale[u % 2]).astype(jnp.bfloat16)
        for h in range(2):
            mixed[head + h, n * both : (n + 1) * both, first : first + BLOCK] = summed[
                h * both : (h + 1) * both
            ]

    last = len(units) - 1
    project(0)
    for first in range(0, count, BLOCK):
        score(0, first)
    project(min(1, last))
    for u in range(len(units)):
        beside = []
        if u < last:
            beside += [functools.partial(score, u + 1, first) for first in range(0, count, BLOCK)]
        if u > 0:
            mixes = [functools.partial(mix, u - 1, first) for first in range(0, depth, BLOCK)]
            beside[1:1] = mixes[:1]
            beside[3:3] = mixes[1:]
        if u + 1 < last:
            beside.append(functools.partial(project, u + 2))
        strips = list(range(0, 2 * both, STRIP))
        for n, first in enumerate(strips):
            for work in beside[n * len(beside) // len(strips) : (n + 1) * len(beside) // len(strips)]:
                work()
            weigh(u, first)
    for first in range(0, depth, BLOCK):
        mix(last, first)


def attend(place, sources, halves, chunk, absorb, keys, latent, bias, rotary, width):
    rows = sources[0].shape[-2]
    heads = sum(piece.shape[0] for piece in absorb)
    depth, plain = latent.shape[1], width // heads - rotary
    count = bias.shape[1]
    factor = math.log2(math.e) / math.sqrt(plain + rotary)
    return call(
        functools.partial(attend_kernel, factor, halves, chunk, rotary),
        in_specs=[SMEM] + [ANY] * (len(sources) + len(absorb)) + [IN_VMEM] * 3,
        out_specs=IN_VMEM,
        out_shape=jax.ShapeDtypeStruct((heads, 2 * len(halves) * rows, depth), jnp.bfloat16),
        scratch_shapes=[
            pltpu.VMEM((len(sources), rows, width), jnp.bfloat16),
            pltpu.VMEM((heads, plain, depth), jnp.bfloat16),
            pltpu.VMEM((2, QUAD * rows, keys.shape[0]), jnp.bfloat16),
            pltpu.VMEM((2, QUAD * rows, count), jnp.float32),
            pltpu.VMEM((2, QUAD * rows, count), jnp.bfloat16),
            pltpu.VMEM((2, QUAD * rows, 1), jnp.float32),
            pltpu.SemaphoreType.DMA((len(sources) + len(absorb) * depth // 128,)),
        ],
        name="attend",
        mib=24,
    )(place, *sources, *absorb, keys, latent, bias)


def value_kernel(mixed, *refs):
    pieces, (one, two, value) = refs[:-3], refs[-3:]
    take_heads(pieces, value)
    rows, width = one.shape[0], value.shape[2]
    for head in range(STEP_HEADS):
        out = dot(mixed[head], value[head]).astype(jnp.bfloat16)
        one[:, head * width : (head + 1) * width] = out[:rows]
        two[:, head * width : (head + 1) * width] = out[rows:]


def value_product(mixed, value, half, rows):
    heads, _, depth = mixed.shape
    width = value[0].shape[2]
    out = pl.BlockSpec((rows, STEP_HEADS * width), lambda i: (0, i))
    return call(
        value_kernel,
        grid=(heads // STEP_HEADS,),
        in_specs=[pl.BlockSpec((STEP_HEADS, 2 * rows, depth), lambda i: (i, half, 0))]
        + [IN_VMEM] * len(value),
        out_specs=[out] * 2,
        out_shape=[jax.ShapeDtypeStruct((rows, heads * width), jnp.bfloat16)] * 2,
        scratch_shapes=[pltpu.VMEM((STEP_HEADS, depth, width), jnp.bfloat16)],
        name="value",
    )(mixed, *value)


def join_kernel(chunks, shifted, place, *refs):
    parts, out = refs[:-1], refs[-1]
    width = out.shape[1] // (chunks * QUAD)
    block = pl.program_id(0)
    if shifted:
        block = order_of(block, place[1], pl.num_programs(0))
    source = pl.ds(pl.multiple_of(block * width, width), width)
    for c in range(chunks):
        for n, k in enumerate(JOIN_ORDER):
            at = (place[0] ^ k) * chunks + lax.rem(place[2] + c, chunks)
            out[:, pl.ds(pl.multiple_of(at * width, width), width)] = parts[c * QUAD + n][:, source]


def join(place, parts, pairs, shifted):
    chunks = len(parts)
    rows, wide = parts[0][0].shape
    return call(
        functools.partial(join_kernel, chunks, shifted),
        grid_spec=pltpu.PrefetchScalarGridSpec(
            num_scalar_prefetch=1,
            grid=(pairs,),
            in_specs=[pl.BlockSpec(memory_space=pltpu.VMEM)] * (chunks * QUAD),
            out_specs=pl.BlockSpec(
                (rows, chunks * QUAD * wide // pairs), lambda i, place: (0, i)
            ),
        ),
        out_shape=jax.ShapeDtypeStruct((rows, chunks * QUAD * wide), jnp.bfloat16),
        name="join",
    )(place, *[chunk[k] for chunk in parts for k in JOIN_ORDER])


def swap(block, k):
    return lax.ppermute(block, ("side", "core"), [(i, i ^ k) for i in range(QUAD)])


def after(later, *earlier):
    return lax.optimization_barrier((later, earlier))[0]


def across(part, distance):
    pairs = lax.axis_size("pair")
    return lax.ppermute(part, "pair", [(i, i ^ distance) for i in range(pairs)])


def from_group(part, c):
    groups = lax.axis_size("groups")
    return lax.ppermute(part, "groups", [((i + c) % groups, i) for i in range(groups)])


def on_device(
    query_plain, query_rotary, key_latent, key_rotary, absorb_weight, value_weight, lengths
):
    rows, head_count, plain = query_plain.shape
    rotary = key_rotary.shape[1]
    depth = key_latent.shape[1]
    held = absorb_weight.shape[0]
    pairs, groups = lax.axis_size("pair"), lax.axis_size("groups")
    names = ("groups", "pair", "side", "core")
    group, pair, side, core = (lax.axis_index(name) for name in names)
    here = 2 * side + core
    place = jnp.stack([here, pair, group]).astype(jnp.int32)
    by_group = held == groups * UNIT and plain == 128 and UNIT * rotary == 128
    by_group = by_group and pairs & (pairs - 1) == 0

    def far_quads(near):
        known, far, distance = near, [], 2
        while distance < pairs:
            far.append(across(known, distance))
            known = jnp.concatenate([known, far[-1]])
            distance *= 2
        return far

    if by_group:
        joined = join_keys(key_latent, key_rotary)
    else:
        joined = jnp.concatenate([key_latent, key_rotary, key_rotary], axis=1)
    before = lax.ppermute(joined, "pair", [(i - 1, i) for i in range(1, pairs)])
    if by_group:
        near, far, mine, mine_value, pair_out = prepare(
            place, query_plain, query_rotary, absorb_weight, value_weight, pairs, groups
        )
        near_pair = across(pair_out, 1)
        absorb = [mine[0]] + [across(mine[0], d) for d in range(2, pairs)] + [near_pair]
        both = jnp.concatenate([mine_value[0], near_pair[:, depth:]])
    else:
        absorb = [lax.all_gather(absorb_weight, "pair", axis=0, tiled=True)]
        value = [lax.all_gather(value_weight, "pair", axis=0, tiled=True)]
        flat = query_plain.reshape(rows, head_count * plain)
        near, far = pack_by_slices(place, flat, query_rotary, pairs)
    chunks, width = len(far), far[0][0].shape[1]

    keys = jnp.concatenate([before, joined], axis=1)
    coming = [swap(jnp.concatenate([far[0][0], keys], axis=1), 2), swap(far[0][1], 3)]
    near = [near[0], swap(near[1], 1)]
    keys = jnp.concatenate([keys, coming[0][:, width:]], axis=1)
    if by_group:
        near_pair = after(near_pair, near[1])
    latent, turned, bias = prepare_keys(place, lengths, keys, swap(keys, 1), depth)
    if by_group:
        crossed = [None] + [from_group(near_pair, c) for c in range(1, groups)]
        value = far_quads(after(both, *absorb))
        value = [mine_value[0], *value, near_pair]

    def work(halves, c, sources, absorb_c):
        return attend(
            place, sources, halves, c, absorb_c, turned, latent, bias, rotary, width
        )

    parts = []
    for c in range(chunks):
        arrived = coming
        if c + 1 < chunks:
            following = after(far[c + 1], *arrived)
            coming = [swap(following[k - 2], k) for k in (2, 3)]
        if c == 0:
            absorb_c, value_c = absorb, value
        else:
            absorb_c = [mine[c], from_group(after(jnp.concatenate(absorb[1:-1]), crossed[c]), c), crossed[c]]
            value_c = [mine_value[c]] + [from_group(piece, c) for piece in value[1:-1]]
            value_c.append(crossed[c])
        out = [None] * 2
        if c + 1 < chunks:
            mixed = work((0, 1), c, [*near, *arrived], absorb_c)
            value[1:-1] = value_c[1:-1] = after(value_c[1:-1], mixed)
            mixed = after(mixed, *coming)
            for half in (1, 0):
                out[half] = value_product(mixed, value_c, half, rows)
        else:
            for half in (1, 0):
                mixed = work((half,), c, (near, arrived)[half], absorb_c)
                out[half] = value_product(mixed, value_c, 0, rows)
                near = after(near, *out[half])
        back = swap(out[0][1], 1)
        coming = after(coming, back, *out[1])
        parts.append([out[0][0], back] + [swap(out[1][k - 2], k) for k in (2, 3)])
    return join(place, parts, pairs, by_group)


def solution(mesh):
    groups, ctx = mesh.shape["groups"], mesh.shape["ctx"]
    names = ("groups", "pair", "side", "core")
    fine = Mesh(np.asarray(mesh.devices).reshape(groups, ctx // QUAD, 2, 2), names)
    return jax.shard_map(
        on_device,
        mesh=fine,
        in_specs=(
            P(names, None, None),
            P(names, None),
            P(names, None),
            P(names, None),
            P(names[1:], None, None),
            P(names[1:], None, None),
            P("groups"),
        ),
        out_specs=P(names, None),
        check_vma=False,
    )
```

```python
import functools
import math

import jax
import jax.numpy as jnp
import numpy as np
from jax import lax
from jax.experimental import pallas as pl
from jax.experimental.pallas import tpu as pltpu
from jax.sharding import Mesh, PartitionSpec as P

QUAD = 4
JOIN_ORDER = (0, 2, 3, 1)
UNIT = 2
STEP_HEADS = 4
BLOCK = 256
STRIP = 32


def dot(a, b):
    return jnp.dot(a, b, preferred_element_type=jnp.float32)


def call(kernel, mib=16, moved=0, **kw):
    return pl.pallas_call(
        kernel,
        compiler_params=pltpu.CompilerParams(vmem_limit_bytes=mib * 2**20),
        cost_estimate=pl.CostEstimate(flops=0, bytes_accessed=moved, transcendentals=0),
        **kw,
    )


HBM, IN_VMEM = pl.BlockSpec(memory_space=pltpu.HBM), pl.BlockSpec(memory_space=pltpu.VMEM)
ANY, SMEM = pl.BlockSpec(memory_space=pl.ANY), pl.BlockSpec(memory_space=pltpu.SMEM)


def take_heads(pieces, held):
    where = []
    for piece in pieces:
        where += [(piece, h) for h in range(piece.shape[0])]
    for first in range(0, len(where), STEP_HEADS):

        @pl.when(pl.program_id(0) == first // STEP_HEADS)
        def _():
            for h in range(STEP_HEADS):
                piece, at = where[first + h]
                held[h] = piece[at, piece.shape[1] - held.shape[1] :, :]


def order_of(quad, here, pairs):
    distance = quad ^ here
    order = jnp.where(distance == 1, pairs - 1, distance - 1)
    return jnp.where(distance == 0, 0, order)


def prepare_kernel(groups, pairs, place, *refs):
    plain, rotary, absorb, value, latent, key_rotary, joined = refs[:7]
    packs, refs = refs[7 : 9 + 2 * groups], refs[9 + 2 * groups :]
    stacked, values, pair = refs[:groups], refs[groups : 2 * groups], refs[2 * groups]
    refs = refs[2 * groups + 1 :]
    plain_in, rotary_in, absorb_in, value_in, key_in, single, flat, sems = refs
    rows, heads, width = plain_in.shape
    depth = value_in.shape[2]
    held, carried = heads // pairs, absorb_in.shape[1]
    copies = []

    def fetch(source, target):
        copies.append(pltpu.make_async_copy(source, target, sems.at[len(copies)]))
        copies[-1].start()

    fetch(key_rotary, key_in)
    fetch(latent, joined.at[:, pl.ds(0, depth)])
    for c in range(groups):
        at = pl.ds(lax.rem(place[2] + c, groups) * carried, carried)
        fetch(absorb.at[at], absorb_in.at[c])
        fetch(value.at[at], value_in.at[c])
    for i in range(pairs):
        at = pl.ds(i * held, held)
        fetch(plain.at[:, at], plain_in.at[:, at])
    fetch(rotary, rotary_in)

    copies[0].wait()
    joined[:, depth:] = jnp.concatenate([key_in[...]] * 2, axis=0).T
    copies[1].wait()

    for c in range(groups):
        copies[2 * c + 2].wait()
        copies[2 * c + 3].wait()
        for first in range(0, depth, width):
            stacked[c][:, first : first + width, :] = absorb_in[c, :, :, first : first + width]
        values[c][...] = value_in[c]
    pair[:, :depth, :] = stacked[0][...]
    pair[:, depth:, :] = value_in[0]

    wide, thin = UNIT * width, rotary_in.shape[1] // (pairs * QUAD * groups)
    copies[-1].wait()
    for i in range(pairs):
        copies[2 * groups + 2 + i].wait()
        part = plain_in[:, i * held : (i + 1) * held, :]
        single[...] = part.astype(jnp.float32).reshape(rows * held, width)
        for head in range(held):
            part = single[pl.ds(head, rows, stride=held), :]
            flat[:, head * width : (head + 1) * width] = part.astype(flat.dtype)
        first = pl.multiple_of(order_of(i, place[1], pairs) * (wide + thin), wide + thin)
        for c in range(groups):
            for k in range(QUAD):
                at = (place[0] ^ k) * groups + lax.rem(place[2] + c, groups)
                out = packs[k].at[c] if k < 2 else packs[2 + c * 2 + k - 2]
                part = flat[:, pl.ds(pl.multiple_of(at * wide, wide), wide)]
                out[:, pl.ds(first, wide)] = part
                at = at * thin + i * thin * QUAD * groups
                part = rotary_in[:, pl.ds(pl.multiple_of(at, thin), thin)]
                out[:, pl.ds(pl.multiple_of(first + wide, thin), thin)] = part


def prepare(place, plain, rotary, absorb, value, latent, key_rotary, pairs, groups):
    rows, heads, wide = plain.shape
    width = (heads * wide + rotary.shape[1]) // (QUAD * groups)
    held = absorb.shape[0] // groups
    part, dtype = (held, *value.shape[1:]), plain.dtype
    shapes = [(rows, latent.shape[1] + 2 * key_rotary.shape[1])]
    shapes += [(groups, rows, width)] * 2 + [(rows, width)] * (2 * groups)
    shapes += [part] * (2 * groups) + [(held, 2 * part[1], part[2])]
    outs = call(
        functools.partial(prepare_kernel, groups, pairs),
        in_specs=[SMEM] + [HBM] * 6,
        out_specs=[IN_VMEM] * len(shapes),
        out_shape=[jax.ShapeDtypeStruct(shape, dtype) for shape in shapes],
        scratch_shapes=[
            pltpu.VMEM(plain.shape, dtype),
            pltpu.VMEM(rotary.shape, dtype),
            pltpu.VMEM((groups, held, *absorb.shape[1:]), dtype),
            pltpu.VMEM((groups, held, *value.shape[1:]), dtype),
            pltpu.VMEM(key_rotary.shape[::-1], dtype),
            pltpu.VMEM((rows * heads // pairs, wide), jnp.float32),
            pltpu.VMEM((rows, heads // pairs * wide), dtype),
            pltpu.SemaphoreType.DMA((2 * groups + pairs + 3,)),
        ],
        moved=12 * 2**20,
        name="prepare",
    )(place, plain, rotary, absorb, value, latent, key_rotary.T)
    far = outs[3 : 3 + 2 * groups]
    weights = outs[3 + 2 * groups :]
    return (
        outs[0],
        outs[1:3],
        [list(far[2 * c : 2 * c + 2]) for c in range(groups)],
        weights[:groups],
        weights[groups : 2 * groups],
        weights[-1],
    )


def pack_by_slices(place, plain, rotary, pairs):
    def sets(array):
        width = array.shape[1] // (QUAD * pairs)
        pick = lambda s: [
            array[:, (QUAD * i + s) * width : (QUAD * i + s + 1) * width] for i in range(pairs)
        ]
        whole = jnp.stack([jnp.concatenate(pick(s), axis=1) for s in range(QUAD)])
        steps = whole.shape[2] // (UNIT * (array.shape[1] // heads))
        return whole.reshape(QUAD, array.shape[0], steps, -1)

    heads = plain.shape[1] // 128
    both = jnp.concatenate([sets(plain), sets(rotary)], axis=3)
    both = both.reshape(QUAD, plain.shape[0], -1)
    packs = [lax.dynamic_index_in_dim(both, place[0] ^ k, 0, False) for k in range(QUAD)]
    return [pack[None] for pack in packs[:2]], [packs[2:]]


def keys_kernel(place, lengths, near, far, latent, turned, bias):
    rows, depth, wide = near.shape[0], latent.shape[1], turned.shape[0]
    side, core = place[0] // 2, place[0] % 2
    for c, blocks in enumerate((near, far)):
        for k in range(2):
            for quad in range(2):
                first = (quad * 2 + (side ^ k)) * 2 * rows + c * rows
                at = pl.ds(pl.multiple_of(first, rows), rows)
                block = blocks[:, (k * 2 + quad) * wide : (k * 2 + quad + 1) * wide]
                latent[at, :] = block[:, :depth]
                turned[:depth, at] = block[:, :depth].T
                turned[depth:, at] = block[:, depth:].T
    count = bias.shape[1]
    spot = lax.broadcasted_iota(jnp.int32, (rows, count), 1) ^ (core * rows)
    row = lax.broadcasted_iota(jnp.int32, (rows, 1), 0)
    for k in range(QUAD):
        spots = spot + (QUAD * (place[1] - 1) + 2 * (side ^ (k // 2))) * rows
        mine = row + (QUAD * place[1] + (place[0] ^ k)) * rows
        begin, end = jnp.zeros_like(mine), 0
        for n in range(lengths.shape[0]):
            end = end + lengths[n]
            begin = jnp.where(mine >= end, end, begin)
        allowed = (spots >= begin) & (spots <= mine)
        bias[k * rows : (k + 1) * rows, :] = jnp.where(allowed, 0.0, -1e30).astype(jnp.float32)


def prepare_keys(place, lengths, near, far, depth):
    rows, wide = near.shape[0], near.shape[1] // QUAD
    return call(
        keys_kernel,
        in_specs=[SMEM] * 2 + [IN_VMEM] * 2,
        out_specs=[IN_VMEM] * 3,
        out_shape=[
            jax.ShapeDtypeStruct((2 * QUAD * rows, depth), near.dtype),
            jax.ShapeDtypeStruct((wide, 2 * QUAD * rows), near.dtype),
            jax.ShapeDtypeStruct((QUAD * rows, (QUAD + 2) * rows), jnp.float32),
        ],
        name="keys",
    )(place, lengths, near, far)


def attend_kernel(factor, halves, chunk, rotary, place, *refs):
    sources, pieces = refs[: 2 * len(halves)], refs[2 * len(halves) : -11]
    keys, latent, bias, mixed, packs, absorb, left, scores, weights, scale, sems = refs[-11:]
    rows, (heads, plain, depth), count = packs.shape[1], absorb.shape, bias.shape[1]
    both = 2 * rows

    def fetch(source, target):
        copies.append(pltpu.make_async_copy(source, target, sems.at[len(copies)]))
        copies[-1].start()
        return copies[-1]

    copies, ready, first = [], {}, 0
    for n, source in enumerate(sources):
        source = source.at[chunk] if len(source.shape) == 3 else source
        copy = fetch(source.at[:, pl.ds(0, packs.shape[2])], packs.at[n])
        ready.setdefault((n // 2, 0), []).append(copy)
    for piece in pieces:
        held = absorb.at[pl.ds(first, piece.shape[0])]
        width = depth if piece.shape[1] == plain else piece.shape[2]
        for at in range(0, depth, width):
            source = piece if width == depth else piece.at[:, pl.ds(at // width * plain, plain)]
            target = held if width == depth else held.at[:, :, pl.ds(at, width)]
            ready.setdefault((0, first), []).append(fetch(source, target))
        first += piece.shape[0]

    lane = lax.broadcasted_iota(jnp.int32, (both, 2 * rotary), 1)
    units = [(n, head) for head in range(0, heads, 2) for n in range(len(halves))]

    def window_of(n):
        return (place[0] // 2 ^ halves[n]) * both

    def project(u):
        n, head = units[u]
        for copy in ready.get((n, head), []):
            copy.wait()
        near, far = packs.at[2 * n], packs.at[2 * n + 1]
        base = head // UNIT * UNIT * (plain + rotary)
        for h in range(2):
            at = slice(base + h * plain, base + (h + 1) * plain)
            q = jnp.concatenate([near[:, at], far[:, at]], axis=0)
            q = dot(q, absorb[head + h]).astype(jnp.bfloat16)
            at = slice(base + UNIT * plain, base + UNIT * plain + 2 * rotary)
            r = jnp.concatenate([near[:, at], far[:, at]], axis=0)
            mine = (lane < rotary) if h == 0 else (lane >= rotary)
            rows_of = slice(h * both, (h + 1) * both)
            left[u % 2, rows_of, :depth] = q
            left[u % 2, rows_of, depth:] = jnp.where(mine, r, jnp.zeros_like(r))

    def score(u, first):
        at = pl.ds(pl.multiple_of(window_of(units[u][0]) + first, BLOCK), BLOCK)
        scores[u % 2, :, first : first + BLOCK] = dot(left[u % 2], keys[:, at])

    def weigh(u, first):
        at = slice(first, first + STRIP)
        start = halves[units[u][0]] * both + first % both
        s = scores[u % 2, at, :] + bias[start : start + STRIP, :]
        w = jnp.exp2((s - jnp.max(s, axis=-1, keepdims=True)) * factor)
        scale[u % 2, at, :] = 1.0 / jnp.sum(w, axis=-1, keepdims=True)
        weights[u % 2, at, :] = w.astype(jnp.bfloat16)

    def mix(u, first):
        n, head = units[u]
        at = pl.ds(pl.multiple_of(window_of(n), BLOCK), count)
        summed = dot(weights[u % 2], latent[at, first : first + BLOCK])
        summed = (summed * scale[u % 2]).astype(jnp.bfloat16)
        for h in range(2):
            mixed[head + h, n * both : (n + 1) * both, first : first + BLOCK] = summed[
                h * both : (h + 1) * both
            ]

    last = len(units) - 1
    project(0)
    for first in range(0, count, BLOCK):
        score(0, first)
    project(min(1, last))
    for u in range(len(units)):
        beside = []
        if u < last:
            beside += [functools.partial(score, u + 1, first) for first in range(0, count, BLOCK)]
        if u > 0:
            mixes = [functools.partial(mix, u - 1, first) for first in range(0, depth, BLOCK)]
            beside[1:1] = mixes[:1]
            beside[3:3] = mixes[1:]
        if u + 1 < last:
            beside.append(functools.partial(project, u + 2))
        strips = list(range(0, 2 * both, STRIP))
        for n, first in enumerate(strips):
            for work in beside[n * len(beside) // len(strips) : (n + 1) * len(beside) // len(strips)]:
                work()
            weigh(u, first)
    for first in range(0, depth, BLOCK):
        mix(last, first)


def attend(place, sources, halves, chunk, absorb, keys, latent, bias, rotary, width):
    rows = sources[0].shape[-2]
    heads = sum(piece.shape[0] for piece in absorb)
    depth, plain = latent.shape[1], width // heads - rotary
    count = bias.shape[1]
    factor = math.log2(math.e) / math.sqrt(plain + rotary)
    return call(
        functools.partial(attend_kernel, factor, halves, chunk, rotary),
        in_specs=[SMEM] + [ANY] * (len(sources) + len(absorb)) + [IN_VMEM] * 3,
        out_specs=IN_VMEM,
        out_shape=jax.ShapeDtypeStruct((heads, 2 * len(halves) * rows, depth), jnp.bfloat16),
        scratch_shapes=[
            pltpu.VMEM((len(sources), rows, width), jnp.bfloat16),
            pltpu.VMEM((heads, plain, depth), jnp.bfloat16),
            pltpu.VMEM((2, QUAD * rows, keys.shape[0]), jnp.bfloat16),
            pltpu.VMEM((2, QUAD * rows, count), jnp.float32),
            pltpu.VMEM((2, QUAD * rows, count), jnp.bfloat16),
            pltpu.VMEM((2, QUAD * rows, 1), jnp.float32),
            pltpu.SemaphoreType.DMA((len(sources) + len(absorb) * depth // 128,)),
        ],
        name="attend",
        mib=24,
    )(place, *sources, *absorb, keys, latent, bias)


def value_kernel(mixed, *refs):
    pieces, (one, two, value) = refs[:-3], refs[-3:]
    take_heads(pieces, value)
    rows, width = one.shape[0], value.shape[2]
    for head in range(STEP_HEADS):
        out = dot(mixed[head], value[head]).astype(jnp.bfloat16)
        one[:, head * width : (head + 1) * width] = out[:rows]
        two[:, head * width : (head + 1) * width] = out[rows:]


def value_product(mixed, value, half, rows):
    heads, _, depth = mixed.shape
    width = value[0].shape[2]
    out = pl.BlockSpec((rows, STEP_HEADS * width), lambda i: (0, i))
    return call(
        value_kernel,
        grid=(heads // STEP_HEADS,),
        in_specs=[pl.BlockSpec((STEP_HEADS, 2 * rows, depth), lambda i: (i, half, 0))]
        + [IN_VMEM] * len(value),
        out_specs=[out] * 2,
        out_shape=[jax.ShapeDtypeStruct((rows, heads * width), jnp.bfloat16)] * 2,
        scratch_shapes=[pltpu.VMEM((STEP_HEADS, depth, width), jnp.bfloat16)],
        name="value",
    )(mixed, *value)


def join_kernel(chunks, pairs, shifted, place, *refs):
    parts, out, sems = refs[:-2], *refs[-2:]
    width = out.shape[1] // (pairs * QUAD * chunks)
    copies = []
    for c in range(chunks):
        for n, k in enumerate(JOIN_ORDER):
            at = (place[0] ^ k) * chunks + lax.rem(place[2] + c, chunks)
            for i in range(pairs):
                block = order_of(i, place[1], pairs) if shifted else i
                source = pl.ds(pl.multiple_of(block * width, width), width)
                target = (i * QUAD * chunks + at) * width
                copies.append(
                    pltpu.make_async_copy(
                        parts[c * QUAD + n].at[:, source],
                        out.at[:, pl.ds(pl.multiple_of(target, width), width)],
                        sems.at[len(copies)],
                    )
                )
                copies[-1].start()
    for copy in copies:
        copy.wait()


def join(place, parts, pairs, shifted):
    chunks = len(parts)
    rows, wide = parts[0][0].shape
    return call(
        functools.partial(join_kernel, chunks, pairs, shifted),
        in_specs=[SMEM] + [ANY] * (chunks * QUAD),
        out_specs=ANY,
        out_shape=jax.ShapeDtypeStruct((rows, chunks * QUAD * wide), jnp.bfloat16),
        scratch_shapes=[pltpu.SemaphoreType.DMA((chunks * QUAD * pairs,))],
        name="join",
    )(place, *[chunk[k] for chunk in parts for k in JOIN_ORDER])


def swap(block, k):
    return lax.ppermute(block, ("side", "core"), [(i, i ^ k) for i in range(QUAD)])


def after(later, *earlier):
    return lax.optimization_barrier((later, earlier))[0]


def across(part, distance):
    pairs = lax.axis_size("pair")
    return lax.ppermute(part, "pair", [(i, i ^ distance) for i in range(pairs)])


def from_group(part, c):
    groups = lax.axis_size("groups")
    return lax.ppermute(part, "groups", [((i + c) % groups, i) for i in range(groups)])


def on_device(
    query_plain, query_rotary, key_latent, key_rotary, absorb_weight, value_weight, lengths
):
    rows, head_count, plain = query_plain.shape
    rotary = key_rotary.shape[1]
    depth = key_latent.shape[1]
    held = absorb_weight.shape[0]
    pairs, groups = lax.axis_size("pair"), lax.axis_size("groups")
    names = ("groups", "pair", "side", "core")
    group, pair, side, core = (lax.axis_index(name) for name in names)
    here = 2 * side + core
    place = jnp.stack([here, pair, group]).astype(jnp.int32)
    by_group = held == groups * UNIT and plain == 128 and UNIT * rotary == 128
    by_group = by_group and pairs & (pairs - 1) == 0

    def far_quads(near):
        known, far, distance = near, [], 2
        while distance < pairs:
            far.append(across(known, distance))
            known = jnp.concatenate([known, far[-1]])
            distance *= 2
        return far

    if by_group:
        joined, near, far, mine, mine_value, pair_out = prepare(
            place,
            query_plain,
            query_rotary,
            absorb_weight,
            value_weight,
            key_latent,
            key_rotary,
            pairs,
            groups,
        )
    else:
        joined = jnp.concatenate([key_latent, key_rotary, key_rotary], axis=1)
    before = lax.ppermute(joined, "pair", [(i - 1, i) for i in range(1, pairs)])
    if by_group:
        near_pair = across(pair_out, 1)
        absorb = [mine[0]] + [across(mine[0], d) for d in range(2, pairs)] + [near_pair]
        both = jnp.concatenate([mine_value[0], near_pair[:, depth:]])
    else:
        absorb = [lax.all_gather(absorb_weight, "pair", axis=0, tiled=True)]
        value = [lax.all_gather(value_weight, "pair", axis=0, tiled=True)]
        flat = query_plain.reshape(rows, head_count * plain)
        near, far = pack_by_slices(place, flat, query_rotary, pairs)
    chunks, width = len(far), far[0][0].shape[1]

    keys = jnp.concatenate([before, joined], axis=1)
    coming = [swap(jnp.concatenate([far[0][0], keys], axis=1), 2), swap(far[0][1], 3)]
    near = [near[0], swap(after(near[1], coming[1]), 1)]
    keys = jnp.concatenate([keys, coming[0][:, width:]], axis=1)
    latent, turned, bias = prepare_keys(place, lengths, keys, swap(keys, 1), depth)
    if by_group:
        crossed = [None] + [from_group(near_pair, c) for c in range(1, groups)]
        value = far_quads(after(both, *absorb))
        value = [mine_value[0], *value, near_pair]

    def work(halves, c, sources, absorb_c):
        return attend(
            place, sources, halves, c, absorb_c, turned, latent, bias, rotary, width
        )

    parts = []
    for c in range(chunks):
        arrived = coming
        if c + 1 < chunks:
            following = after(far[c + 1], *arrived)
            coming = [swap(following[k - 2], k) for k in (2, 3)]
        if c == 0:
            absorb_c, value_c = absorb, value
        else:
            absorb_c = [mine[c], from_group(jnp.concatenate(absorb[1:-1]), c), crossed[c]]
            value_c = [mine_value[c]] + [from_group(piece, c) for piece in value[1:-1]]
            value_c.append(crossed[c])
        out = [None] * 2
        if c + 1 < chunks:
            mixed = work((0, 1), c, [*near, *arrived], absorb_c)
            value[1:-1] = value_c[1:-1] = after(value_c[1:-1], mixed)
            mixed = after(mixed, *coming)
            for half in (1, 0):
                out[half] = value_product(mixed, value_c, half, rows)
        else:
            for half in (1, 0):
                mixed = work((half,), c, (near, arrived)[half], absorb_c)
                out[half] = value_product(mixed, value_c, 0, rows)
                near = after(near, *out[half])
        back = swap(out[0][1], 1)
        coming = after(coming, back, *out[1])
        parts.append([out[0][0], back] + [swap(out[1][k - 2], k) for k in (2, 3)])
    return join(place, parts, pairs, by_group)


def solution(mesh):
    groups, ctx = mesh.shape["groups"], mesh.shape["ctx"]
    names = ("groups", "pair", "side", "core")
    fine = Mesh(np.asarray(mesh.devices).reshape(groups, ctx // QUAD, 2, 2), names)
    return jax.shard_map(
        on_device,
        mesh=fine,
        in_specs=(
            P(names, None, None),
            P(names, None),
            P(names, None),
            P(names, None),
            P(names[1:], None, None),
            P(names[1:], None, None),
            P("groups"),
        ),
        out_specs=P(names, None),
        check_vma=False,
    )
```

```python
import functools
import math

import jax
import jax.numpy as jnp
import numpy as np
from jax import lax
from jax.experimental import pallas as pl
from jax.experimental.pallas import tpu as pltpu
from jax.sharding import Mesh, PartitionSpec as P

QUAD = 4
JOIN_ORDER = (0, 2, 3, 1)
UNIT = 2
STEP_HEADS = 4
STRIP = 32


def dot(a, b):
    return jnp.dot(a, b, preferred_element_type=jnp.float32)


def call(kernel, mib=16, moved=0, **kw):
    return pl.pallas_call(
        kernel,
        compiler_params=pltpu.CompilerParams(vmem_limit_bytes=mib * 2**20),
        cost_estimate=pl.CostEstimate(flops=0, bytes_accessed=moved, transcendentals=0),
        **kw,
    )


HBM, IN_VMEM = pl.BlockSpec(memory_space=pltpu.HBM), pl.BlockSpec(memory_space=pltpu.VMEM)
ANY, SMEM = pl.BlockSpec(memory_space=pl.ANY), pl.BlockSpec(memory_space=pltpu.SMEM)


def take_heads(pieces, held):
    where = []
    for piece in pieces:
        where += [(piece, h) for h in range(piece.shape[0])]
    for first in range(0, len(where), STEP_HEADS):

        @pl.when(pl.program_id(0) == first // STEP_HEADS)
        def _():
            for h in range(STEP_HEADS):
                piece, at = where[first + h]
                held[h] = piece[at, piece.shape[1] - held.shape[1] :, :]


def order_of(quad, here, pairs):
    distance = quad ^ here
    order = jnp.where(distance == 1, pairs - 1, distance - 1)
    return jnp.where(distance == 0, 0, order)


def prepare_kernel(groups, pairs, place, *refs):
    plain, rotary, absorb, value = refs[:4]
    packs, refs = refs[4 : 6 + 2 * groups], refs[6 + 2 * groups :]
    stacked, values, both = (refs[c * groups : (c + 1) * groups] for c in range(3))
    refs = refs[3 * groups :]
    plain_in, rotary_in, absorb_in, value_in, single, flat, sems = refs
    rows, heads, width = plain_in.shape
    depth = value_in.shape[2]
    held, carried = heads // pairs, absorb_in.shape[1]
    copies = []

    def fetch(source, target):
        copies.append(pltpu.make_async_copy(source, target, sems.at[len(copies)]))
        copies[-1].start()

    for c in range(groups):
        at = pl.ds(lax.rem(place[2] + c, groups) * carried, carried)
        fetch(absorb.at[at], absorb_in.at[c])
        fetch(value.at[at], value_in.at[c])
    for i in range(pairs):
        at = pl.ds(i * held, held)
        fetch(plain.at[:, at], plain_in.at[:, at])
    fetch(rotary, rotary_in)

    for c in range(groups):
        copies[2 * c].wait()
        copies[2 * c + 1].wait()
        for first in range(0, depth, width):
            stacked[c][:, first : first + width, :] = absorb_in[c, :, :, first : first + width]
        values[c][...] = value_in[c]
        both[c][:, :depth, :] = stacked[c][...]
        both[c][:, depth:, :] = value_in[c]

    wide, thin = UNIT * width, rotary_in.shape[1] // (pairs * QUAD * groups)
    copies[-1].wait()
    for i in range(pairs):
        copies[2 * groups + i].wait()
        part = plain_in[:, i * held : (i + 1) * held, :]
        single[...] = part.astype(jnp.float32).reshape(rows * held, width)
        for head in range(held):
            part = single[pl.ds(head, rows, stride=held), :]
            flat[:, head * width : (head + 1) * width] = part.astype(flat.dtype)
        first = pl.multiple_of(order_of(i, place[1], pairs) * (wide + thin), wide + thin)
        for c in range(groups):
            for k in range(QUAD):
                at = (place[0] ^ k) * groups + lax.rem(place[2] + c, groups)
                out = packs[k].at[c] if k < 2 else packs[2 + c * 2 + k - 2]
                part = flat[:, pl.ds(pl.multiple_of(at * wide, wide), wide)]
                out[:, pl.ds(first, wide)] = part
                at = at * thin + i * thin * QUAD * groups
                part = rotary_in[:, pl.ds(pl.multiple_of(at, thin), thin)]
                out[:, pl.ds(pl.multiple_of(first + wide, thin), thin)] = part


def prepare(place, plain, rotary, absorb, value, pairs, groups):
    rows, heads, wide = plain.shape
    width = (heads * wide + rotary.shape[1]) // (QUAD * groups)
    held = absorb.shape[0] // groups
    part, dtype = (held, *value.shape[1:]), plain.dtype
    shapes = [(groups, rows, width)] * 2 + [(rows, width)] * (2 * groups)
    shapes += [part] * (2 * groups) + [(held, 2 * part[1], part[2])] * groups
    outs = call(
        functools.partial(prepare_kernel, groups, pairs),
        in_specs=[SMEM] + [HBM] * 4,
        out_specs=[IN_VMEM] * len(shapes),
        out_shape=[jax.ShapeDtypeStruct(shape, dtype) for shape in shapes],
        scratch_shapes=[
            pltpu.VMEM(plain.shape, dtype),
            pltpu.VMEM(rotary.shape, dtype),
            pltpu.VMEM((groups, held, *absorb.shape[1:]), dtype),
            pltpu.VMEM((groups, held, *value.shape[1:]), dtype),
            pltpu.VMEM((rows * heads // pairs, wide), jnp.float32),
            pltpu.VMEM((rows, heads // pairs * wide), dtype),
            pltpu.SemaphoreType.DMA((2 * groups + pairs + 1,)),
        ],
        moved=12 * 2**20,
        name="prepare",
    )(place, plain, rotary, absorb, value)
    far = outs[2 : 2 + 2 * groups]
    weights = outs[2 + 2 * groups :]
    return (
        outs[:2],
        [list(far[2 * c : 2 * c + 2]) for c in range(groups)],
        weights[:groups],
        weights[groups : 2 * groups],
        weights[2 * groups :],
    )


def pack_by_slices(place, plain, rotary, pairs):
    def sets(array):
        width = array.shape[1] // (QUAD * pairs)
        pick = lambda s: [
            array[:, (QUAD * i + s) * width : (QUAD * i + s + 1) * width] for i in range(pairs)
        ]
        whole = jnp.stack([jnp.concatenate(pick(s), axis=1) for s in range(QUAD)])
        steps = whole.shape[2] // (UNIT * (array.shape[1] // heads))
        return whole.reshape(QUAD, array.shape[0], steps, -1)

    heads = plain.shape[1] // 128
    both = jnp.concatenate([sets(plain), sets(rotary)], axis=3)
    both = both.reshape(QUAD, plain.shape[0], -1)
    packs = [lax.dynamic_index_in_dim(both, place[0] ^ k, 0, False) for k in range(QUAD)]
    return [pack[None] for pack in packs[:2]], [packs[2:]]


def joined_kernel(latent, rotary, joined, rotary_in, sems):
    depth = latent.shape[1]
    copies = [
        pltpu.make_async_copy(rotary, rotary_in, sems.at[0]),
        pltpu.make_async_copy(latent, joined.at[:, pl.ds(0, depth)], sems.at[1]),
    ]
    for copy in copies:
        copy.start()
    copies[0].wait()
    joined[:, depth:] = jnp.concatenate([rotary_in[...]] * 2, axis=0).T
    copies[1].wait()


def join_keys(latent, rotary):
    shape = (latent.shape[0], latent.shape[1] + 2 * rotary.shape[1])
    return call(
        joined_kernel,
        in_specs=[HBM, HBM],
        out_specs=IN_VMEM,
        out_shape=jax.ShapeDtypeStruct(shape, latent.dtype),
        scratch_shapes=[
            pltpu.VMEM(rotary.shape[::-1], rotary.dtype),
            pltpu.SemaphoreType.DMA((2,)),
        ],
        name="joined",
    )(latent, rotary.T)


def keys_kernel(place, lengths, near, far, latent, turned, bias):
    rows, depth, wide = near.shape[0], latent.shape[1], turned.shape[0]
    side, core = place[0] // 2, place[0] % 2
    for c, blocks in enumerate((near, far)):
        for k in range(2):
            for quad in range(2):
                first = (quad * 2 + (side ^ k)) * 2 * rows + c * rows
                at = pl.ds(pl.multiple_of(first, rows), rows)
                block = blocks[:, (k * 2 + quad) * wide : (k * 2 + quad + 1) * wide]
                latent[at, :] = block[:, :depth]
                turned[:depth, at] = block[:, :depth].T
                turned[depth:, at] = block[:, depth:].T
    count = bias.shape[1]
    spot = lax.broadcasted_iota(jnp.int32, (rows, count), 1) ^ (core * rows)
    row = lax.broadcasted_iota(jnp.int32, (rows, 1), 0)
    for k in range(QUAD):
        spots = spot + (QUAD * (place[1] - 1) + 2 * (side ^ (k // 2))) * rows
        mine = row + (QUAD * place[1] + (place[0] ^ k)) * rows
        begin, end = jnp.zeros_like(mine), 0
        for n in range(lengths.shape[0]):
            end = end + lengths[n]
            begin = jnp.where(mine >= end, end, begin)
        allowed = (spots >= begin) & (spots <= mine)
        bias[k * rows : (k + 1) * rows, :] = jnp.where(allowed, 0.0, -1e30).astype(jnp.float32)


def prepare_keys(place, lengths, near, far, depth):
    rows, wide = near.shape[0], near.shape[1] // QUAD
    return call(
        keys_kernel,
        in_specs=[SMEM] * 2 + [IN_VMEM] * 2,
        out_specs=[IN_VMEM] * 3,
        out_shape=[
            jax.ShapeDtypeStruct((2 * QUAD * rows, depth), near.dtype),
            jax.ShapeDtypeStruct((wide, 2 * QUAD * rows), near.dtype),
            jax.ShapeDtypeStruct((QUAD * rows, (QUAD + 2) * rows), jnp.float32),
        ],
        name="keys",
    )(place, lengths, near, far)


def attend_kernel(factor, halves, chunk, rotary, place, *refs):
    sources, pieces = refs[: 2 * len(halves)], refs[2 * len(halves) : -9]
    keys, latent, bias, mixed, packs, absorb, scores, weights, sems = refs[-9:]
    rows, (heads, plain, depth), count = packs.shape[1], absorb.shape, bias.shape[1]
    both = 2 * rows

    def fetch(source, target):
        copies.append(pltpu.make_async_copy(source, target, sems.at[len(copies)]))
        copies[-1].start()
        return copies[-1]

    copies, ready, first = [], {}, 0
    for n, source in enumerate(sources):
        source = source.at[chunk] if len(source.shape) == 3 else source
        copy = fetch(source.at[:, pl.ds(0, packs.shape[2])], packs.at[n])
        ready.setdefault((n // 2, 0), []).append(copy)
    for piece in pieces:
        held = absorb.at[pl.ds(first, piece.shape[0])]
        width = depth if piece.shape[1] == plain else piece.shape[2]
        for at in range(0, depth, width):
            source = piece if width == depth else piece.at[:, pl.ds(at // width * plain, plain)]
            target = held if width == depth else held.at[:, :, pl.ds(at, width)]
            ready.setdefault((0, first), []).append(fetch(source, target))
        first += piece.shape[0]

    lane = lax.broadcasted_iota(jnp.int32, (both, 2 * rotary), 1)
    units = [(n, head) for head in range(0, heads, 2) for n in range(len(halves))]

    def window(n):
        return pl.ds(pl.multiple_of((place[0] // 2 ^ halves[n]) * both, both), count)

    def score(u):
        n, head = units[u]
        for copy in ready.get((n, head), []):
            copy.wait()
        near, far = packs.at[2 * n], packs.at[2 * n + 1]
        base = head // UNIT * UNIT * (plain + rotary)
        for h in range(2):
            at = slice(base + h * plain, base + (h + 1) * plain)
            q = jnp.concatenate([near[:, at], far[:, at]], axis=0)
            q = dot(q, absorb[head + h]).astype(jnp.bfloat16)
            at = slice(base + UNIT * plain, base + UNIT * plain + 2 * rotary)
            r = jnp.concatenate([near[:, at], far[:, at]], axis=0)
            mine = (lane < rotary) if h == 0 else (lane >= rotary)
            left = jnp.concatenate([q, jnp.where(mine, r, jnp.zeros_like(r))], axis=1)
            scores[u % 2, h * both : (h + 1) * both, :] = dot(left, keys[:, window(n)])

    def weigh(u):
        scale = []
        for first in range(0, 2 * both, STRIP):
            at = slice(first, first + STRIP)
            start = halves[units[u][0]] * both + first % both
            s = scores[u % 2, at, :] + bias[start : start + STRIP, :]
            w = jnp.exp2((s - jnp.max(s, axis=-1, keepdims=True)) * factor)
            scale.append(1.0 / jnp.sum(w, axis=-1, keepdims=True))
            weights[u % 2, at, :] = w.astype(jnp.bfloat16)
        return jnp.concatenate(scale, axis=0)

    score(0)
    for u, (n, head) in enumerate(units):
        if u + 1 < len(units):
            score(u + 1)
        scale = weigh(u)
        for h in range(2):
            at = slice(h * both, (h + 1) * both)
            summed = dot(weights[u % 2, at, :], latent[window(n), :])
            mixed[head + h, n * both : (n + 1) * both, :] = (summed * scale[at]).astype(jnp.bfloat16)


def attend(place, sources, halves, chunk, absorb, keys, latent, bias, rotary, width):
    rows = sources[0].shape[-2]
    heads = sum(piece.shape[0] for piece in absorb)
    depth, plain = latent.shape[1], width // heads - rotary
    count = bias.shape[1]
    factor = math.log2(math.e) / math.sqrt(plain + rotary)
    return call(
        functools.partial(attend_kernel, factor, halves, chunk, rotary),
        in_specs=[SMEM] + [ANY] * (len(sources) + len(absorb)) + [IN_VMEM] * 3,
        out_specs=IN_VMEM,
        out_shape=jax.ShapeDtypeStruct((heads, 2 * len(halves) * rows, depth), jnp.bfloat16),
        scratch_shapes=[
            pltpu.VMEM((len(sources), rows, width), jnp.bfloat16),
            pltpu.VMEM((heads, plain, depth), jnp.bfloat16),
            pltpu.VMEM((2, QUAD * rows, count), jnp.float32),
            pltpu.VMEM((2, QUAD * rows, count), jnp.bfloat16),
            pltpu.SemaphoreType.DMA((len(sources) + len(absorb) * depth // 128,)),
        ],
        name="attend",
        mib=24,
    )(place, *sources, *absorb, keys, latent, bias)


def value_kernel(mixed, *refs):
    pieces, (one, two, value) = refs[:-3], refs[-3:]
    take_heads(pieces, value)
    rows, width = one.shape[0], value.shape[2]
    for head in range(STEP_HEADS):
        out = dot(mixed[head], value[head]).astype(jnp.bfloat16)
        one[:, head * width : (head + 1) * width] = out[:rows]
        two[:, head * width : (head + 1) * width] = out[rows:]


def value_product(mixed, value, half, rows):
    heads, _, depth = mixed.shape
    width = value[0].shape[2]
    out = pl.BlockSpec((rows, STEP_HEADS * width), lambda i: (0, i))
    return call(
        value_kernel,
        grid=(heads // STEP_HEADS,),
        in_specs=[pl.BlockSpec((STEP_HEADS, 2 * rows, depth), lambda i: (i, half, 0))]
        + [IN_VMEM] * len(value),
        out_specs=[out] * 2,
        out_shape=[jax.ShapeDtypeStruct((rows, heads * width), jnp.bfloat16)] * 2,
        scratch_shapes=[pltpu.VMEM((STEP_HEADS, depth, width), jnp.bfloat16)],
        name="value",
    )(mixed, *value)


def join_kernel(chunks, pairs, shifted, place, *refs):
    parts, out, sems = refs[:-2], *refs[-2:]
    width = out.shape[1] // (pairs * QUAD * chunks)
    copies = []
    for c in range(chunks):
        for n, k in enumerate(JOIN_ORDER):
            at = (place[0] ^ k) * chunks + lax.rem(place[2] + c, chunks)
            for i in range(pairs):
                block = order_of(i, place[1], pairs) if shifted else i
                source = pl.ds(pl.multiple_of(block * width, width), width)
                target = (i * QUAD * chunks + at) * width
                copies.append(
                    pltpu.make_async_copy(
                        parts[c * QUAD + n].at[:, source],
                        out.at[:, pl.ds(pl.multiple_of(target, width), width)],
                        sems.at[len(copies)],
                    )
                )
                copies[-1].start()
    for copy in copies:
        copy.wait()


def join(place, parts, pairs, shifted):
    chunks = len(parts)
    rows, wide = parts[0][0].shape
    return call(
        functools.partial(join_kernel, chunks, pairs, shifted),
        in_specs=[SMEM] + [ANY] * (chunks * QUAD),
        out_specs=ANY,
        out_shape=jax.ShapeDtypeStruct((rows, chunks * QUAD * wide), jnp.bfloat16),
        scratch_shapes=[pltpu.SemaphoreType.DMA((chunks * QUAD * pairs,))],
        name="join",
    )(place, *[chunk[k] for chunk in parts for k in JOIN_ORDER])


def swap(block, k):
    return lax.ppermute(block, ("side", "core"), [(i, i ^ k) for i in range(QUAD)])


def after(later, *earlier):
    return lax.optimization_barrier((later, earlier))[0]


def across(part, distance):
    pairs = lax.axis_size("pair")
    return lax.ppermute(part, "pair", [(i, i ^ distance) for i in range(pairs)])


def from_group(part, c):
    groups = lax.axis_size("groups")
    return lax.ppermute(part, "groups", [((i + c) % groups, i) for i in range(groups)])


def on_device(
    query_plain, query_rotary, key_latent, key_rotary, absorb_weight, value_weight, lengths
):
    rows, head_count, plain = query_plain.shape
    rotary = key_rotary.shape[1]
    depth = key_latent.shape[1]
    held = absorb_weight.shape[0]
    pairs, groups = lax.axis_size("pair"), lax.axis_size("groups")
    names = ("groups", "pair", "side", "core")
    group, pair, side, core = (lax.axis_index(name) for name in names)
    here = 2 * side + core
    place = jnp.stack([here, pair, group]).astype(jnp.int32)
    by_group = held == groups * UNIT and plain == 128 and UNIT * rotary == 128
    by_group = by_group and pairs & (pairs - 1) == 0

    def far_quads(near):
        known, far, distance = near, [], 2
        while distance < pairs:
            far.append(across(known, distance))
            known = jnp.concatenate([known, far[-1]])
            distance *= 2
        return far

    if by_group:
        joined = join_keys(key_latent, key_rotary)
    else:
        joined = jnp.concatenate([key_latent, key_rotary, key_rotary], axis=1)
    before = lax.ppermute(joined, "pair", [(i - 1, i) for i in range(1, pairs)])
    if by_group:
        near, far, mine, mine_value, pair_out = prepare(
            place, query_plain, query_rotary, absorb_weight, value_weight, pairs, groups
        )
        nearest = [across(pair, 1) for pair in pair_out]
        near_pair = nearest[0]
        absorb = [mine[0]] + [across(mine[0], d) for d in range(2, pairs)] + [near_pair]
        both = jnp.concatenate([mine_value[0], near_pair[:, depth:]])
        value = [mine_value[0], *far_quads(after(both, *absorb)), near_pair]
    else:
        absorb = [lax.all_gather(absorb_weight, "pair", axis=0, tiled=True)]
        value = [lax.all_gather(value_weight, "pair", axis=0, tiled=True)]
        flat = query_plain.reshape(rows, head_count * plain)
        near, far = pack_by_slices(place, flat, query_rotary, pairs)
    chunks, width = len(far), far[0][0].shape[1]

    keys = jnp.concatenate([before, joined], axis=1)
    coming = [swap(jnp.concatenate([far[0][0], keys], axis=1), 2), swap(far[0][1], 3)]
    near = [near[0], swap(after(near[1], coming[1]), 1)]
    keys = jnp.concatenate([keys, coming[0][:, width:]], axis=1)
    latent, turned, bias = prepare_keys(place, lengths, keys, swap(keys, 1), depth)

    def work(halves, c, sources, absorb_c):
        return attend(
            place, sources, halves, c, absorb_c, turned, latent, bias, rotary, width
        )

    parts = []
    for c in range(chunks):
        arrived = coming
        if c + 1 < chunks:
            following = after(far[c + 1], *arrived)
            coming = [swap(following[k - 2], k) for k in (2, 3)]
        if c == 0:
            absorb_c, value_c = absorb, value
        else:
            absorb_c = [mine[c], from_group(jnp.concatenate(absorb[1:-1]), c), nearest[c]]
            value_c = [mine_value[c]] + [from_group(piece, c) for piece in value[1:-1]]
            value_c.append(nearest[c])
        out = [None] * 2
        if c + 1 < chunks:
            mixed = work((0, 1), c, [*near, *arrived], absorb_c)
            value[1:-1] = value_c[1:-1] = after(value_c[1:-1], mixed)
            mixed = after(mixed, *coming)
            for half in (1, 0):
                out[half] = value_product(mixed, value_c, half, rows)
        else:
            for half in (1, 0):
                mixed = work((half,), c, (near, arrived)[half], absorb_c)
                out[half] = value_product(mixed, value_c, 0, rows)
                near = after(near, *out[half])
        back = swap(out[0][1], 1)
        coming = after(coming, back, *out[1])
        parts.append([out[0][0], back] + [swap(out[1][k - 2], k) for k in (2, 3)])
    return join(place, parts, pairs, by_group)


def solution(mesh):
    groups, ctx = mesh.shape["groups"], mesh.shape["ctx"]
    names = ("groups", "pair", "side", "core")
    fine = Mesh(np.asarray(mesh.devices).reshape(groups, ctx // QUAD, 2, 2), names)
    return jax.shard_map(
        on_device,
        mesh=fine,
        in_specs=(
            P(names, None, None),
            P(names, None),
            P(names, None),
            P(names, None),
            P(names[1:], None, None),
            P(names[1:], None, None),
            P("groups"),
        ),
        out_specs=P(names, None),
        check_vma=False,
    )
```

```python
import functools
import math

import jax
import jax.numpy as jnp
import numpy as np
from jax import lax
from jax.experimental import pallas as pl
from jax.experimental.pallas import tpu as pltpu
from jax.sharding import Mesh, PartitionSpec as P

QUAD = 4
JOIN_ORDER = (0, 2, 3, 1)
UNIT = 2
STEP_HEADS = 4
STRIP = 32


def dot(a, b):
    return jnp.dot(a, b, preferred_element_type=jnp.float32)


def call(kernel, mib=16, moved=0, **kw):
    return pl.pallas_call(
        kernel,
        compiler_params=pltpu.CompilerParams(vmem_limit_bytes=mib * 2**20),
        cost_estimate=pl.CostEstimate(flops=0, bytes_accessed=moved, transcendentals=0),
        **kw,
    )


HBM, IN_VMEM = pl.BlockSpec(memory_space=pltpu.HBM), pl.BlockSpec(memory_space=pltpu.VMEM)
ANY, SMEM = pl.BlockSpec(memory_space=pl.ANY), pl.BlockSpec(memory_space=pltpu.SMEM)


def take_heads(pieces, held):
    where = []
    for piece in pieces:
        where += [(piece, h) for h in range(piece.shape[0])]
    for first in range(0, len(where), STEP_HEADS):

        @pl.when(pl.program_id(0) == first // STEP_HEADS)
        def _():
            for h in range(STEP_HEADS):
                piece, at = where[first + h]
                held[h] = piece[at, piece.shape[1] - held.shape[1] :, :]


def order_of(quad, here, pairs):
    distance = quad ^ here
    order = jnp.where(distance == 1, pairs - 1, distance - 1)
    return jnp.where(distance == 0, 0, order)


def prepare_kernel(groups, pairs, place, *refs):
    plain, rotary, absorb, value = refs[:4]
    packs, refs = refs[4 : 6 + 2 * groups], refs[6 + 2 * groups :]
    stacked, values, pair = refs[:groups], refs[groups : 2 * groups], refs[2 * groups]
    refs = refs[2 * groups + 1 :]
    plain_in, rotary_in, absorb_in, value_in, single, flat, sems = refs
    rows, heads, width = plain_in.shape
    depth = value_in.shape[2]
    held, carried = heads // pairs, absorb_in.shape[1]
    copies = []

    def fetch(source, target):
        copies.append(pltpu.make_async_copy(source, target, sems.at[len(copies)]))
        copies[-1].start()

    for c in range(groups):
        at = pl.ds(lax.rem(place[2] + c, groups) * carried, carried)
        fetch(absorb.at[at], absorb_in.at[c])
        fetch(value.at[at], value_in.at[c])
    for i in range(pairs):
        at = pl.ds(i * held, held)
        fetch(plain.at[:, at], plain_in.at[:, at])
    fetch(rotary, rotary_in)

    for c in range(groups):
        copies[2 * c].wait()
        copies[2 * c + 1].wait()
        for first in range(0, depth, width):
            stacked[c][:, first : first + width, :] = absorb_in[c, :, :, first : first + width]
        values[c][...] = value_in[c]
    pair[:, :depth, :] = stacked[0][...]
    pair[:, depth:, :] = value_in[0]

    wide, thin = UNIT * width, rotary_in.shape[1] // (pairs * QUAD * groups)
    copies[-1].wait()
    for i in range(pairs):
        copies[2 * groups + i].wait()
        part = plain_in[:, i * held : (i + 1) * held, :]
        single[...] = part.astype(jnp.float32).reshape(rows * held, width)
        for head in range(held):
            part = single[pl.ds(head, rows, stride=held), :]
            flat[:, head * width : (head + 1) * width] = part.astype(flat.dtype)
        first = pl.multiple_of(order_of(i, place[1], pairs) * (wide + thin), wide + thin)
        for c in range(groups):
            for k in range(QUAD):
                at = (place[0] ^ k) * groups + lax.rem(place[2] + c, groups)
                out = packs[k].at[c] if k < 2 else packs[2 + c * 2 + k - 2]
                part = flat[:, pl.ds(pl.multiple_of(at * wide, wide), wide)]
                out[:, pl.ds(first, wide)] = part
                at = at * thin + i * thin * QUAD * groups
                part = rotary_in[:, pl.ds(pl.multiple_of(at, thin), thin)]
                out[:, pl.ds(pl.multiple_of(first + wide, thin), thin)] = part


def prepare(place, plain, rotary, absorb, value, pairs, groups):
    rows, heads, wide = plain.shape
    width = (heads * wide + rotary.shape[1]) // (QUAD * groups)
    held = absorb.shape[0] // groups
    part, dtype = (held, *value.shape[1:]), plain.dtype
    shapes = [(groups, rows, width)] * 2 + [(rows, width)] * (2 * groups)
    shapes += [part] * (2 * groups) + [(held, 2 * part[1], part[2])]
    outs = call(
        functools.partial(prepare_kernel, groups, pairs),
        in_specs=[SMEM] + [HBM] * 4,
        out_specs=[IN_VMEM] * len(shapes),
        out_shape=[jax.ShapeDtypeStruct(shape, dtype) for shape in shapes],
        scratch_shapes=[
            pltpu.VMEM(plain.shape, dtype),
            pltpu.VMEM(rotary.shape, dtype),
            pltpu.VMEM((groups, held, *absorb.shape[1:]), dtype),
            pltpu.VMEM((groups, held, *value.shape[1:]), dtype),
            pltpu.VMEM((rows * heads // pairs, wide), jnp.float32),
            pltpu.VMEM((rows, heads // pairs * wide), dtype),
            pltpu.SemaphoreType.DMA((2 * groups + pairs + 1,)),
        ],
        moved=12 * 2**20,
        mib=48,
        name="prepare",
    )(place, plain, rotary, absorb, value)
    far = outs[2 : 2 + 2 * groups]
    weights = outs[2 + 2 * groups :]
    return (
        outs[:2],
        [list(far[2 * c : 2 * c + 2]) for c in range(groups)],
        weights[:groups],
        weights[groups : 2 * groups],
        weights[-1],
    )


def pack_by_slices(place, plain, rotary, pairs):
    def sets(array):
        width = array.shape[1] // (QUAD * pairs)
        pick = lambda s: [
            array[:, (QUAD * i + s) * width : (QUAD * i + s + 1) * width] for i in range(pairs)
        ]
        whole = jnp.stack([jnp.concatenate(pick(s), axis=1) for s in range(QUAD)])
        steps = whole.shape[2] // (UNIT * (array.shape[1] // heads))
        return whole.reshape(QUAD, array.shape[0], steps, -1)

    heads = plain.shape[1] // 128
    both = jnp.concatenate([sets(plain), sets(rotary)], axis=3)
    both = both.reshape(QUAD, plain.shape[0], -1)
    packs = [lax.dynamic_index_in_dim(both, place[0] ^ k, 0, False) for k in range(QUAD)]
    return [pack[None] for pack in packs[:2]], [packs[2:]]


def joined_kernel(latent, rotary, joined, rotary_in, sems):
    depth = latent.shape[1]
    copies = [
        pltpu.make_async_copy(rotary, rotary_in, sems.at[0]),
        pltpu.make_async_copy(latent, joined.at[:, pl.ds(0, depth)], sems.at[1]),
    ]
    for copy in copies:
        copy.start()
    copies[0].wait()
    joined[:, depth:] = jnp.concatenate([rotary_in[...]] * 2, axis=0).T
    copies[1].wait()


def join_keys(latent, rotary):
    shape = (latent.shape[0], latent.shape[1] + 2 * rotary.shape[1])
    return call(
        joined_kernel,
        in_specs=[HBM, HBM],
        out_specs=IN_VMEM,
        out_shape=jax.ShapeDtypeStruct(shape, latent.dtype),
        scratch_shapes=[
            pltpu.VMEM(rotary.shape[::-1], rotary.dtype),
            pltpu.SemaphoreType.DMA((2,)),
        ],
        name="joined",
    )(latent, rotary.T)


def keys_kernel(place, lengths, near, far, latent, turned, bias):
    rows, depth, wide = near.shape[0], latent.shape[1], turned.shape[0]
    side, core = place[0] // 2, place[0] % 2
    for c, blocks in enumerate((near, far)):
        for k in range(2):
            for quad in range(2):
                first = (quad * 2 + (side ^ k)) * 2 * rows + c * rows
                at = pl.ds(pl.multiple_of(first, rows), rows)
                block = blocks[:, (k * 2 + quad) * wide : (k * 2 + quad + 1) * wide]
                latent[at, :] = block[:, :depth]
                turned[:depth, at] = block[:, :depth].T
                turned[depth:, at] = block[:, depth:].T
    count = bias.shape[1]
    spot = lax.broadcasted_iota(jnp.int32, (rows, count), 1) ^ (core * rows)
    row = lax.broadcasted_iota(jnp.int32, (rows, 1), 0)
    for k in range(QUAD):
        spots = spot + (QUAD * (place[1] - 1) + 2 * (side ^ (k // 2))) * rows
        mine = row + (QUAD * place[1] + (place[0] ^ k)) * rows
        begin, end = jnp.zeros_like(mine), 0
        for n in range(lengths.shape[0]):
            end = end + lengths[n]
            begin = jnp.where(mine >= end, end, begin)
        allowed = (spots >= begin) & (spots <= mine)
        bias[k * rows : (k + 1) * rows, :] = jnp.where(allowed, 0.0, -1e30).astype(jnp.float32)


def prepare_keys(place, lengths, near, far, depth):
    rows, wide = near.shape[0], near.shape[1] // QUAD
    return call(
        keys_kernel,
        in_specs=[SMEM] * 2 + [IN_VMEM] * 2,
        out_specs=[IN_VMEM] * 3,
        out_shape=[
            jax.ShapeDtypeStruct((2 * QUAD * rows, depth), near.dtype),
            jax.ShapeDtypeStruct((wide, 2 * QUAD * rows), near.dtype),
            jax.ShapeDtypeStruct((QUAD * rows, (QUAD + 2) * rows), jnp.float32),
        ],
        name="keys",
    )(place, lengths, near, far)


def attend_kernel(factor, halves, chunk, rotary, place, *refs):
    sources, pieces = refs[: 2 * len(halves)], refs[2 * len(halves) : -9]
    keys, latent, bias, mixed, packs, absorb, scores, weights, sems = refs[-9:]
    rows, (heads, plain, depth), count = packs.shape[1], absorb.shape, bias.shape[1]
    both = 2 * rows

    def fetch(source, target):
        copies.append(pltpu.make_async_copy(source, target, sems.at[len(copies)]))
        copies[-1].start()
        return copies[-1]

    copies, ready, first = [], {}, 0
    for n, source in enumerate(sources):
        source = source.at[chunk] if len(source.shape) == 3 else source
        copy = fetch(source.at[:, pl.ds(0, packs.shape[2])], packs.at[n])
        ready.setdefault((n // 2, 0), []).append(copy)
    for piece in pieces:
        held = absorb.at[pl.ds(first, piece.shape[0])]
        width = depth if piece.shape[1] == plain else piece.shape[2]
        for at in range(0, depth, width):
            source = piece if width == depth else piece.at[:, pl.ds(at // width * plain, plain)]
            target = held if width == depth else held.at[:, :, pl.ds(at, width)]
            ready.setdefault((0, first), []).append(fetch(source, target))
        first += piece.shape[0]

    lane = lax.broadcasted_iota(jnp.int32, (both, 2 * rotary), 1)
    units = [(n, head) for head in range(0, heads, 2) for n in range(len(halves))]

    def window(n):
        return pl.ds(pl.multiple_of((place[0] // 2 ^ halves[n]) * both, both), count)

    def score(u):
        n, head = units[u]
        for copy in ready.get((n, head), []):
            copy.wait()
        near, far = packs.at[2 * n], packs.at[2 * n + 1]
        base = head // UNIT * UNIT * (plain + rotary)
        for h in range(2):
            at = slice(base + h * plain, base + (h + 1) * plain)
            q = jnp.concatenate([near[:, at], far[:, at]], axis=0)
            q = dot(q, absorb[head + h]).astype(jnp.bfloat16)
            at = slice(base + UNIT * plain, base + UNIT * plain + 2 * rotary)
            r = jnp.concatenate([near[:, at], far[:, at]], axis=0)
            mine = (lane < rotary) if h == 0 else (lane >= rotary)
            left = jnp.concatenate([q, jnp.where(mine, r, jnp.zeros_like(r))], axis=1)
            scores[u % 2, h * both : (h + 1) * both, :] = dot(left, keys[:, window(n)])

    def weigh(u):
        scale = []
        for first in range(0, 2 * both, STRIP):
            at = slice(first, first + STRIP)
            start = halves[units[u][0]] * both + first % both
            s = scores[u % 2, at, :] + bias[start : start + STRIP, :]
            w = jnp.exp2((s - jnp.max(s, axis=-1, keepdims=True)) * factor)
            scale.append(1.0 / jnp.sum(w, axis=-1, keepdims=True))
            weights[u % 2, at, :] = w.astype(jnp.bfloat16)
        return jnp.concatenate(scale, axis=0)

    score(0)
    for u, (n, head) in enumerate(units):
        if u + 1 < len(units):
            score(u + 1)
        scale = weigh(u)
        for h in range(2):
            at = slice(h * both, (h + 1) * both)
            summed = dot(weights[u % 2, at, :], latent[window(n), :])
            mixed[head + h, n * both : (n + 1) * both, :] = (summed * scale[at]).astype(jnp.bfloat16)


def attend(place, sources, halves, chunk, absorb, keys, latent, bias, rotary, width):
    rows = sources[0].shape[-2]
    heads = sum(piece.shape[0] for piece in absorb)
    depth, plain = latent.shape[1], width // heads - rotary
    count = bias.shape[1]
    factor = math.log2(math.e) / math.sqrt(plain + rotary)
    return call(
        functools.partial(attend_kernel, factor, halves, chunk, rotary),
        in_specs=[SMEM] + [ANY] * (len(sources) + len(absorb)) + [IN_VMEM] * 3,
        out_specs=IN_VMEM,
        out_shape=jax.ShapeDtypeStruct((heads, 2 * len(halves) * rows, depth), jnp.bfloat16),
        scratch_shapes=[
            pltpu.VMEM((len(sources), rows, width), jnp.bfloat16),
            pltpu.VMEM((heads, plain, depth), jnp.bfloat16),
            pltpu.VMEM((2, QUAD * rows, count), jnp.float32),
            pltpu.VMEM((2, QUAD * rows, count), jnp.bfloat16),
            pltpu.SemaphoreType.DMA((len(sources) + len(absorb) * depth // 128,)),
        ],
        name="attend",
        mib=24,
    )(place, *sources, *absorb, keys, latent, bias)


def value_kernel(mixed, *refs):
    pieces, (one, two, value) = refs[:-3], refs[-3:]
    take_heads(pieces, value)
    rows, width = one.shape[0], value.shape[2]
    for head in range(STEP_HEADS):
        out = dot(mixed[head], value[head]).astype(jnp.bfloat16)
        one[:, head * width : (head + 1) * width] = out[:rows]
        two[:, head * width : (head + 1) * width] = out[rows:]


def value_product(mixed, value, half, rows):
    heads, _, depth = mixed.shape
    width = value[0].shape[2]
    out = pl.BlockSpec((rows, STEP_HEADS * width), lambda i: (0, i))
    return call(
        value_kernel,
        grid=(heads // STEP_HEADS,),
        in_specs=[pl.BlockSpec((STEP_HEADS, 2 * rows, depth), lambda i: (i, half, 0))]
        + [IN_VMEM] * len(value),
        out_specs=[out] * 2,
        out_shape=[jax.ShapeDtypeStruct((rows, heads * width), jnp.bfloat16)] * 2,
        scratch_shapes=[pltpu.VMEM((STEP_HEADS, depth, width), jnp.bfloat16)],
        name="value",
    )(mixed, *value)


def join_kernel(chunks, pairs, shifted, place, *refs):
    parts, out, sems = refs[:-2], *refs[-2:]
    width = out.shape[1] // (pairs * QUAD * chunks)
    copies = []
    for c in range(chunks):
        for n, k in enumerate(JOIN_ORDER):
            at = (place[0] ^ k) * chunks + lax.rem(place[2] + c, chunks)
            for i in range(pairs):
                block = order_of(i, place[1], pairs) if shifted else i
                source = pl.ds(pl.multiple_of(block * width, width), width)
                target = (i * QUAD * chunks + at) * width
                copies.append(
                    pltpu.make_async_copy(
                        parts[c * QUAD + n].at[:, source],
                        out.at[:, pl.ds(pl.multiple_of(target, width), width)],
                        sems.at[len(copies)],
                    )
                )
                copies[-1].start()
    for copy in copies:
        copy.wait()


def join(place, parts, pairs, shifted):
    chunks = len(parts)
    rows, wide = parts[0][0].shape
    return call(
        functools.partial(join_kernel, chunks, pairs, shifted),
        in_specs=[SMEM] + [ANY] * (chunks * QUAD),
        out_specs=ANY,
        out_shape=jax.ShapeDtypeStruct((rows, chunks * QUAD * wide), jnp.bfloat16),
        scratch_shapes=[pltpu.SemaphoreType.DMA((chunks * QUAD * pairs,))],
        name="join",
    )(place, *[chunk[k] for chunk in parts for k in JOIN_ORDER])


def swap(block, k):
    return lax.ppermute(block, ("side", "core"), [(i, i ^ k) for i in range(QUAD)])


def after(later, *earlier):
    return lax.optimization_barrier((later, earlier))[0]


def across(part, distance):
    pairs = lax.axis_size("pair")
    return lax.ppermute(part, "pair", [(i, i ^ distance) for i in range(pairs)])


def from_group(part, c):
    groups = lax.axis_size("groups")
    return lax.ppermute(part, "groups", [((i + c) % groups, i) for i in range(groups)])


def on_device(
    query_plain, query_rotary, key_latent, key_rotary, absorb_weight, value_weight, lengths
):
    rows, head_count, plain = query_plain.shape
    rotary = key_rotary.shape[1]
    depth = key_latent.shape[1]
    held = absorb_weight.shape[0]
    pairs, groups = lax.axis_size("pair"), lax.axis_size("groups")
    names = ("groups", "pair", "side", "core")
    group, pair, side, core = (lax.axis_index(name) for name in names)
    here = 2 * side + core
    place = jnp.stack([here, pair, group]).astype(jnp.int32)
    by_group = held == groups * UNIT and plain == 128 and UNIT * rotary == 128
    by_group = by_group and pairs & (pairs - 1) == 0

    def far_quads(near):
        known, far, distance = near, [], 2
        while distance < pairs:
            far.append(across(known, distance))
            known = jnp.concatenate([known, far[-1]])
            distance *= 2
        return far

    if by_group:
        joined = join_keys(key_latent, key_rotary)
    else:
        joined = jnp.concatenate([key_latent, key_rotary, key_rotary], axis=1)
    before = lax.ppermute(joined, "pair", [(i - 1, i) for i in range(1, pairs)])
    if by_group:
        near, far, mine, mine_value, pair_out = prepare(
            place, query_plain, query_rotary, absorb_weight, value_weight, pairs, groups
        )
        near_pair = across(pair_out, 1)
        absorb = [mine[0]] + [across(mine[0], d) for d in range(2, pairs)] + [near_pair]
        both = jnp.concatenate([mine_value[0], near_pair[:, depth:]])
        value = [mine_value[0], *far_quads(after(both, *absorb)), near_pair]
    else:
        absorb = [lax.all_gather(absorb_weight, "pair", axis=0, tiled=True)]
        value = [lax.all_gather(value_weight, "pair", axis=0, tiled=True)]
        flat = query_plain.reshape(rows, head_count * plain)
        near, far = pack_by_slices(place, flat, query_rotary, pairs)
    chunks, width = len(far), far[0][0].shape[1]

    keys = jnp.concatenate([before, joined], axis=1)
    coming = [swap(jnp.concatenate([far[0][0], keys], axis=1), 2), swap(far[0][1], 3)]
    near = [near[0], swap(after(near[1], coming[0]), 1)]
    keys = jnp.concatenate([keys, coming[0][:, width:]], axis=1)
    latent, turned, bias = prepare_keys(place, lengths, keys, swap(keys, 1), depth)

    def work(halves, c, sources, absorb_c):
        return attend(
            place, sources, halves, c, absorb_c, turned, latent, bias, rotary, width
        )

    parts = []
    for c in range(chunks):
        arrived = coming
        if c + 1 < chunks:
            following = after(far[c + 1], *arrived)
            coming = [swap(following[k - 2], k) for k in (2, 3)]
        if c == 0:
            absorb_c, value_c = absorb, value
        else:
            crossed = from_group(near_pair, c)
            absorb_c = [mine[c], from_group(jnp.concatenate(absorb[1:-1]), c), crossed]
            value_c = [mine_value[c]] + [from_group(piece, c) for piece in value[1:-1]] + [crossed]
        out = [None] * 2
        if c + 1 < chunks:
            mixed = work((0, 1), c, [*near, *arrived], absorb_c)
            value[1:-1] = value_c[1:-1] = after(value_c[1:-1], mixed)
            mixed = after(mixed, *coming)
            for half in (1, 0):
                out[half] = value_product(mixed, value_c, half, rows)
        else:
            for half in (1, 0):
                mixed = work((half,), c, (near, arrived)[half], absorb_c)
                out[half] = value_product(mixed, value_c, 0, rows)
                near = after(near, *out[half])
        back = swap(out[0][1], 1)
        coming = after(coming, back, *out[1])
        parts.append([out[0][0], back] + [swap(out[1][k - 2], k) for k in (2, 3)])
    return join(place, parts, pairs, by_group)


def solution(mesh):
    groups, ctx = mesh.shape["groups"], mesh.shape["ctx"]
    names = ("groups", "pair", "side", "core")
    fine = Mesh(np.asarray(mesh.devices).reshape(groups, ctx // QUAD, 2, 2), names)
    return jax.shard_map(
        on_device,
        mesh=fine,
        in_specs=(
            P(names, None, None),
            P(names, None),
            P(names, None),
            P(names, None),
            P(names[1:], None, None),
            P(names[1:], None, None),
            P("groups"),
        ),
        out_specs=P(names, None),
        check_vma=False,
    )
```

```python
import functools
import math

import jax
import jax.numpy as jnp
import numpy as np
from jax import lax
from jax.experimental import pallas as pl
from jax.experimental.pallas import tpu as pltpu
from jax.sharding import Mesh, PartitionSpec as P

QUAD = 4
JOIN_ORDER = (0, 2, 3, 1)
UNIT = 2
STEP_HEADS = 4
STRIP = 32


def dot(a, b):
    return jnp.dot(a, b, preferred_element_type=jnp.float32)


def call(kernel, mib=16, moved=0, **kw):
    return pl.pallas_call(
        kernel,
        compiler_params=pltpu.CompilerParams(vmem_limit_bytes=mib * 2**20),
        cost_estimate=pl.CostEstimate(flops=0, bytes_accessed=moved, transcendentals=0),
        **kw,
    )


HBM, IN_VMEM = pl.BlockSpec(memory_space=pltpu.HBM), pl.BlockSpec(memory_space=pltpu.VMEM)
ANY, SMEM = pl.BlockSpec(memory_space=pl.ANY), pl.BlockSpec(memory_space=pltpu.SMEM)


def take_heads(pieces, held):
    where = []
    for piece in pieces:
        where += [(piece, h) for h in range(piece.shape[0])]
    for first in range(0, len(where), STEP_HEADS):

        @pl.when(pl.program_id(0) == first // STEP_HEADS)
        def _():
            for h in range(STEP_HEADS):
                piece, at = where[first + h]
                held[h] = piece[at, piece.shape[1] - held.shape[1] :, :]


def order_of(quad, here, pairs):
    distance = quad ^ here
    order = jnp.where(distance == 1, pairs - 1, distance - 1)
    return jnp.where(distance == 0, 0, order)


def prepare_kernel(groups, pairs, place, *refs):
    plain, rotary, absorb, value = refs[:4]
    packs, refs = refs[4 : 6 + 2 * groups], refs[6 + 2 * groups :]
    stacked, values, pair = refs[:groups], refs[groups : 2 * groups], refs[2 * groups]
    refs = refs[2 * groups + 1 :]
    plain_in, rotary_in, absorb_in, value_in, single, flat, sems = refs
    rows, heads, width = plain_in.shape
    depth = value_in.shape[2]
    held, carried = heads // pairs, absorb_in.shape[1]
    copies = []

    def fetch(source, target):
        copies.append(pltpu.make_async_copy(source, target, sems.at[len(copies)]))
        copies[-1].start()

    for c in range(groups):
        at = pl.ds(lax.rem(place[2] + c, groups) * carried, carried)
        fetch(absorb.at[at], absorb_in.at[c])
        fetch(value.at[at], value_in.at[c])
    for i in range(pairs):
        at = pl.ds(i * held, held)
        fetch(plain.at[:, at], plain_in.at[:, at])
    fetch(rotary, rotary_in)

    for c in range(groups):
        copies[2 * c].wait()
        copies[2 * c + 1].wait()
        for first in range(0, depth, width):
            stacked[c][:, first : first + width, :] = absorb_in[c, :, :, first : first + width]
        values[c][...] = value_in[c]
    pair[:, :depth, :] = stacked[0][...]
    pair[:, depth:, :] = value_in[0]

    wide, thin = UNIT * width, rotary_in.shape[1] // (pairs * QUAD * groups)
    copies[-1].wait()
    for i in range(pairs):
        copies[2 * groups + i].wait()
        part = plain_in[:, i * held : (i + 1) * held, :]
        single[...] = part.astype(jnp.float32).reshape(rows * held, width)
        for head in range(held):
            part = single[pl.ds(head, rows, stride=held), :]
            flat[:, head * width : (head + 1) * width] = part.astype(flat.dtype)
        first = pl.multiple_of(order_of(i, place[1], pairs) * (wide + thin), wide + thin)
        for c in range(groups):
            for k in range(QUAD):
                at = (place[0] ^ k) * groups + lax.rem(place[2] + c, groups)
                out = packs[k].at[c] if k < 2 else packs[2 + c * 2 + k - 2]
                part = flat[:, pl.ds(pl.multiple_of(at * wide, wide), wide)]
                out[:, pl.ds(first, wide)] = part
                at = at * thin + i * thin * QUAD * groups
                part = rotary_in[:, pl.ds(pl.multiple_of(at, thin), thin)]
                out[:, pl.ds(pl.multiple_of(first + wide, thin), thin)] = part


def prepare(place, plain, rotary, absorb, value, pairs, groups):
    rows, heads, wide = plain.shape
    width = (heads * wide + rotary.shape[1]) // (QUAD * groups)
    held = absorb.shape[0] // groups
    part, dtype = (held, *value.shape[1:]), plain.dtype
    shapes = [(groups, rows, width)] * 2 + [(rows, width)] * (2 * groups)
    shapes += [part] * (2 * groups) + [(held, 2 * part[1], part[2])]
    outs = call(
        functools.partial(prepare_kernel, groups, pairs),
        in_specs=[SMEM] + [HBM] * 4,
        out_specs=[IN_VMEM] * len(shapes),
        out_shape=[jax.ShapeDtypeStruct(shape, dtype) for shape in shapes],
        scratch_shapes=[
            pltpu.VMEM(plain.shape, dtype),
            pltpu.VMEM(rotary.shape, dtype),
            pltpu.VMEM((groups, held, *absorb.shape[1:]), dtype),
            pltpu.VMEM((groups, held, *value.shape[1:]), dtype),
            pltpu.VMEM((rows * heads // pairs, wide), jnp.float32),
            pltpu.VMEM((rows, heads // pairs * wide), dtype),
            pltpu.SemaphoreType.DMA((2 * groups + pairs + 1,)),
        ],
        moved=12 * 2**20,
        mib=48,
        name="prepare",
    )(place, plain, rotary, absorb, value)
    far = outs[2 : 2 + 2 * groups]
    weights = outs[2 + 2 * groups :]
    return (
        outs[:2],
        [list(far[2 * c : 2 * c + 2]) for c in range(groups)],
        weights[:groups],
        weights[groups : 2 * groups],
        weights[-1],
    )


def pack_by_slices(place, plain, rotary, pairs):
    def sets(array):
        width = array.shape[1] // (QUAD * pairs)
        pick = lambda s: [
            array[:, (QUAD * i + s) * width : (QUAD * i + s + 1) * width] for i in range(pairs)
        ]
        whole = jnp.stack([jnp.concatenate(pick(s), axis=1) for s in range(QUAD)])
        steps = whole.shape[2] // (UNIT * (array.shape[1] // heads))
        return whole.reshape(QUAD, array.shape[0], steps, -1)

    heads = plain.shape[1] // 128
    both = jnp.concatenate([sets(plain), sets(rotary)], axis=3)
    both = both.reshape(QUAD, plain.shape[0], -1)
    packs = [lax.dynamic_index_in_dim(both, place[0] ^ k, 0, False) for k in range(QUAD)]
    return [pack[None] for pack in packs[:2]], [packs[2:]]


def joined_kernel(latent, rotary, joined, rotary_in, sems):
    depth = latent.shape[1]
    copies = [
        pltpu.make_async_copy(rotary, rotary_in, sems.at[0]),
        pltpu.make_async_copy(latent, joined.at[:, pl.ds(0, depth)], sems.at[1]),
    ]
    for copy in copies:
        copy.start()
    copies[0].wait()
    joined[:, depth:] = jnp.concatenate([rotary_in[...]] * 2, axis=0).T
    copies[1].wait()


def join_keys(latent, rotary):
    shape = (latent.shape[0], latent.shape[1] + 2 * rotary.shape[1])
    return call(
        joined_kernel,
        in_specs=[HBM, HBM],
        out_specs=IN_VMEM,
        out_shape=jax.ShapeDtypeStruct(shape, latent.dtype),
        scratch_shapes=[
            pltpu.VMEM(rotary.shape[::-1], rotary.dtype),
            pltpu.SemaphoreType.DMA((2,)),
        ],
        name="joined",
    )(latent, rotary.T)


def keys_kernel(place, lengths, near, far, latent, turned, bias):
    rows, depth, wide = near.shape[0], latent.shape[1], turned.shape[0]
    side, core = place[0] // 2, place[0] % 2
    for c, blocks in enumerate((near, far)):
        for k in range(2):
            for quad in range(2):
                first = (quad * 2 + (side ^ k)) * 2 * rows + c * rows
                at = pl.ds(pl.multiple_of(first, rows), rows)
                block = blocks[:, (k * 2 + quad) * wide : (k * 2 + quad + 1) * wide]
                latent[at, :] = block[:, :depth]
                turned[:depth, at] = block[:, :depth].T
                turned[depth:, at] = block[:, depth:].T
    count = bias.shape[1]
    spot = lax.broadcasted_iota(jnp.int32, (rows, count), 1) ^ (core * rows)
    row = lax.broadcasted_iota(jnp.int32, (rows, 1), 0)
    for k in range(QUAD):
        spots = spot + (QUAD * (place[1] - 1) + 2 * (side ^ (k // 2))) * rows
        mine = row + (QUAD * place[1] + (place[0] ^ k)) * rows
        begin, end = jnp.zeros_like(mine), 0
        for n in range(lengths.shape[0]):
            end = end + lengths[n]
            begin = jnp.where(mine >= end, end, begin)
        allowed = (spots >= begin) & (spots <= mine)
        bias[k * rows : (k + 1) * rows, :] = jnp.where(allowed, 0.0, -1e30).astype(jnp.float32)


def prepare_keys(place, lengths, near, far, depth):
    rows, wide = near.shape[0], near.shape[1] // QUAD
    return call(
        keys_kernel,
        in_specs=[SMEM] * 2 + [IN_VMEM] * 2,
        out_specs=[IN_VMEM] * 3,
        out_shape=[
            jax.ShapeDtypeStruct((2 * QUAD * rows, depth), near.dtype),
            jax.ShapeDtypeStruct((wide, 2 * QUAD * rows), near.dtype),
            jax.ShapeDtypeStruct((QUAD * rows, (QUAD + 2) * rows), jnp.float32),
        ],
        name="keys",
    )(place, lengths, near, far)


def attend_kernel(factor, halves, chunk, rotary, place, *refs):
    sources, pieces = refs[: 2 * len(halves)], refs[2 * len(halves) : -9]
    keys, latent, bias, mixed, packs, absorb, scores, weights, sems = refs[-9:]
    rows, (heads, plain, depth), count = packs.shape[1], absorb.shape, bias.shape[1]
    both = 2 * rows

    def fetch(source, target):
        copies.append(pltpu.make_async_copy(source, target, sems.at[len(copies)]))
        copies[-1].start()
        return copies[-1]

    copies, ready, first = [], {}, 0
    for n, source in enumerate(sources):
        source = source.at[chunk] if len(source.shape) == 3 else source
        copy = fetch(source.at[:, pl.ds(0, packs.shape[2])], packs.at[n])
        ready.setdefault((n // 2, 0), []).append(copy)
    for piece in pieces:
        held = absorb.at[pl.ds(first, piece.shape[0])]
        width = depth if piece.shape[1] == plain else piece.shape[2]
        for at in range(0, depth, width):
            source = piece if width == depth else piece.at[:, pl.ds(at // width * plain, plain)]
            target = held if width == depth else held.at[:, :, pl.ds(at, width)]
            ready.setdefault((0, first), []).append(fetch(source, target))
        first += piece.shape[0]

    lane = lax.broadcasted_iota(jnp.int32, (both, 2 * rotary), 1)
    units = [(n, head) for head in range(0, heads, 2) for n in range(len(halves))]

    def window(n):
        return pl.ds(pl.multiple_of((place[0] // 2 ^ halves[n]) * both, both), count)

    def score(u):
        n, head = units[u]
        for copy in ready.get((n, head), []):
            copy.wait()
        near, far = packs.at[2 * n], packs.at[2 * n + 1]
        base = head // UNIT * UNIT * (plain + rotary)
        for h in range(2):
            at = slice(base + h * plain, base + (h + 1) * plain)
            q = jnp.concatenate([near[:, at], far[:, at]], axis=0)
            q = dot(q, absorb[head + h]).astype(jnp.bfloat16)
            at = slice(base + UNIT * plain, base + UNIT * plain + 2 * rotary)
            r = jnp.concatenate([near[:, at], far[:, at]], axis=0)
            mine = (lane < rotary) if h == 0 else (lane >= rotary)
            left = jnp.concatenate([q, jnp.where(mine, r, jnp.zeros_like(r))], axis=1)
            scores[u % 2, h * both : (h + 1) * both, :] = dot(left, keys[:, window(n)])

    def weigh(u):
        scale = []
        for first in range(0, 2 * both, STRIP):
            at = slice(first, first + STRIP)
            start = halves[units[u][0]] * both + first % both
            s = scores[u % 2, at, :] + bias[start : start + STRIP, :]
            w = jnp.exp2((s - jnp.max(s, axis=-1, keepdims=True)) * factor)
            scale.append(1.0 / jnp.sum(w, axis=-1, keepdims=True))
            weights[u % 2, at, :] = w.astype(jnp.bfloat16)
        return jnp.concatenate(scale, axis=0)

    score(0)
    for u, (n, head) in enumerate(units):
        if u + 1 < len(units):
            score(u + 1)
        scale = weigh(u)
        for h in range(2):
            at = slice(h * both, (h + 1) * both)
            summed = dot(weights[u % 2, at, :], latent[window(n), :])
            mixed[head + h, n * both : (n + 1) * both, :] = (summed * scale[at]).astype(jnp.bfloat16)


def attend(place, sources, halves, chunk, absorb, keys, latent, bias, rotary, width):
    rows = sources[0].shape[-2]
    heads = sum(piece.shape[0] for piece in absorb)
    depth, plain = latent.shape[1], width // heads - rotary
    count = bias.shape[1]
    factor = math.log2(math.e) / math.sqrt(plain + rotary)
    return call(
        functools.partial(attend_kernel, factor, halves, chunk, rotary),
        in_specs=[SMEM] + [ANY] * (len(sources) + len(absorb)) + [IN_VMEM] * 3,
        out_specs=IN_VMEM,
        out_shape=jax.ShapeDtypeStruct((heads, 2 * len(halves) * rows, depth), jnp.bfloat16),
        scratch_shapes=[
            pltpu.VMEM((len(sources), rows, width), jnp.bfloat16),
            pltpu.VMEM((heads, plain, depth), jnp.bfloat16),
            pltpu.VMEM((2, QUAD * rows, count), jnp.float32),
            pltpu.VMEM((2, QUAD * rows, count), jnp.bfloat16),
            pltpu.SemaphoreType.DMA((len(sources) + len(absorb) * depth // 128,)),
        ],
        name="attend",
        mib=24,
    )(place, *sources, *absorb, keys, latent, bias)


def value_kernel(mixed, *refs):
    pieces, (one, two, value) = refs[:-3], refs[-3:]
    take_heads(pieces, value)
    rows, width = one.shape[0], value.shape[2]
    for head in range(STEP_HEADS):
        out = dot(mixed[head], value[head]).astype(jnp.bfloat16)
        one[:, head * width : (head + 1) * width] = out[:rows]
        two[:, head * width : (head + 1) * width] = out[rows:]


def value_product(mixed, value, half, rows):
    heads, _, depth = mixed.shape
    width = value[0].shape[2]
    out = pl.BlockSpec((rows, STEP_HEADS * width), lambda i: (0, i))
    return call(
        value_kernel,
        grid=(heads // STEP_HEADS,),
        in_specs=[pl.BlockSpec((STEP_HEADS, 2 * rows, depth), lambda i: (i, half, 0))]
        + [IN_VMEM] * len(value),
        out_specs=[out] * 2,
        out_shape=[jax.ShapeDtypeStruct((rows, heads * width), jnp.bfloat16)] * 2,
        scratch_shapes=[pltpu.VMEM((STEP_HEADS, depth, width), jnp.bfloat16)],
        name="value",
    )(mixed, *value)


def join_kernel(chunks, pairs, shifted, place, *refs):
    parts, out, sems = refs[:-2], *refs[-2:]
    width = out.shape[1] // (pairs * QUAD * chunks)
    copies = []
    for c in range(chunks):
        for n, k in enumerate(JOIN_ORDER):
            at = (place[0] ^ k) * chunks + lax.rem(place[2] + c, chunks)
            for i in range(pairs):
                block = order_of(i, place[1], pairs) if shifted else i
                source = pl.ds(pl.multiple_of(block * width, width), width)
                target = (i * QUAD * chunks + at) * width
                copies.append(
                    pltpu.make_async_copy(
                        parts[c * QUAD + n].at[:, source],
                        out.at[:, pl.ds(pl.multiple_of(target, width), width)],
                        sems.at[len(copies)],
                    )
                )
                copies[-1].start()
    for copy in copies:
        copy.wait()


def join(place, parts, pairs, shifted):
    chunks = len(parts)
    rows, wide = parts[0][0].shape
    return call(
        functools.partial(join_kernel, chunks, pairs, shifted),
        in_specs=[SMEM] + [ANY] * (chunks * QUAD),
        out_specs=ANY,
        out_shape=jax.ShapeDtypeStruct((rows, chunks * QUAD * wide), jnp.bfloat16),
        scratch_shapes=[pltpu.SemaphoreType.DMA((chunks * QUAD * pairs,))],
        name="join",
    )(place, *[chunk[k] for chunk in parts for k in JOIN_ORDER])


def swap(block, k):
    return lax.ppermute(block, ("side", "core"), [(i, i ^ k) for i in range(QUAD)])


def after(later, *earlier):
    return lax.optimization_barrier((later, earlier))[0]


def across(part, distance):
    pairs = lax.axis_size("pair")
    return lax.ppermute(part, "pair", [(i, i ^ distance) for i in range(pairs)])


def from_group(part, c):
    groups = lax.axis_size("groups")
    return lax.ppermute(part, "groups", [((i + c) % groups, i) for i in range(groups)])


def on_device(
    query_plain, query_rotary, key_latent, key_rotary, absorb_weight, value_weight, lengths
):
    rows, head_count, plain = query_plain.shape
    rotary = key_rotary.shape[1]
    depth = key_latent.shape[1]
    held = absorb_weight.shape[0]
    pairs, groups = lax.axis_size("pair"), lax.axis_size("groups")
    names = ("groups", "pair", "side", "core")
    group, pair, side, core = (lax.axis_index(name) for name in names)
    here = 2 * side + core
    place = jnp.stack([here, pair, group]).astype(jnp.int32)
    by_group = held == groups * UNIT and plain == 128 and UNIT * rotary == 128
    by_group = by_group and pairs & (pairs - 1) == 0

    def far_quads(near):
        known, far, distance = near, [], 2
        while distance < pairs:
            far.append(across(known, distance))
            known = jnp.concatenate([known, far[-1]])
            distance *= 2
        return far

    if by_group:
        joined = join_keys(key_latent, key_rotary)
    else:
        joined = jnp.concatenate([key_latent, key_rotary, key_rotary], axis=1)
    before = lax.ppermute(joined, "pair", [(i - 1, i) for i in range(1, pairs)])
    if by_group:
        near, far, mine, mine_value, pair_out = prepare(
            place, query_plain, query_rotary, absorb_weight, value_weight, pairs, groups
        )
        near_pair = across(pair_out, 1)
        absorb = [mine[0]] + [across(mine[0], d) for d in range(2, pairs)] + [near_pair]
        both = jnp.concatenate([mine_value[0], near_pair[:, depth:]])
        value = [mine_value[0], *far_quads(after(both, *absorb)), near_pair]
    else:
        absorb = [lax.all_gather(absorb_weight, "pair", axis=0, tiled=True)]
        value = [lax.all_gather(value_weight, "pair", axis=0, tiled=True)]
        flat = query_plain.reshape(rows, head_count * plain)
        near, far = pack_by_slices(place, flat, query_rotary, pairs)
    chunks, width = len(far), far[0][0].shape[1]

    keys = jnp.concatenate([before, joined], axis=1)
    coming = [swap(jnp.concatenate([far[0][0], keys], axis=1), 2), swap(far[0][1], 3)]
    near = [near[0], swap(near[1], 1)]
    keys = jnp.concatenate([keys, coming[0][:, width:]], axis=1)
    latent, turned, bias = prepare_keys(place, lengths, keys, swap(keys, 1), depth)

    def work(halves, c, sources, absorb_c):
        return attend(
            place, sources, halves, c, absorb_c, turned, latent, bias, rotary, width
        )

    parts = []
    for c in range(chunks):
        arrived = coming
        if c + 1 < chunks:
            following = after(far[c + 1], *arrived)
            coming = [swap(following[k - 2], k) for k in (2, 3)]
        if c == 0:
            absorb_c, value_c = absorb, value
        else:
            crossed = from_group(after(near_pair, near[1]), c)
            rest = after(jnp.concatenate(absorb[1:-1]), crossed)
            absorb_c = [mine[c], from_group(rest, c), crossed]
            value_c = [mine_value[c]] + [from_group(piece, c) for piece in value[1:-1]] + [crossed]
        out = [None] * 2
        if c + 1 < chunks:
            mixed = work((0, 1), c, [*near, *arrived], absorb_c)
            value[1:-1] = value_c[1:-1] = after(value_c[1:-1], mixed)
            mixed = after(mixed, *coming)
            for half in (1, 0):
                out[half] = value_product(mixed, value_c, half, rows)
        else:
            for half in (1, 0):
                mixed = work((half,), c, (near, arrived)[half], absorb_c)
                out[half] = value_product(mixed, value_c, 0, rows)
                near = after(near, *out[half])
        back = swap(out[0][1], 1)
        coming = after(coming, back, *out[1])
        parts.append([out[0][0], back] + [swap(out[1][k - 2], k) for k in (2, 3)])
    return join(place, parts, pairs, by_group)


def solution(mesh):
    groups, ctx = mesh.shape["groups"], mesh.shape["ctx"]
    names = ("groups", "pair", "side", "core")
    fine = Mesh(np.asarray(mesh.devices).reshape(groups, ctx // QUAD, 2, 2), names)
    return jax.shard_map(
        on_device,
        mesh=fine,
        in_specs=(
            P(names, None, None),
            P(names, None),
            P(names, None),
            P(names, None),
            P(names[1:], None, None),
            P(names[1:], None, None),
            P("groups"),
        ),
        out_specs=P(names, None),
        check_vma=False,
    )
```
